32 devices in a mesh: tile: 4 (over x, core), freq: 8 (over z, y).
Axes of the slice: x: 2, y: 2, z: 4, core: 2. Of those that a mesh axis runs over, the one named last changes fastest.
Arguments:
- sky: bfloat16 [4, 512, 2, 4096], P('tile', 'freq'), may hold values from -6 to 6
- kernel: bfloat16 [4, 8, 2, 4096, 128], P('tile', 'freq'), may hold values from -0.0625 to 0.0625
- data: bfloat16 [8, 2, 128, 512], P('freq'), may hold values from -6 to 6
- block_tiles: int32 [8, 4], P('freq'), may hold values 0 or 1
- length_bin: int32 [8, 128], P('freq'), may hold values from 0 to 31
- wedge_keep: int32 [32, 512], replicated, may hold values 0 or 1
Outputs:
- gradient: float32 [4, 512, 2, 4096], P('tile', 'freq')
The draws below stay inside these ranges and needn't reach their ends.
All inputs are finite; a program needn't handle non-finite values. No bound on the sum of `block_tiles` on one device may be relied on, other than what follows from the above.
Results may differ from the reference program's by a relative error of at most 0.0027.
Values may be sent and summed in bfloat16 or wider, within the bound.
No kernel may reach another device: no remote copies, remote signals or barrier semaphores. Data moves between devices by JAX's collectives and lax.ppermute only.
A program may use at most 128 MiB of HBM per device.

```python
import math
import jax
import jax.numpy as jnp
from jax import lax

CELLS = 4096
CH = 512
BL = 128
LBINS = 32
NBLK = 8
TILES = 4


def with_ends(entries, own_key, low, top_value):
    spot = [jax.random.randint(jax.random.fold_in(own_key, axis), (), 0, length) for axis, length in enumerate(entries.shape)]
    main_axis = entries.shape.index(max(entries.shape))
    neighbour = spot[:main_axis] + [(spot[main_axis] + 1) % entries.shape[main_axis]] + spot[main_axis + 1:]
    return entries.at[tuple(spot)].set(low).at[tuple(neighbour)].set(top_value)


def block_scale(own_key, shape, split, least, top_value):
    factor_of = 1.0
    for axis_at, shards_of in split:
        heights = jax.random.uniform(jax.random.fold_in(jax.random.fold_in(own_key, 6), axis_at), (shards_of,), jnp.float32, least / len(split), top_value / len(split))
        factor_of = factor_of * jnp.repeat(jnp.exp(heights), shape[axis_at] // shards_of).reshape((-1,) + (1,) * (len(shape) - 1 - axis_at))
    return factor_of


def bell_draw(stream_key, shape, deviation, limit, split=(), held_as=jnp.bfloat16):
    array = deviation * jax.random.normal(stream_key, shape, jnp.float32)
    if split:
        array = array * block_scale(stream_key, shape, split, -0.22, 0.18)
    return jnp.clip(array, -limit, limit).astype(held_as)


def setup_inputs(seed: int = 0) -> dict:
    arg_keys = jax.random.split(jax.random.key(seed), 7)
    return {
        "sky": bell_draw(arg_keys[0], (TILES, CH, 2, CELLS), 1.0, 6.0, ((0, 4), (1, 8))),
        "kernel": bell_draw(arg_keys[1], (TILES, NBLK, 2, CELLS, BL), (2 * CELLS) ** -0.5, 0.0625, ((0, 4), (1, 8))),
        "data": bell_draw(arg_keys[2], (NBLK, 2, BL, CH), 1.0, 6.0, ((0, 8),)),
        "block_tiles": with_ends((jax.random.randint(arg_keys[3], (NBLK, TILES), 0, 4) < 3).astype(jnp.int32), jax.random.fold_in(arg_keys[3], 1), 0, 1),
        "length_bin": with_ends(jax.random.randint(arg_keys[4], (NBLK, BL), 0, LBINS), jax.random.fold_in(arg_keys[4], 1), 0, LBINS - 1).astype(jnp.int32),
        "wedge_keep": with_ends((jax.random.randint(arg_keys[5], (LBINS, CH), 0, 2) < 1).astype(jnp.int32), jax.random.fold_in(arg_keys[5], 1), 0, 1),
    }


def delay_tables(length):
    indices = jnp.arange(length, dtype=jnp.int32)
    product = indices[:, None] * indices[None, :] % length
    angle = product.astype(jnp.float32) * (2.0 * math.pi / length)
    return (jnp.cos(angle), jnp.sin(angle))

def real_form(kernel_pair):
    upper_half = jnp.concatenate([kernel_pair[0], kernel_pair[1]], axis=1)
    lower_half = jnp.concatenate([-kernel_pair[1], kernel_pair[0]], axis=1)
    return jnp.concatenate([upper_half, lower_half], axis=0)

def transform(values, table):
    return jnp.einsum('...c,ck->...k', values, table, precision=lax.Precision.HIGHEST)

def back_project(visibility, data, keep_mask, cosine, sine_table):
    norm_factor = 1.0 / math.sqrt(cosine.shape[0])
    real_vis = visibility[:, 0]
    imag_vis = visibility[:, 1]
    spec_real = (transform(real_vis, cosine) + transform(imag_vis, sine_table)) * norm_factor
    spec_imag = (transform(imag_vis, cosine) - transform(real_vis, sine_table)) * norm_factor
    miss_real = keep_mask * (spec_real - data[:, 0].astype(jnp.float32))
    miss_imag = keep_mask * (spec_imag - data[:, 1].astype(jnp.float32))
    back_real = (transform(miss_real, cosine) - transform(miss_imag, sine_table)) * norm_factor
    back_imag = (transform(miss_imag, cosine) + transform(miss_real, sine_table)) * norm_factor
    return jnp.stack([back_real, back_imag], axis=1).astype(jnp.bfloat16)

def reference(sky, kernel, data, block_tiles, length_bin, wedge_keep):
    cosine, sine_table = delay_tables(CH)
    flat_sky = sky.reshape(TILES, CH, 2 * CELLS)

    def forward(block):
        running = jnp.zeros((CH, 2 * BL), jnp.float32)
        for tile_num in range(TILES):
            weight = block_tiles[block, tile_num].astype(jnp.float32)
            running = running + weight * jnp.dot(flat_sky[tile_num], real_form(kernel[tile_num, block]), preferred_element_type=jnp.float32)
        return running.T.reshape(2, BL, CH)
    visibility = lax.map(forward, jnp.arange(NBLK, dtype=jnp.int32))
    keep_mask = wedge_keep[length_bin].astype(jnp.float32)
    back_field = back_project(visibility, data, keep_mask, cosine, sine_table)

    def adjoint(running, block):
        field_rows = back_field[block].reshape(2 * BL, CH)
        updates = []
        for tile_num in range(TILES):
            weight = block_tiles[block, tile_num].astype(jnp.float32)
            updates.append(weight * jnp.dot(field_rows.T, real_form(kernel[tile_num, block]).T, preferred_element_type=jnp.float32))
        return (running + jnp.stack(updates), None)
    start_grad = jnp.zeros((TILES, CH, 2 * CELLS), jnp.float32)
    gradient, _ = lax.scan(adjoint, start_grad, jnp.arange(NBLK, dtype=jnp.int32))
    return gradient.reshape(TILES, CH, 2, CELLS)
```

```python
import math

import jax
import jax.numpy as jnp
from jax import lax
from jax.sharding import Mesh, PartitionSpec as P

SWAP = [(0, 1), (1, 0)]
ENDS = [(0, 1), (1, 0), (2, 3), (3, 2)]
MIDS = [(0, 0), (1, 2), (2, 1), (3, 3)]


def xor_chunks(rows, hi, lo):
    planes, count, cells = rows.shape
    rows = rows.reshape(planes, 2, 2, count // 4, cells)
    rows = jnp.where(hi == 1, rows[:, ::-1], rows)
    rows = jnp.where(lo == 1, rows[:, :, ::-1], rows)
    return rows.reshape(planes * count, cells)


def project(kernel_rows, sky_rows):
    out = lax.dot_general(
        kernel_rows, sky_rows, (((1,), (1,)), ((), ())), preferred_element_type=jnp.float32
    )
    base, chans = out.shape[0] // 2, out.shape[1] // 2
    real = out[:base, :chans] - out[base:, chans:]
    imag = out[:base, chans:] + out[base:, :chans]
    return jnp.stack([real, imag])


def adjoint(field, kernel_rows):
    total = 0.0
    for blk in range(2):
        real, imag = field[blk][0], field[blk][1]
        lhs = jnp.concatenate(
            [jnp.concatenate([real, imag], 1), jnp.concatenate([imag, -real], 1)], 0
        )
        total = total + lax.dot_general(
            lhs, kernel_rows[blk], (((0,), (0,)), ((), ())), preferred_element_type=jnp.float32
        )
    return total


def tables(channels, length):
    product = channels[:, None] * jnp.arange(length, dtype=jnp.int32)[None, :] % length
    angle = product.astype(jnp.float32) * (2.0 * math.pi / length)
    return jnp.cos(angle), jnp.sin(angle)


def mm(a, b):
    return jnp.einsum("bc,ck->bk", a, b, precision=lax.Precision.HIGHEST)


def mmt(a, b):
    return jnp.einsum("bk,ck->bc", a, b, precision=lax.Precision.HIGHEST)


def body(sky, kernel, data, block_tiles, length_bin, wedge_keep):
    length = data.shape[3]
    local, cells = sky.shape[1], sky.shape[3]
    base = kernel.shape[4]
    hi, lo = lax.axis_index("th"), lax.axis_index("tl")
    zpos, ypos = lax.axis_index("outer"), lax.axis_index("inner")
    depth = lax.axis_size("outer")
    tile_pos = hi * 2 + lo
    chunk = base // 4

    column = jnp.arange(block_tiles.shape[1], dtype=jnp.int32) == tile_pos
    weight = jnp.sum(jnp.where(column, block_tiles[0], 0)).astype(jnp.bfloat16)

    own_sky = sky[0].transpose(1, 0, 2).reshape(2 * local, cells)
    own_rows = xor_chunks((kernel[0, 0] * weight).transpose(0, 2, 1), hi, lo)
    kernels = [own_rows, lax.ppermute(own_rows, "inner", SWAP)]

    chain = depth == 4
    if chain:
        is_mid = (zpos == 1) | (zpos == 2)
        e1 = lax.ppermute(own_sky, "outer", ENDS)
        e2 = lax.ppermute(own_sky, "outer", MIDS)
        f1 = lax.ppermute(e2, "outer", ENDS)
        f2 = lax.ppermute(e1, "outer", MIDS)
        g1 = lax.ppermute(f2, "outer", ENDS)
        order = jnp.array([[0, 1, 2, 3], [1, 0, 2, 3], [2, 3, 1, 0], [3, 2, 1, 0]], jnp.int32)[zpos]
        vis = []
        for rows in kernels:
            parts = [
                project(rows, own_sky),
                project(rows, e1),
                jnp.where(is_mid, project(rows, e2), project(rows, f1)),
                jnp.where(is_mid, project(rows, f2), project(rows, g1)),
            ]
            vis.append(jnp.concatenate(parts, axis=2))
    else:
        every = lax.all_gather(own_sky, "outer")
        order = jnp.arange(depth, dtype=jnp.int32)
        vis = [
            jnp.concatenate([project(rows, every[s]) for s in range(depth)], axis=2)
            for rows in kernels
        ]

    def channels(half):
        place = (order[:, None] * 2 + half) * local + jnp.arange(local, dtype=jnp.int32)[None, :]
        return place.reshape(-1)

    own_cos, own_sin = tables(channels(ypos), length)
    far_cos, far_sin = tables(channels(1 - ypos), length)

    count = vis[0].shape[2]
    vis = jnp.stack(vis).reshape(2, 2, 2, 2, chunk, count)
    vis = vis[:, :, :, 0] + lax.ppermute(vis[:, :, :, 1], "tl", SWAP)
    diag = [(0, 3), (1, 2), (2, 1), (3, 0)]
    from_x = lax.ppermute(vis[0, :, 1], "th", SWAP)
    from_y = lax.ppermute(vis[1, :, 0], "inner", SWAP)
    from_d = lax.ppermute(vis[1, :, 1], ("th", "inner"), diag)
    own_vis = vis[0, :, 0] + from_x
    far_vis = from_y + from_d

    norm = 1.0 / math.sqrt(length)
    own_data = lax.dynamic_slice_in_dim(data[0], tile_pos * chunk, chunk, 1).astype(jnp.float32)
    own_bins = lax.dynamic_slice_in_dim(length_bin[0], tile_pos * chunk, chunk, 0)
    keep = wedge_keep[own_bins].astype(jnp.float32)
    cos_sum = [mm(own_vis[p], own_cos) + mm(far_vis[p], far_cos) for p in range(2)]
    sin_sum = [mm(own_vis[p], own_sin) + mm(far_vis[p], far_sin) for p in range(2)]
    miss_real = keep * ((cos_sum[0] + sin_sum[1]) * norm - own_data[0])
    miss_imag = keep * ((cos_sum[1] - sin_sum[0]) * norm - own_data[1])

    def back(cosine, sine):
        real = (mmt(miss_real, cosine) - mmt(miss_imag, sine)) * norm
        imag = (mmt(miss_imag, cosine) + mmt(miss_real, sine)) * norm
        return jnp.stack([real, imag]).astype(jnp.bfloat16)

    own_back, far_back = back(own_cos, own_sin), back(far_cos, far_sin)
    back_x = lax.ppermute(own_back, "th", SWAP)
    back_y = lax.ppermute(far_back, "inner", SWAP)
    back_d = lax.ppermute(far_back, ("th", "inner"), diag)
    half = jnp.stack([jnp.stack([own_back, back_x], 1), jnp.stack([back_y, back_d], 1)])
    other = lax.ppermute(half, "tl", SWAP)
    field = jnp.stack([half, other], 3).reshape(2, 2, base, count)

    def update(slot):
        return adjoint(field[..., slot * local : (slot + 1) * local], kernels)

    if chain:
        low = jnp.bfloat16
        near = lax.ppermute(update(3).astype(low), "outer", ENDS)
        sums3 = (update(3) + near.astype(jnp.float32)).astype(low)
        far3 = lax.ppermute(sums3, "outer", MIDS)
        near2 = lax.ppermute(update(2).astype(low), "outer", ENDS)
        sums2 = (update(2) + near2.astype(jnp.float32)).astype(low)
        far2 = lax.ppermute(sums2, "outer", MIDS)
        zero = jnp.zeros((), jnp.float32)
        last = (update(1) + jnp.where(is_mid, far3.astype(jnp.float32), zero)).astype(low)
        near1 = lax.ppermute(last, "outer", ENDS)
        gradient = update(0) + near1.astype(jnp.float32)
        gradient = gradient + jnp.where(is_mid, far2.astype(jnp.float32), zero)
    else:
        every = jnp.concatenate([update(s) for s in range(depth)], 0)
        gradient = lax.psum_scatter(every, "outer", scatter_dimension=0, tiled=True)
    return gradient.reshape(2, local, cells).transpose(1, 0, 2)[None]


def solution(mesh):
    tiles, freqs = mesh.shape["tile"], mesh.shape["freq"]
    fine = Mesh(mesh.devices.reshape(tiles // 2, 2, freqs // 2, 2), ("th", "tl", "outer", "inner"))
    tile, freq = ("th", "tl"), ("outer", "inner")
    return jax.shard_map(
        body,
        mesh=fine,
        in_specs=(
            P(tile, freq, None, None),
            P(tile, freq, None, None, None),
            P(freq, None, None, None),
            P(freq, None),
            P(freq, None),
            P(),
        ),
        out_specs=P(tile, freq, None, None),
        check_vma=False,
    )
```

```python
import functools
import math

import jax
import jax.numpy as jnp
from jax import lax
from jax.experimental import pallas as pl
from jax.experimental.pallas import tpu as pltpu
from jax.sharding import Mesh, PartitionSpec as P

SWAP = [(0, 1), (1, 0)]
ENDS = [(0, 1), (1, 0), (2, 3), (3, 2)]
MIDS = [(0, 0), (1, 2), (2, 1), (3, 3)]
DIAG = [(0, 3), (1, 2), (2, 1), (3, 0)]
LANES = 128
STEPS = 4
VMEM_LIMIT = 40 * 2**20
NT = (((1,), (1,)), ((), ()))


def xor_chunks(rows, hi, lo):
    planes, count, cells = rows.shape
    rows = rows.reshape(planes, 2, 2, count // 4, cells)
    rows = jnp.where(hi == 1, rows[:, ::-1], rows)
    rows = jnp.where(lo == 1, rows[:, :, ::-1], rows)
    return rows.reshape(planes * count, cells)


def project(kernel_rows, sky_rows):
    out = lax.dot_general(
        kernel_rows, sky_rows, (((1,), (1,)), ((), ())), preferred_element_type=jnp.float32
    )
    base, chans = out.shape[0] // 2, out.shape[1] // 2
    real = out[:base, :chans] - out[base:, chans:]
    imag = out[:base, chans:] + out[base:, :chans]
    return jnp.stack([real, imag])


def adjoint(field, kernel_rows):
    total = 0.0
    for blk in range(2):
        real, imag = field[blk][0], field[blk][1]
        lhs = jnp.concatenate(
            [jnp.concatenate([real, imag], 1), jnp.concatenate([imag, -real], 1)], 0
        )
        total = total + lax.dot_general(
            lhs, kernel_rows[blk], (((0,), (0,)), ((), ())), preferred_element_type=jnp.float32
        )
    return total


def tables(channels, length):
    product = channels[:, None] * jnp.arange(length, dtype=jnp.int32)[None, :] % length
    angle = product.astype(jnp.float32) * (2.0 * math.pi / length)
    return jnp.cos(angle), jnp.sin(angle)


def mm(a, b):
    return jnp.einsum("bc,ck->bk", a, b, precision=lax.Precision.HIGHEST)


def mmt(a, b):
    return jnp.einsum("bk,ck->bc", a, b, precision=lax.Precision.HIGHEST)


def any_body(sky, kernel, data, block_tiles, length_bin, wedge_keep):
    length = data.shape[3]
    local, cells = sky.shape[1], sky.shape[3]
    base = kernel.shape[4]
    hi, lo = lax.axis_index("th"), lax.axis_index("tl")
    zpos, ypos = lax.axis_index("outer"), lax.axis_index("inner")
    depth = lax.axis_size("outer")
    tile_pos = hi * 2 + lo
    chunk = base // 4

    column = jnp.arange(block_tiles.shape[1], dtype=jnp.int32) == tile_pos
    weight = jnp.sum(jnp.where(column, block_tiles[0], 0)).astype(jnp.bfloat16)

    own_sky = sky[0].transpose(1, 0, 2).reshape(2 * local, cells)
    own_rows = xor_chunks((kernel[0, 0] * weight).transpose(0, 2, 1), hi, lo)
    kernels = [own_rows, lax.ppermute(own_rows, "inner", SWAP)]

    every = lax.all_gather(own_sky, "outer")
    order = jnp.arange(depth, dtype=jnp.int32)
    vis = [
        jnp.concatenate([project(rows, every[s]) for s in range(depth)], axis=2)
        for rows in kernels
    ]

    def channels(half):
        place = (order[:, None] * 2 + half) * local + jnp.arange(local, dtype=jnp.int32)[None, :]
        return place.reshape(-1)

    own_cos, own_sin = tables(channels(ypos), length)
    far_cos, far_sin = tables(channels(1 - ypos), length)

    count = vis[0].shape[2]
    vis = jnp.stack(vis).reshape(2, 2, 2, 2, chunk, count)
    vis = vis[:, :, :, 0] + lax.ppermute(vis[:, :, :, 1], "tl", SWAP)
    from_x = lax.ppermute(vis[0, :, 1], "th", SWAP)
    from_y = lax.ppermute(vis[1, :, 0], "inner", SWAP)
    from_d = lax.ppermute(vis[1, :, 1], ("th", "inner"), DIAG)
    own_vis = vis[0, :, 0] + from_x
    far_vis = from_y + from_d

    norm = 1.0 / math.sqrt(length)
    own_data = lax.dynamic_slice_in_dim(data[0], tile_pos * chunk, chunk, 1).astype(jnp.float32)
    own_bins = lax.dynamic_slice_in_dim(length_bin[0], tile_pos * chunk, chunk, 0)
    keep = wedge_keep[own_bins].astype(jnp.float32)
    cos_sum = [mm(own_vis[p], own_cos) + mm(far_vis[p], far_cos) for p in range(2)]
    sin_sum = [mm(own_vis[p], own_sin) + mm(far_vis[p], far_sin) for p in range(2)]
    miss_real = keep * ((cos_sum[0] + sin_sum[1]) * norm - own_data[0])
    miss_imag = keep * ((cos_sum[1] - sin_sum[0]) * norm - own_data[1])

    def back(cosine, sine):
        real = (mmt(miss_real, cosine) - mmt(miss_imag, sine)) * norm
        imag = (mmt(miss_imag, cosine) + mmt(miss_real, sine)) * norm
        return jnp.stack([real, imag]).astype(jnp.bfloat16)

    own_back, far_back = back(own_cos, own_sin), back(far_cos, far_sin)
    back_x = lax.ppermute(own_back, "th", SWAP)
    back_y = lax.ppermute(far_back, "inner", SWAP)
    back_d = lax.ppermute(far_back, ("th", "inner"), DIAG)
    half = jnp.stack([jnp.stack([own_back, back_x], 1), jnp.stack([back_y, back_d], 1)])
    other = lax.ppermute(half, "tl", SWAP)
    field = jnp.stack([half, other], 3).reshape(2, 2, base, count)

    def update(slot):
        return adjoint(field[..., slot * local : (slot + 1) * local], kernels)

    every = jnp.concatenate([update(s) for s in range(depth)], 0)
    gradient = lax.psum_scatter(every, "outer", scatter_dimension=0, tiled=True)
    return gradient.reshape(2, local, cells).transpose(1, 0, 2)[None]


def wide(tiles):
    return jnp.concatenate([tiles[t] for t in range(tiles.shape[0])], axis=1)


def forward_kernel(
    place, own_k, far_k, slot0, slot1, mid2, mid3, end2, end3, out, total
):
    step = pl.program_id(0)
    is_mid = place[0] == 1

    @pl.when(step == 0)
    def _():
        total[...] = jnp.zeros_like(total)

    rows = jnp.concatenate(
        [
            wide(slot0[...]),
            wide(slot1[...]),
            wide(jnp.where(is_mid, mid2[...], end2[...])),
            wide(jnp.where(is_mid, mid3[...], end3[...])),
        ],
        axis=0,
    )
    for blk, part in enumerate((own_k, far_k)):
        pair = jnp.concatenate([part[0], part[1]], axis=1)
        total[blk] += jnp.dot(rows, pair, preferred_element_type=jnp.float32)

    @pl.when(step == STEPS - 1)
    def _():
        store_visibility(place, total, out)


def store_visibility(place, total, out):
    base = total.shape[2] // 2
    local = total.shape[1] // 8
    chunk = base // 4
    for blk in range(2):
        for two in range(2):
            planes = [[], []]
            for slot in (2 * two, 2 * two + 1):
                own = total[blk, slot * 2 * local : (slot + 1) * 2 * local, :]
                planes[0].append(own[:local, :base] - own[local:, base:])
                planes[1].append(own[local:, :base] + own[:local, base:])
            for p in range(2):
                turned = jnp.concatenate(planes[p], axis=0).T
                for n in range(4):
                    m = ((n & 1) ^ place[2]) * 2 + ((n >> 1) ^ place[1])
                    out[m, blk, p, :, two * 2 * local : (two + 1) * 2 * local] = turned[
                        n * chunk : (n + 1) * chunk
                    ]


def forward(place, own_k, far_k, slots, chunk):
    count, rows, _ = slots[0].shape
    tiles = count // STEPS
    base = own_k.shape[2]
    k_spec = pl.BlockSpec((2, tiles * LANES, base), lambda i: (0, i, 0))
    s_spec = pl.BlockSpec((tiles, rows, LANES), lambda i: (i, 0, 0))
    shape = (4, 2, 2, chunk, rows * 2)
    return pl.pallas_call(
        forward_kernel,
        grid=(STEPS,),
        in_specs=[pl.BlockSpec(memory_space=pltpu.SMEM), k_spec, k_spec] + [s_spec] * 6,
        out_specs=pl.BlockSpec(shape, lambda i: (0,) * 5),
        out_shape=jax.ShapeDtypeStruct(shape, jnp.float32),
        scratch_shapes=[pltpu.VMEM((2, 4 * rows, 2 * base), jnp.float32)],
        compiler_params=pltpu.CompilerParams(vmem_limit_bytes=VMEM_LIMIT),
        cost_estimate=pl.CostEstimate(
            flops=16 * rows * count * LANES * 2 * base, bytes_accessed=10 * 2**20, transcendentals=0
        ),
        name="forward",
    )(place, own_k, far_k, *slots)


def split(value):
    high = value.astype(jnp.bfloat16)
    return high, (value - high.astype(jnp.float32)).astype(jnp.bfloat16)


def times(value, high, low, dims):
    rows = value.shape[0]
    upper, lower = split(value)
    both = lax.dot_general(
        jnp.concatenate([upper, lower], axis=0), high, dims, preferred_element_type=jnp.float32
    )
    rest = lax.dot_general(upper, low, dims, preferred_element_type=jnp.float32)
    return both[:rows] + both[rows:] + rest


def delay_kernel(vis0, from_x, from_y, from_d, data, keep, ch, cl, sh, sl, own_out, far_out):
    length = keep.shape[1]
    chunk = keep.shape[0]
    half = length // 2
    norm = 1.0 / math.sqrt(length)
    nn = (((1,), (0,)), ((), ()))
    own = vis0[...] + from_x[...]
    far = from_y[...] + from_d[...]
    rows = jnp.concatenate(
        [jnp.concatenate([own[p], far[p]], axis=1) for p in range(2)], axis=0
    )
    cos_sum = times(rows, ch[...], cl[...], nn)
    sin_sum = times(rows, sh[...], sl[...], nn)
    kept = keep[...]
    real = kept * ((cos_sum[:chunk] + sin_sum[chunk:]) * norm - data[0])
    imag = kept * ((cos_sum[chunk:] - sin_sum[:chunk]) * norm - data[1])
    miss = jnp.concatenate([real, imag], axis=0)
    cos_back = times(miss, ch[...], cl[...], NT)
    sin_back = times(miss, sh[...], sl[...], NT)
    back_real = ((cos_back[:chunk] - sin_back[chunk:]) * norm).astype(jnp.bfloat16)
    back_imag = ((cos_back[chunk:] + sin_back[:chunk]) * norm).astype(jnp.bfloat16)
    own_out[0] = back_real[:, :half]
    own_out[1] = back_imag[:, :half]
    far_out[0] = back_real[:, half:]
    far_out[1] = back_imag[:, half:]


def delay(*parts):
    shape = jax.ShapeDtypeStruct(parts[0].shape, jnp.bfloat16)
    length = parts[5].shape[1]
    return pl.pallas_call(
        delay_kernel,
        out_shape=(shape, shape),
        compiler_params=pltpu.CompilerParams(vmem_limit_bytes=VMEM_LIMIT),
        cost_estimate=pl.CostEstimate(
            flops=24 * parts[5].shape[0] * length * length,
            bytes_accessed=8 * length * length,
            transcendentals=0,
        ),
        name="delay",
    )(*parts)


def turn_field(place, half, other, slots, out):
    chunk, wide_c = half.shape[3], half.shape[4]
    local = wide_c // 4
    base = 4 * chunk
    for blk in range(2):
        for two in sorted({s // 2 for s in slots}):
            turned = []
            for p in range(2):
                rows = []
                for n in range(4):
                    hi, lo = (n >> 1) ^ place[1], (n & 1) ^ place[2]
                    lanes = slice(two * 2 * local, (two + 1) * 2 * local)
                    near = half[hi, blk, p, :, lanes].astype(jnp.float32)
                    away = other[hi, blk, p, :, lanes].astype(jnp.float32)
                    rows.append(jnp.where(lo == 0, near, away))
                turned.append(jnp.concatenate(rows, axis=0).T)
            for s in slots:
                if s // 2 != two:
                    continue
                low = (s % 2) * local
                real = turned[0][low : low + local].astype(jnp.bfloat16)
                imag = turned[1][low : low + local].astype(jnp.bfloat16)
                at = blk * 2 * base
                i = slots.index(s)
                out[i * 2 * local : i * 2 * local + local, at : at + base] = real
                out[i * 2 * local : i * 2 * local + local, at + base : at + 2 * base] = imag
                out[i * 2 * local + local : (i + 1) * 2 * local, at : at + base] = imag
                out[i * 2 * local + local : (i + 1) * 2 * local, at + base : at + 2 * base] = -real


def adjoint_kernel(slots, place, half, other, own_k, far_k, *rest):
    outs, field = rest[:-1], rest[-1]

    @pl.when(pl.program_id(0) == 0)
    def _():
        turn_field(place, half, other, slots, field)

    cells = jnp.concatenate([own_k[0], own_k[1], far_k[0], far_k[1]], axis=1)
    sums = lax.dot_general(field[...], cells, NT, preferred_element_type=jnp.float32)
    rows = sums.shape[0] // len(slots)
    for i in range(len(slots)):
        for t in range(outs[i].shape[0]):
            outs[i][t] = sums[i * rows : (i + 1) * rows, t * LANES : (t + 1) * LANES]


def adjoint_parts(place, half, other, own_k, far_k, slots):
    base = own_k.shape[2]
    count = own_k.shape[1] // LANES
    tiles = count // STEPS
    rows = half.shape[4] // 2
    k_spec = pl.BlockSpec((2, tiles * LANES, base), lambda i: (0, i, 0))
    f_spec = pl.BlockSpec(half.shape, lambda i: (0,) * 5)
    return pl.pallas_call(
        functools.partial(adjoint_kernel, slots),
        grid=(STEPS,),
        in_specs=[pl.BlockSpec(memory_space=pltpu.SMEM), f_spec, f_spec, k_spec, k_spec],
        out_specs=[pl.BlockSpec((tiles, rows, LANES), lambda i: (i, 0, 0))] * len(slots),
        out_shape=[jax.ShapeDtypeStruct((count, rows, LANES), jnp.float32)] * len(slots),
        scratch_shapes=[pltpu.VMEM((rows * len(slots), 4 * base), jnp.bfloat16)],
        compiler_params=pltpu.CompilerParams(vmem_limit_bytes=VMEM_LIMIT),
        cost_estimate=pl.CostEstimate(
            flops=8 * rows * len(slots) * count * LANES * base,
            bytes_accessed=(4 + 2 * len(slots)) * 2**20,
            transcendentals=0,
        ),
        name="adjoint",
    )(place, half, other, own_k, far_k)


def table_parts(value):
    high = lax.reduce_precision(value, 8, 7)
    return high.astype(jnp.bfloat16), (value - high).astype(jnp.bfloat16)


def line_body(sky, kernel, data, block_tiles, length_bin, wedge_keep):
    length = data.shape[3]
    local, cells = sky.shape[1], sky.shape[3]
    base = kernel.shape[4]
    hi, lo = lax.axis_index("th"), lax.axis_index("tl")
    zpos, ypos = lax.axis_index("outer"), lax.axis_index("inner")
    tile_pos = hi * 2 + lo
    chunk = base // 4
    is_mid = (zpos == 1) | (zpos == 2)
    place = jnp.stack([is_mid.astype(jnp.int32), hi, lo])

    own_sky = sky[0].reshape(local, 2, cells // LANES, LANES).transpose(2, 1, 0, 3)
    own_sky = own_sky.reshape(cells // LANES, 2 * local, LANES)
    column = jnp.arange(block_tiles.shape[1], dtype=jnp.int32) == tile_pos
    weight = jnp.sum(jnp.where(column, block_tiles[0], 0)).astype(jnp.bfloat16)

    e1 = lax.ppermute(own_sky, "outer", ENDS)
    e2 = lax.ppermute(own_sky, "outer", MIDS)
    own_k = kernel[0, 0] * weight
    far_k = lax.ppermute(own_k, "inner", SWAP)
    f2 = lax.ppermute(e1, "outer", MIDS)
    f1 = lax.ppermute(e2, "outer", ENDS)
    g1 = lax.ppermute(f2, "outer", ENDS)

    order = jnp.array([[0, 1, 2, 3], [1, 0, 2, 3], [2, 3, 1, 0], [3, 2, 1, 0]], jnp.int32)[zpos]
    halves = jnp.stack([ypos, 1 - ypos])
    place_of = (order[None, :, None] * 2 + halves[:, None, None]) * local
    place_of = place_of + jnp.arange(local, dtype=jnp.int32)
    cosine, sine = tables(place_of.reshape(-1), length)
    parts = table_parts(cosine) + table_parts(sine)
    own_data = lax.dynamic_slice_in_dim(data[0], tile_pos * chunk, chunk, 1).astype(jnp.float32)
    own_bins = lax.dynamic_slice_in_dim(length_bin[0], tile_pos * chunk, chunk, 0)
    keep = wedge_keep[own_bins].astype(jnp.float32)

    vis = forward(place, own_k, far_k, (own_sky, e1, e2, f2, f1, g1), chunk)
    vis = vis[:2] + lax.ppermute(vis[2:], "tl", SWAP)
    from_x = lax.ppermute(vis[1, 0], "th", SWAP)
    from_y = lax.ppermute(vis[0, 1], "inner", SWAP)
    from_d = lax.ppermute(vis[1, 1], ("th", "inner"), DIAG)
    own_back, far_back = delay(vis[0, 0], from_x, from_y, from_d, own_data, keep, *parts)
    back_x = lax.ppermute(own_back, "th", SWAP)
    back_y = lax.ppermute(far_back, "inner", SWAP)
    back_d = lax.ppermute(far_back, ("th", "inner"), DIAG)
    half = jnp.stack([jnp.stack([own_back, back_y]), jnp.stack([back_x, back_d])])
    other = lax.ppermute(half, "tl", SWAP)

    (part3,) = adjoint_parts(place, half, other, own_k, far_k, (3,))
    (part2,) = adjoint_parts(place, half, other, own_k, far_k, (2,))
    part1, part0 = adjoint_parts(place, half, other, own_k, far_k, (1, 0))
    low = jnp.bfloat16
    near3 = lax.ppermute(part3.astype(low), "outer", ENDS)
    far3 = lax.ppermute((part3 + near3.astype(jnp.float32)).astype(low), "outer", MIDS)
    near2 = lax.ppermute(part2.astype(low), "outer", ENDS)
    far2 = lax.ppermute((part2 + near2.astype(jnp.float32)).astype(low), "outer", MIDS)
    zero = jnp.zeros((), jnp.float32)
    last = (part1 + jnp.where(is_mid, far3.astype(jnp.float32), zero)).astype(low)
    near1 = lax.ppermute(last, "outer", ENDS)
    gradient = part0 + near1.astype(jnp.float32)
    gradient = gradient + jnp.where(is_mid, far2.astype(jnp.float32), zero)
    gradient = gradient.reshape(cells // LANES, 2, local, LANES).transpose(2, 1, 0, 3)
    return gradient.reshape(1, local, 2, cells)


def body(sky, kernel, *rest):
    local, cells = sky.shape[1], sky.shape[3]
    line = lax.axis_size("outer") == 4 and 2 * local == LANES and kernel.shape[4] == LANES
    chosen = line_body if line and cells % (STEPS * LANES) == 0 else any_body
    return chosen(sky, kernel, *rest)


def solution(mesh):
    tiles, freqs = mesh.shape["tile"], mesh.shape["freq"]
    fine = Mesh(mesh.devices.reshape(tiles // 2, 2, freqs // 2, 2), ("th", "tl", "outer", "inner"))
    tile, freq = ("th", "tl"), ("outer", "inner")
    return jax.shard_map(
        body,
        mesh=fine,
        in_specs=(
            P(tile, freq, None, None),
            P(tile, freq, None, None, None),
            P(freq, None, None, None),
            P(freq, None),
            P(freq, None),
            P(),
        ),
        out_specs=P(tile, freq, None, None),
        check_vma=False,
    )
```

```python
import functools
import math

import jax
import jax.numpy as jnp
import ml_dtypes
import numpy as np
from jax import lax
from jax.experimental import pallas as pl
from jax.experimental.pallas import tpu as pltpu
from jax.sharding import Mesh, PartitionSpec as P

SWAP = [(0, 1), (1, 0)]
ENDS = [(0, 1), (1, 0), (2, 3), (3, 2)]
MIDS = [(1, 2), (2, 1), (5, 6), (6, 5), (0, 4), (4, 0), (3, 7), (7, 3)]
DIAG = [(0, 3), (1, 2), (2, 1), (3, 0)]
LANES = 128
PARTS = ((0, 1), (1, 2))
VMEM_LIMIT = 24 * 2**20
NT = (((1,), (1,)), ((), ()))


def cost(flops, bytes_accessed, transcendentals, times=1):
    return pl.CostEstimate(
        flops=times * flops, bytes_accessed=times * bytes_accessed, transcendentals=transcendentals
    )


def xor_chunks(rows, hi, lo):
    planes, count, cells = rows.shape
    rows = rows.reshape(planes, 2, 2, count // 4, cells)
    rows = jnp.where(hi == 1, rows[:, ::-1], rows)
    rows = jnp.where(lo == 1, rows[:, :, ::-1], rows)
    return rows.reshape(planes * count, cells)


def project(kernel_rows, sky_rows):
    out = lax.dot_general(
        kernel_rows, sky_rows, (((1,), (1,)), ((), ())), preferred_element_type=jnp.float32
    )
    base, chans = out.shape[0] // 2, out.shape[1] // 2
    real = out[:base, :chans] - out[base:, chans:]
    imag = out[:base, chans:] + out[base:, :chans]
    return jnp.stack([real, imag])


def adjoint_any(field, kernel_rows):
    total = 0.0
    for blk in range(2):
        real, imag = field[blk][0], field[blk][1]
        lhs = jnp.concatenate(
            [jnp.concatenate([real, imag], 1), jnp.concatenate([imag, -real], 1)], 0
        )
        total = total + lax.dot_general(
            lhs, kernel_rows[blk], (((0,), (0,)), ((), ())), preferred_element_type=jnp.float32
        )
    return total


def tables(channels, length):
    product = channels[:, None] * jnp.arange(length, dtype=jnp.int32)[None, :] % length
    angle = product.astype(jnp.float32) * (2.0 * math.pi / length)
    return jnp.cos(angle), jnp.sin(angle)


def mm(a, b):
    return jnp.einsum("bc,ck->bk", a, b, precision=lax.Precision.HIGHEST)


def mmt(a, b):
    return jnp.einsum("bk,ck->bc", a, b, precision=lax.Precision.HIGHEST)


def any_body(sky, kernel, data, block_tiles, length_bin, wedge_keep):
    length = data.shape[3]
    local, cells = sky.shape[1], sky.shape[3]
    base = kernel.shape[4]
    hi, lo = lax.axis_index("th"), lax.axis_index("tl")
    zpos, ypos = lax.axis_index("outer"), lax.axis_index("inner")
    depth = lax.axis_size("outer")
    tile_pos = hi * 2 + lo
    chunk = base // 4

    column = jnp.arange(block_tiles.shape[1], dtype=jnp.int32) == tile_pos
    weight = jnp.sum(jnp.where(column, block_tiles[0], 0)).astype(jnp.bfloat16)

    own_sky = sky[0].transpose(1, 0, 2).reshape(2 * local, cells)
    own_rows = xor_chunks((kernel[0, 0] * weight).transpose(0, 2, 1), hi, lo)
    kernels = [own_rows, lax.ppermute(own_rows, "inner", SWAP)]

    every = lax.all_gather(own_sky, "outer")
    order = jnp.arange(depth, dtype=jnp.int32)
    vis = [
        jnp.concatenate([project(rows, every[s]) for s in range(depth)], axis=2)
        for rows in kernels
    ]

    def channels(half):
        place = (order[:, None] * 2 + half) * local + jnp.arange(local, dtype=jnp.int32)[None, :]
        return place.reshape(-1)

    own_cos, own_sin = tables(channels(ypos), length)
    far_cos, far_sin = tables(channels(1 - ypos), length)

    count = vis[0].shape[2]
    vis = jnp.stack(vis).reshape(2, 2, 2, 2, chunk, count)
    vis = vis[:, :, :, 0] + lax.ppermute(vis[:, :, :, 1], "tl", SWAP)
    from_x = lax.ppermute(vis[0, :, 1], "th", SWAP)
    from_y = lax.ppermute(vis[1, :, 0], "inner", SWAP)
    from_d = lax.ppermute(vis[1, :, 1], ("th", "inner"), DIAG)
    own_vis = vis[0, :, 0] + from_x
    far_vis = from_y + from_d

    norm = 1.0 / math.sqrt(length)
    own_data = lax.dynamic_slice_in_dim(data[0], tile_pos * chunk, chunk, 1).astype(jnp.float32)
    own_bins = lax.dynamic_slice_in_dim(length_bin[0], tile_pos * chunk, chunk, 0)
    keep = wedge_keep[own_bins].astype(jnp.float32)
    cos_sum = [mm(own_vis[p], own_cos) + mm(far_vis[p], far_cos) for p in range(2)]
    sin_sum = [mm(own_vis[p], own_sin) + mm(far_vis[p], far_sin) for p in range(2)]
    miss_real = keep * ((cos_sum[0] + sin_sum[1]) * norm - own_data[0])
    miss_imag = keep * ((cos_sum[1] - sin_sum[0]) * norm - own_data[1])

    def back(cosine, sine):
        real = (mmt(miss_real, cosine) - mmt(miss_imag, sine)) * norm
        imag = (mmt(miss_imag, cosine) + mmt(miss_real, sine)) * norm
        return jnp.stack([real, imag]).astype(jnp.bfloat16)

    own_back, far_back = back(own_cos, own_sin), back(far_cos, far_sin)
    back_x = lax.ppermute(own_back, "th", SWAP)
    back_y = lax.ppermute(far_back, "inner", SWAP)
    back_d = lax.ppermute(far_back, ("th", "inner"), DIAG)
    half = jnp.stack([jnp.stack([own_back, back_x], 1), jnp.stack([back_y, back_d], 1)])
    other = lax.ppermute(half, "tl", SWAP)
    field = jnp.stack([half, other], 3).reshape(2, 2, base, count)

    def update(slot):
        return adjoint_any(field[..., slot * local : (slot + 1) * local], kernels)

    every = jnp.concatenate([update(s) for s in range(depth)], 0)
    gradient = lax.psum_scatter(every, "outer", scatter_dimension=0, tiled=True)
    return gradient.reshape(2, local, cells).transpose(1, 0, 2)[None]


def wide(tiles):
    return jnp.concatenate([tiles[t] for t in range(tiles.shape[0])], axis=1)


def paired(part):
    return jnp.concatenate([part[0], part[1]], axis=1)


def tall(tiles):
    return tiles.reshape(tiles.shape[0] * tiles.shape[1], tiles.shape[2])


def dot(a, b):
    return jnp.dot(a, b, preferred_element_type=jnp.float32)


def near_sum_kernel(keep, got, out):
    out[...] = (keep[...] + got[...]).astype(out.dtype)


def near_sum(keep, got):
    vmem = pl.BlockSpec(memory_space=pltpu.VMEM)
    return pl.pallas_call(
        near_sum_kernel,
        in_specs=[vmem, vmem],
        out_specs=vmem,
        out_shape=jax.ShapeDtypeStruct(keep.shape, jnp.bfloat16),
        compiler_params=pltpu.CompilerParams(vmem_limit_bytes=VMEM_LIMIT),
        cost_estimate=cost(flops=keep.size, bytes_accessed=10 * keep.size, transcendentals=0),
        name="near_sum",
    )(keep, got)


def own_sum_kernel(place, keep, got, near, mine, to_x, to_y, to_d):
    for hi, blk, out in ((0, 0, mine), (1, 0, to_x), (0, 1, to_y), (1, 1, to_d)):
        added = jnp.where(place[0] == 1, 0.0, near[hi, blk].astype(jnp.float32))
        out[...] = keep[hi, blk] + got[hi, blk] + added


def own_sum(place, keep, got, near):
    vmem = pl.BlockSpec(memory_space=pltpu.VMEM)
    shape = keep.shape[2:]
    return pl.pallas_call(
        own_sum_kernel,
        in_specs=[pl.BlockSpec(memory_space=pltpu.SMEM)] + [vmem] * 3,
        out_specs=[vmem] * 4,
        out_shape=[jax.ShapeDtypeStruct(shape, jnp.float32)] * 4,
        compiler_params=pltpu.CompilerParams(vmem_limit_bytes=VMEM_LIMIT),
        cost_estimate=cost(flops=2 * keep.size, bytes_accessed=14 * keep.size, transcendentals=0),
        name="own_sum",
    )(place, keep, got, near)


def early_kernel(place, own_k, far_k, slot0, slot1, mid2, end2, *rest):
    total = rest[-1]

    @pl.when(pl.program_id(0) == 0)
    def _():
        total[...] = jnp.zeros_like(total)

    third = jnp.where(place[0] == 1, mid2[...], end2[...])
    rows = jnp.concatenate([wide(slot0[...]), wide(slot1[...]), wide(third)], axis=0)
    for blk, part in enumerate((own_k, far_k)):
        total[blk] += dot(rows, paired(part))


def early(place, own_k, far_k, sky, r1, m1, r2, ready):
    count, rows, _ = r1.shape
    base = own_k.shape[2]
    tiles = count // 3
    k_spec = pl.BlockSpec((2, tiles * LANES, base), lambda i: (0, i, 0))
    own_spec = pl.BlockSpec((tiles, rows, LANES), lambda i: (i + 1, 0, 0))
    s_spec = pl.BlockSpec((tiles, rows, LANES), lambda i: (i, 0, 0))
    shape = (2, 3 * rows, 2 * base)
    return pl.pallas_call(
        early_kernel,
        grid=(3,),
        in_specs=[pl.BlockSpec(memory_space=pltpu.SMEM), k_spec, k_spec, own_spec]
        + [s_spec] * 3
        + [pl.BlockSpec(memory_space=pl.ANY)] * len(ready),
        out_specs=pl.BlockSpec(shape, lambda i: (0, 0, 0)),
        out_shape=jax.ShapeDtypeStruct(shape, jnp.float32),
        compiler_params=pltpu.CompilerParams(vmem_limit_bytes=VMEM_LIMIT),
        cost_estimate=cost(
            flops=12 * rows * count * LANES * 2 * base, bytes_accessed=8 * 2**20, transcendentals=0
        ),
        name="early",
    )(place, own_k, far_k, sky, r1, m1, r2, *ready)


def late_kernel(
    place, done, own_k, far_k, mid3, end3, own_a, far_a, sky_a, near_sky, peer_sky, peer_near_sky,
    near_k, near_far_k, keep, send, near_keep, near_send, total, near_total
):
    step = pl.program_id(0)
    is_mid = place[0] == 1
    done_rows = done.shape[1]
    rows = done_rows // 3

    @pl.when(step == 0)
    def _():
        total[:, :done_rows] = done[...]
        total[:, done_rows:] = jnp.zeros_like(total[:, done_rows:])

    @pl.when(step < 3)
    def _():
        last = wide(jnp.where(is_mid, mid3[...], end3[...]))
        for blk, part in enumerate((own_k, far_k)):
            total[blk, done_rows:] += dot(last, paired(part))

    @pl.when((step == 3) & is_mid)
    def _():
        tiles = sky_a.shape[0]
        sky = jnp.concatenate(
            [wide(part[...]) for part in (sky_a, near_sky, peer_sky, peer_near_sky)], axis=0
        )
        for blk, part in enumerate((own_a, far_a)):
            total[blk] += dot(sky, paired(part))
        for blk, part in enumerate((near_k, near_far_k)):
            pair = jnp.concatenate([tall(part[:tiles]), tall(part[tiles:])], axis=1)
            near_total[blk] = dot(sky, pair)

        store_visibility(place, near_total, near_keep, near_send, (1, 0, 2, 3))

    @pl.when(step == 3)
    def _():
        store_visibility(place, total, keep, send, (0, 1, 2, 3))


def store_visibility(place, total, keep, send, slots):
    base = total.shape[2] // 2
    local = total.shape[1] // 8
    chunk = base // 4
    for blk in range(2):
        for two in range(2):
            planes = [[], []]
            for slot in (slots[2 * two], slots[2 * two + 1]):
                own = total[blk, slot * 2 * local : (slot + 1) * 2 * local, :]
                planes[0].append(own[:local, :base] - own[local:, base:])
                planes[1].append(own[local:, :base] + own[:local, base:])
            turned = [jnp.concatenate(planes[p], axis=0).T for p in range(2)]
            lanes = slice(two * 2 * local, (two + 1) * 2 * local)
            for near, even, odd in ((0, keep, send), (1, send, keep)):

                @pl.when(place[2] == near)
                def _():
                    for p in range(2):
                        for n in range(4):
                            out = even if n & 1 == 0 else odd
                            out[(n >> 1) ^ place[1], blk, p, :, lanes] = turned[p][
                                n * chunk : (n + 1) * chunk
                            ]


def late(place, done, own_k, far_k, mid3, own_a, far_a, sky, r2, r3, m3, chunk):
    count, rows, _ = mid3.shape
    base = own_k.shape[2]
    tiles = count // 3
    k_spec = pl.BlockSpec((2, tiles * LANES, base), lambda i: (0, jnp.minimum(i, 2), 0))
    s_spec = pl.BlockSpec((tiles, rows, LANES), lambda i: (jnp.minimum(i, 2), 0, 0))
    a_spec = pl.BlockSpec((2, tiles * LANES, base), lambda i: (0, 0, 0))
    one = pl.BlockSpec((tiles, rows, LANES), lambda i: (0, 0, 0))
    second = pl.BlockSpec((tiles, rows, LANES), lambda i: (1, 0, 0))
    third = pl.BlockSpec((tiles, rows, LANES), lambda i: (2, 0, 0))
    two = pl.BlockSpec((2 * tiles, rows, LANES), lambda i: (0, 0, 0))
    shape = (2, 2, 2, chunk, 2 * rows)
    return pl.pallas_call(
        late_kernel,
        grid=(4,),
        in_specs=[
            pl.BlockSpec(memory_space=pltpu.SMEM),
            pl.BlockSpec(done.shape, lambda i: (0, 0, 0)),
            k_spec, k_spec, s_spec, s_spec, a_spec, a_spec, one, third, one, second, two, two,
        ],
        out_specs=[pl.BlockSpec(shape, lambda i: (0,) * 5)] * 4,
        out_shape=[jax.ShapeDtypeStruct(shape, jnp.float32)] * 4,
        scratch_shapes=[
            pltpu.VMEM((2, 4 * rows, 2 * base), jnp.float32),
            pltpu.VMEM((2, 4 * rows, 2 * base), jnp.float32),
        ],
        compiler_params=pltpu.CompilerParams(vmem_limit_bytes=VMEM_LIMIT),
        cost_estimate=cost(
            flops=10 * rows * count * LANES * 2 * base, bytes_accessed=9 * 2**20, transcendentals=0
        ),
        name="late",
    )(
        place, done, own_k, far_k, mid3, r3, own_a, far_a, sky, r2, m3, m3, r2, r3
    )


def pack_kernel(place, mid, end0, end1, out):
    is_mid = place[0] == 1
    head = end0.shape[0]

    @pl.when(is_mid)
    def _():
        out[...] = mid[...]

    @pl.when(jnp.logical_not(is_mid))
    def _():
        out[:head] = end0[...]
        out[head:] = end1[...]


def pack(place, mid, end0, end1):
    vmem = pl.BlockSpec(memory_space=pltpu.VMEM)
    return pl.pallas_call(
        pack_kernel,
        in_specs=[pl.BlockSpec(memory_space=pltpu.SMEM)] + [vmem] * 3,
        out_specs=vmem,
        out_shape=jax.ShapeDtypeStruct(mid.shape, mid.dtype),
        compiler_params=pltpu.CompilerParams(vmem_limit_bytes=VMEM_LIMIT),
        cost_estimate=cost(
            flops=0, bytes_accessed=2 * mid.size * mid.dtype.itemsize, transcendentals=0
        ),
        name="pack",
    )(place, mid, end0, end1)


def split(value):
    high = value.astype(jnp.bfloat16)
    return high, (value - high.astype(jnp.float32)).astype(jnp.bfloat16)


def times(value, high, low, dims):
    rows = value.shape[0]
    upper, lower = split(value)
    both = lax.dot_general(
        jnp.concatenate([upper, lower], axis=0), high, dims, preferred_element_type=jnp.float32
    )
    rest = lax.dot_general(upper, low, dims, preferred_element_type=jnp.float32)
    return both[:rows] + both[rows:] + rest


def delay_kernel(
    place, vis0, from_x, from_y, from_d, data, keep, turn, ch, cl, sh, sl, own_out, far_out, rows, back
):
    length = keep.shape[1]
    chunk = keep.shape[0]
    local = length // 8
    norm = 1.0 / math.sqrt(length)
    nn = (((1,), (0,)), ((), ()))
    lower = place[3] == 0
    own = vis0[...] + from_x[...]
    far = from_y[...] + from_d[...]

    def plane_of(slot):
        return pl.ds(pl.multiple_of(place[4 + slot] * 2 * local, 2 * local), 2 * local)

    for slot in range(4):
        lanes = slice(slot * local, (slot + 1) * local)
        for p in range(2):
            mine, other = own[p][:, lanes], far[p][:, lanes]
            both = jnp.where(
                lower,
                jnp.concatenate([mine, other], axis=1),
                jnp.concatenate([other, mine], axis=1),
            )
            rows[p * chunk : (p + 1) * chunk, plane_of(slot)] = both
    half = length // 2
    turn_cos, turn_sin = turn[0:1], turn[1:2]
    low_half, high_half = rows[:, :half], rows[:, half:]
    plus, minus = low_half + high_half, low_half - high_half
    odd_real = minus[:chunk] * turn_cos + minus[chunk:] * turn_sin
    odd_imag = minus[chunk:] * turn_cos - minus[:chunk] * turn_sin
    value = jnp.concatenate([plus, odd_real, odd_imag], axis=0)
    cos_sum = times(value, ch[...], cl[...], nn)
    sin_sum = times(value, sh[...], sl[...], nn)
    miss = []
    for odd in range(2):
        real, imag = (slice((2 * odd + p) * chunk, (2 * odd + p + 1) * chunk) for p in range(2))
        lanes = slice(odd * half, (odd + 1) * half)
        kept = keep[:, lanes]
        spec_real = (cos_sum[real] + sin_sum[imag]) * norm
        spec_imag = (cos_sum[imag] - sin_sum[real]) * norm
        miss.append(kept * (spec_real - data[0, :, lanes].astype(jnp.float32)))
        miss.append(kept * (spec_imag - data[1, :, lanes].astype(jnp.float32)))
    miss = jnp.concatenate(miss, axis=0)
    cos_back = times(miss, ch[...], cl[...], nn)
    sin_back = times(miss, sh[...], sl[...], nn)
    even_real, odd_real = (
        cos_back[at : at + chunk] - sin_back[at + chunk : at + 2 * chunk] for at in (0, 2 * chunk)
    )
    even_imag, odd_imag = (
        cos_back[at + chunk : at + 2 * chunk] + sin_back[at : at + chunk] for at in (0, 2 * chunk)
    )
    turned_real = odd_real * turn_cos - odd_imag * turn_sin
    turned_imag = odd_imag * turn_cos + odd_real * turn_sin
    back[:chunk, :half] = (even_real + turned_real) * norm
    back[:chunk, half:] = (even_real - turned_real) * norm
    back[chunk:, :half] = (even_imag + turned_imag) * norm
    back[chunk:, half:] = (even_imag - turned_imag) * norm
    for p in range(2):
        found = [back[p * chunk : (p + 1) * chunk, plane_of(slot)] for slot in range(4)]
        first = jnp.concatenate([f[:, :local] for f in found], axis=1)
        second = jnp.concatenate([f[:, local:] for f in found], axis=1)
        own_out[p] = jnp.where(lower, first, second).astype(jnp.bfloat16)
        far_out[p] = jnp.where(lower, second, first).astype(jnp.bfloat16)


def delay(place, *parts):
    shape = jax.ShapeDtypeStruct(parts[0].shape, jnp.bfloat16)
    chunk, length = parts[5].shape
    vmem = pl.BlockSpec(memory_space=pltpu.VMEM)
    return pl.pallas_call(
        delay_kernel,
        in_specs=[pl.BlockSpec(memory_space=pltpu.SMEM)] + [vmem] * len(parts),
        out_specs=(vmem, vmem),
        out_shape=(shape, shape),
        scratch_shapes=[pltpu.VMEM((2 * chunk, length), jnp.float32)] * 2,
        compiler_params=pltpu.CompilerParams(vmem_limit_bytes=VMEM_LIMIT),
        cost_estimate=cost(
            flops=24 * chunk * length * length, bytes_accessed=8 * length * length, transcendentals=0
        ),
        name="delay",
    )(place, *parts)


def field_rows(place, half, other, slots, out, at):
    chunk, local = half.shape[3], half.shape[4] // 4
    base = 4 * chunk
    for blk in range(2):
        for n in range(4):
            hi, lo = (n >> 1) ^ place[1], (n & 1) ^ place[2]
            planes = [
                jnp.where(
                    lo == 0,
                    half[hi, blk, p].astype(jnp.float32),
                    other[hi, blk, p].astype(jnp.float32),
                )
                for p in range(2)
            ]
            first = at + blk * 2 * base + n * chunk
            for i, s in enumerate(slots):
                real = planes[0][:, s * local : (s + 1) * local]
                imag = planes[1][:, s * local : (s + 1) * local]
                lanes = slice(i * 2 * local, (i + 1) * 2 * local)
                upper = jnp.concatenate([real, imag], axis=1)
                lower = jnp.concatenate([imag, -real], axis=1)
                out[first : first + chunk, lanes] = upper.astype(jnp.bfloat16)
                out[first + base : first + base + chunk, lanes] = lower.astype(jnp.bfloat16)


def store_tiles(sums, slot, out):
    lanes = slice(slot * LANES, (slot + 1) * LANES)
    for t in range(out.shape[0]):
        out[t] = sums[t * LANES : (t + 1) * LANES, lanes].T.astype(out.dtype)


def adjoint_kernel(slots, ends_only, place, half, other, own_k, far_k, *rest):
    outs, field = rest[:-1], rest[-1]
    step = pl.program_id(0)

    @pl.when((place[0] == 0) | (not ends_only))
    def _():
        @pl.when(step == 0)
        def _():
            field_rows(place, half, other, slots, field, 0)

        cells = jnp.concatenate([own_k[0], own_k[1], far_k[0], far_k[1]], axis=1)
        sums = dot(cells, field[...])
        for i in range(len(slots)):

            @pl.when(step == 0)
            def _():
                store_tiles(sums, i, outs[2 * i])

            @pl.when(step > 0)
            def _():
                store_tiles(sums, i, outs[2 * i + 1])


def adjoint(place, half, other, own_k, far_k, slots, dtype, ends_only=False):
    base = own_k.shape[2]
    count = own_k.shape[1] // LANES
    tiles = count // 3
    rows = half.shape[4] // 2
    k_spec = pl.BlockSpec((2, tiles * LANES, base), lambda i: (0, i, 0))
    f_spec = pl.BlockSpec(half.shape, lambda i: (0,) * 5)
    block = (tiles, rows, LANES)
    outs = pl.pallas_call(
        functools.partial(adjoint_kernel, slots, ends_only),
        grid=(3,),
        in_specs=[pl.BlockSpec(memory_space=pltpu.SMEM), f_spec, f_spec, k_spec, k_spec],
        out_specs=[
            pl.BlockSpec(block, lambda i: (0, 0, 0)),
            pl.BlockSpec(block, lambda i: (jnp.maximum(i - 1, 0), 0, 0)),
        ]
        * len(slots),
        out_shape=[
            jax.ShapeDtypeStruct((n * tiles, rows, LANES), dtype) for _ in slots for n in (1, 2)
        ],
        scratch_shapes=[pltpu.VMEM((4 * base, rows * len(slots)), jnp.bfloat16)],
        compiler_params=pltpu.CompilerParams(vmem_limit_bytes=VMEM_LIMIT),
        cost_estimate=cost(
            flops=8 * rows * len(slots) * count * LANES * base,
            bytes_accessed=(4 + 2 * len(slots)) * 2**20,
            transcendentals=0,
            times=20,
        ),
        name="adjoint",
    )(place, half, other, own_k, far_k)
    return [outs[2 * i : 2 * i + 2] for i in range(len(slots))]


def first_kernel(slot, place, half, other, own_k, far_k, out, field):
    @pl.when(place[0] == 0)
    def _():
        @pl.when(pl.program_id(0) == 0)
        def _():
            field_rows(place, half, other, (slot,), field, 0)

        cells = jnp.concatenate([own_k[0], own_k[1], far_k[0], far_k[1]], axis=1)
        store_tiles(dot(cells, field[...]), 0, out)


def first_adjoint(place, half, other, own_k, far_k, slot, begin, steps):
    base = own_k.shape[2]
    tiles = own_k.shape[1] // LANES // 3
    rows = half.shape[4] // 2
    k_spec = pl.BlockSpec((2, tiles * LANES, base), lambda i: (0, i + begin, 0))
    f_spec = pl.BlockSpec(half.shape, lambda i: (0,) * 5)
    return pl.pallas_call(
        functools.partial(first_kernel, slot),
        grid=(steps,),
        in_specs=[pl.BlockSpec(memory_space=pltpu.SMEM), f_spec, f_spec, k_spec, k_spec],
        out_specs=pl.BlockSpec((tiles, rows, LANES), lambda i: (i, 0, 0)),
        out_shape=jax.ShapeDtypeStruct((steps * tiles, rows, LANES), jnp.bfloat16),
        scratch_shapes=[pltpu.VMEM((4 * base, rows), jnp.bfloat16)],
        compiler_params=pltpu.CompilerParams(vmem_limit_bytes=VMEM_LIMIT),
        cost_estimate=cost(
            flops=8 * rows * steps * tiles * LANES * base,
            bytes_accessed=steps * 2**21,
            transcendentals=0,
            times=20,
        ),
        name="first_adjoint",
    )(place, half, other, own_k, far_k)


def near_kernel(
    place, half, other, near_half, near_other, own_a, far_a, near_k, near_far_k, send, part1, part0,
    field
):
    @pl.when(place[0] == 1)
    def _():
        field_rows(place, half, other, (3, 2, 1, 0), field, 0)
        rows = field.shape[0] // 2
        field_rows(place, near_half, near_other, (3, 2, 0, 1), field, rows)
        tiles = near_k.shape[0] // 2
        cells = jnp.concatenate(
            [own_a[0], own_a[1], far_a[0], far_a[1]]
            + [tall(part[i * tiles : (i + 1) * tiles]) for part in (near_k, near_far_k) for i in (0, 1)],
            axis=1,
        )
        sums = dot(cells, field[...])
        outs = (send.at[pl.ds(0, tiles)], send.at[pl.ds(tiles, tiles)], part1, part0)
        for i, out in enumerate(outs):
            store_tiles(sums, i, out)


def near_adjoint(place, half, other, near_half, near_other, own_a, far_a, r2, r3):
    base = own_a.shape[2]
    tiles = own_a.shape[1] // LANES
    rows = half.shape[4] // 2
    whole = lambda a: pl.BlockSpec(a.shape, lambda i: (0,) * a.ndim)
    two = pl.BlockSpec((2 * tiles, LANES, rows), lambda i: (0, 0, 0))
    one = pl.BlockSpec((tiles, LANES, rows), lambda i: (0, 0, 0))
    types = ((2, jnp.bfloat16), (1, jnp.float32), (1, jnp.float32))
    return pl.pallas_call(
        near_kernel,
        grid=(1,),
        in_specs=[pl.BlockSpec(memory_space=pltpu.SMEM)]
        + [whole(a) for a in (half, other, near_half, near_other, own_a, far_a)]
        + [two, two],
        out_specs=[two, one, one],
        out_shape=[jax.ShapeDtypeStruct((n * tiles, LANES, rows), t) for n, t in types],
        scratch_shapes=[pltpu.VMEM((8 * base, rows * 4), jnp.bfloat16)],
        compiler_params=pltpu.CompilerParams(vmem_limit_bytes=VMEM_LIMIT),
        cost_estimate=cost(
            flops=64 * rows * tiles * LANES * base,
            bytes_accessed=6 * 2**20,
            transcendentals=0,
            times=20,
        ),
        name="near_adjoint",
    )(place, half, other, near_half, near_other, own_a, far_a, r2, r3)


def final_kernel(place, part_a, peer_a, end_a, *rest):
    part_b, near_b, far_b = (rest[2 * i : 2 * i + 2] for i in range(3))
    out = rest[-1]
    step = pl.program_id(0)
    is_mid = place[0] == 1
    local = out.shape[0]

    def store(value):
        for t in range(value.shape[0]):
            lanes = slice(t * LANES, (t + 1) * LANES)
            out[:, 0, lanes] = value[t][:local]
            out[:, 1, lanes] = value[t][local:]

    @pl.when(step == 0)
    def _():
        mid = part_a[...] + peer_a[...].astype(jnp.float32)
        store(jnp.where(is_mid, mid, end_a[...].astype(jnp.float32)))

    @pl.when(step > 0)
    def _():
        def piece(parts):
            return jnp.where(step == 1, parts[0][...], parts[1][...]).astype(jnp.float32)

        store(piece(part_b) + piece(near_b) + jnp.where(is_mid, piece(far_b), 0.0))


def final(place, part_a, peer_a, end_a, part_b, near_b, far_b):
    tiles, _, rows = part_a.shape
    count = 4 * tiles
    shape = (tiles, LANES, rows)
    one = pl.BlockSpec(shape, lambda i: (0, 0, 0))
    second = pl.BlockSpec(shape, lambda i: (1, 0, 0))
    rest = pl.BlockSpec(shape, lambda i: (jnp.maximum(i - 2, 0), 0, 0))
    return pl.pallas_call(
        final_kernel,
        grid=(4,),
        in_specs=[pl.BlockSpec(memory_space=pltpu.SMEM), one, second, one] + [one, rest] * 3,
        out_specs=pl.BlockSpec((rows // 2, 2, tiles * LANES), lambda i: (0, 0, i)),
        out_shape=jax.ShapeDtypeStruct((rows // 2, 2, count * LANES), jnp.float32),
        compiler_params=pltpu.CompilerParams(vmem_limit_bytes=VMEM_LIMIT),
        cost_estimate=cost(
            flops=4 * rows * count * LANES, bytes_accessed=6 * 2**20, transcendentals=0
        ),
        name="final",
    )(place, part_a, peer_a, end_a, *part_b, *near_b, *far_b)


def table_parts(length):
    half = length // 2
    steps = np.arange(half)
    turn = steps * (2.0 * math.pi / length)
    parts = [np.stack([np.cos(turn), np.sin(turn)]).astype(np.float32)]
    angle = (steps[:, None] * steps[None, :] % half) * (2.0 * math.pi / half)
    for table in (np.cos(angle), np.sin(angle)):
        high = table.astype(ml_dtypes.bfloat16)
        parts += [high, (table - high.astype(np.float64)).astype(ml_dtypes.bfloat16)]
    return [jnp.asarray(part) for part in parts]


def line_body(sky, kernel, data, block_tiles, length_bin, wedge_keep):
    length = data.shape[3]
    local, cells = sky.shape[1], sky.shape[3]
    base = kernel.shape[4]
    hi, lo = lax.axis_index("th"), lax.axis_index("tl")
    zpos, ypos = lax.axis_index("outer"), lax.axis_index("inner")
    tile_pos = hi * 2 + lo
    chunk = base // 4
    is_mid = (zpos == 1) | (zpos == 2)
    order = jnp.array([[0, 1, 2, 3], [1, 0, 2, 3], [2, 3, 1, 0], [3, 2, 1, 0]], jnp.int32)[zpos]
    place = jnp.concatenate([jnp.stack([is_mid.astype(jnp.int32), hi, lo, ypos]), order])

    tiles = cells // LANES // 4
    cut = tiles * LANES
    own_sky = sky[0].reshape(local, 2, cells // LANES, LANES).transpose(2, 1, 0, 3)
    own_sky = own_sky.reshape(cells // LANES, 2 * local, LANES)
    sky_a, sky_b = own_sky[:tiles], own_sky[tiles:]
    def ends(*values):
        return [lax.ppermute(value, "outer", ENDS) for value in values]

    def mids(*values):
        return [lax.ppermute(value, ("tl", "outer"), MIDS) for value in values]

    def as_tiles(part):
        return part.reshape(2 * tiles, LANES, base)

    (r1,) = ends(sky_b)
    (m1,) = mids(sky_b)
    column = jnp.arange(block_tiles.shape[1], dtype=jnp.int32) == tile_pos
    weight = jnp.sum(jnp.where(column, block_tiles[0], 0)).astype(jnp.bfloat16)
    own_a = lax.optimization_barrier(kernel[0, 0, :, :cut] * weight)
    own_b = kernel[0, 0, :, cut:] * weight
    far_a = lax.ppermute(own_a, "inner", SWAP)
    (m2,) = mids(r1)
    own_b, far_a, m1 = lax.optimization_barrier((own_b, far_a, m1))
    far_b = lax.ppermute(own_b, "inner", SWAP)
    (r2,) = ends(pack(place, m1, as_tiles(own_a), sky_a))
    (r3,) = ends(pack(place, m2, as_tiles(far_a), sky_a))
    (m3,) = mids(jnp.concatenate([sky_a, r2[2 * tiles :]]))

    parts = table_parts(length)
    def by_parity(value):
        pairs = value.reshape(value.shape[:-1] + (length // 2, 2))
        return jnp.swapaxes(pairs, -1, -2).reshape(value.shape)

    own_data = by_parity(lax.dynamic_slice_in_dim(data[0], tile_pos * chunk, chunk, 1))
    own_bins = lax.dynamic_slice_in_dim(length_bin[0], tile_pos * chunk, chunk, 0)
    keep = by_parity(wedge_keep.astype(jnp.float32))[own_bins]

    done = early(place, own_b, far_b, own_sky, r1, m1, r2, (own_data, keep))
    keep_vis, send_vis, near_keep, near_send = late(
        place, done, own_b, far_b, m2, own_a, far_a, own_sky, r2, r3, m3, chunk
    )
    (near,) = ends(near_sum(near_keep, lax.ppermute(near_send, "tl", SWAP)))
    got = lax.ppermute(send_vis, "tl", SWAP)
    mine, to_x, to_y, to_d = own_sum(place, keep_vis, got, near)
    from_x = lax.ppermute(to_x, "th", SWAP)
    from_y = lax.ppermute(to_y, "inner", SWAP)
    from_d = lax.ppermute(to_d, ("th", "inner"), DIAG)
    own_back, far_back = delay(place, mine, from_x, from_y, from_d, own_data, keep, *parts)
    back_x = lax.ppermute(own_back, "th", SWAP)
    back_y = lax.ppermute(far_back, "inner", SWAP)
    back_d = lax.ppermute(far_back, ("th", "inner"), DIAG)
    half = jnp.stack([jnp.stack([own_back, back_y]), jnp.stack([back_x, back_d])])
    other = lax.ppermute(half, "tl", SWAP)
    (near_half,) = ends(half)

    low = jnp.bfloat16

    def plus(part, got):
        return (part + got.astype(jnp.float32)).astype(low)

    send3 = [first_adjoint(place, half, other, own_b, far_b, 3, *part) for part in PARTS]
    g1 = ends(*send3)
    near_half, _ = lax.optimization_barrier((near_half, send3[1]))
    near_other = lax.ppermute(near_half, "tl", SWAP)
    send_a, part1_a, part0_a = near_adjoint(
        place, half, other, near_half, near_other, own_a, far_a, r2, r3
    )
    (peer_a,) = mids(send_a)
    half, send_a = lax.optimization_barrier((half, send_a))
    part3, part2, part1, part0 = adjoint(
        place, half, other, own_b, far_b, (3, 2, 1, 0), jnp.float32
    )
    far3 = mids(*(plus(part, got) for part, got in zip(part3, g1)))
    first = jnp.where(is_mid, plus(part1_a, peer_a[:tiles]), part2[0].astype(low))
    (g2,) = ends(jnp.concatenate([first, part2[1].astype(low)]))
    far2 = mids(plus(part2[0], g2[:tiles]), plus(part2[1], g2[tiles:]))
    g3 = ends(
        *(plus(part, jnp.where(is_mid, got, jnp.zeros_like(got))) for part, got in zip(part1, far3))
    )
    return final(place, part0_a, peer_a, g2, part0, g3, far2)[None]


def body(sky, kernel, *rest):
    local, cells = sky.shape[1], sky.shape[3]
    line = lax.axis_size("outer") == 4 and 2 * local == LANES and kernel.shape[4] == LANES
    chosen = line_body if line and cells % (4 * LANES) == 0 else any_body
    return chosen(sky, kernel, *rest)


def solution(mesh):
    tiles, freqs = mesh.shape["tile"], mesh.shape["freq"]
    fine = Mesh(mesh.devices.reshape(tiles // 2, 2, freqs // 2, 2), ("th", "tl", "outer", "inner"))
    tile, freq = ("th", "tl"), ("outer", "inner")
    return jax.shard_map(
        body,
        mesh=fine,
        in_specs=(
            P(tile, freq, None, None),
            P(tile, freq, None, None, None),
            P(freq, None, None, None),
            P(freq, None),
            P(freq, None),
            P(),
        ),
        out_specs=P(tile, freq, None, None),
        check_vma=False,
    )
```

```python
import functools
import math

import jax
import jax.numpy as jnp
import ml_dtypes
import numpy as np
from jax import lax
from jax.experimental import pallas as pl
from jax.experimental.pallas import tpu as pltpu
from jax.sharding import Mesh, PartitionSpec as P

SWAP = [(0, 1), (1, 0)]
ENDS = [(0, 1), (1, 0), (2, 3), (3, 2)]
MIDS = [(1, 2), (2, 1), (5, 6), (6, 5), (0, 4), (4, 0), (3, 7), (7, 3)]
DIAG = [(0, 3), (1, 2), (2, 1), (3, 0)]
LANES = 128
PARTS = ((0, 1), (1, 2))
VMEM_LIMIT = 24 * 2**20
NT = (((1,), (1,)), ((), ()))


def cost(flops, bytes_accessed, transcendentals, times=1):
    return pl.CostEstimate(
        flops=times * flops, bytes_accessed=times * bytes_accessed, transcendentals=transcendentals
    )


def xor_chunks(rows, hi, lo):
    planes, count, cells = rows.shape
    rows = rows.reshape(planes, 2, 2, count // 4, cells)
    rows = jnp.where(hi == 1, rows[:, ::-1], rows)
    rows = jnp.where(lo == 1, rows[:, :, ::-1], rows)
    return rows.reshape(planes * count, cells)


def project(kernel_rows, sky_rows):
    out = lax.dot_general(
        kernel_rows, sky_rows, (((1,), (1,)), ((), ())), preferred_element_type=jnp.float32
    )
    base, chans = out.shape[0] // 2, out.shape[1] // 2
    real = out[:base, :chans] - out[base:, chans:]
    imag = out[:base, chans:] + out[base:, :chans]
    return jnp.stack([real, imag])


def adjoint_any(field, kernel_rows):
    total = 0.0
    for blk in range(2):
        real, imag = field[blk][0], field[blk][1]
        lhs = jnp.concatenate(
            [jnp.concatenate([real, imag], 1), jnp.concatenate([imag, -real], 1)], 0
        )
        total = total + lax.dot_general(
            lhs, kernel_rows[blk], (((0,), (0,)), ((), ())), preferred_element_type=jnp.float32
        )
    return total


def tables(channels, length):
    product = channels[:, None] * jnp.arange(length, dtype=jnp.int32)[None, :] % length
    angle = product.astype(jnp.float32) * (2.0 * math.pi / length)
    return jnp.cos(angle), jnp.sin(angle)


def mm(a, b):
    return jnp.einsum("bc,ck->bk", a, b, precision=lax.Precision.HIGHEST)


def mmt(a, b):
    return jnp.einsum("bk,ck->bc", a, b, precision=lax.Precision.HIGHEST)


def any_body(sky, kernel, data, block_tiles, length_bin, wedge_keep):
    length = data.shape[3]
    local, cells = sky.shape[1], sky.shape[3]
    base = kernel.shape[4]
    hi, lo = lax.axis_index("th"), lax.axis_index("tl")
    zpos, ypos = lax.axis_index("outer"), lax.axis_index("inner")
    depth = lax.axis_size("outer")
    tile_pos = hi * 2 + lo
    chunk = base // 4

    column = jnp.arange(block_tiles.shape[1], dtype=jnp.int32) == tile_pos
    weight = jnp.sum(jnp.where(column, block_tiles[0], 0)).astype(jnp.bfloat16)

    own_sky = sky[0].transpose(1, 0, 2).reshape(2 * local, cells)
    own_rows = xor_chunks((kernel[0, 0] * weight).transpose(0, 2, 1), hi, lo)
    kernels = [own_rows, lax.ppermute(own_rows, "inner", SWAP)]

    every = lax.all_gather(own_sky, "outer")
    order = jnp.arange(depth, dtype=jnp.int32)
    vis = [
        jnp.concatenate([project(rows, every[s]) for s in range(depth)], axis=2)
        for rows in kernels
    ]

    def channels(half):
        place = (order[:, None] * 2 + half) * local + jnp.arange(local, dtype=jnp.int32)[None, :]
        return place.reshape(-1)

    own_cos, own_sin = tables(channels(ypos), length)
    far_cos, far_sin = tables(channels(1 - ypos), length)

    count = vis[0].shape[2]
    vis = jnp.stack(vis).reshape(2, 2, 2, 2, chunk, count)
    vis = vis[:, :, :, 0] + lax.ppermute(vis[:, :, :, 1], "tl", SWAP)
    from_x = lax.ppermute(vis[0, :, 1], "th", SWAP)
    from_y = lax.ppermute(vis[1, :, 0], "inner", SWAP)
    from_d = lax.ppermute(vis[1, :, 1], ("th", "inner"), DIAG)
    own_vis = vis[0, :, 0] + from_x
    far_vis = from_y + from_d

    norm = 1.0 / math.sqrt(length)
    own_data = lax.dynamic_slice_in_dim(data[0], tile_pos * chunk, chunk, 1).astype(jnp.float32)
    own_bins = lax.dynamic_slice_in_dim(length_bin[0], tile_pos * chunk, chunk, 0)
    keep = wedge_keep[own_bins].astype(jnp.float32)
    cos_sum = [mm(own_vis[p], own_cos) + mm(far_vis[p], far_cos) for p in range(2)]
    sin_sum = [mm(own_vis[p], own_sin) + mm(far_vis[p], far_sin) for p in range(2)]
    miss_real = keep * ((cos_sum[0] + sin_sum[1]) * norm - own_data[0])
    miss_imag = keep * ((cos_sum[1] - sin_sum[0]) * norm - own_data[1])

    def back(cosine, sine):
        real = (mmt(miss_real, cosine) - mmt(miss_imag, sine)) * norm
        imag = (mmt(miss_imag, cosine) + mmt(miss_real, sine)) * norm
        return jnp.stack([real, imag]).astype(jnp.bfloat16)

    own_back, far_back = back(own_cos, own_sin), back(far_cos, far_sin)
    back_x = lax.ppermute(own_back, "th", SWAP)
    back_y = lax.ppermute(far_back, "inner", SWAP)
    back_d = lax.ppermute(far_back, ("th", "inner"), DIAG)
    half = jnp.stack([jnp.stack([own_back, back_x], 1), jnp.stack([back_y, back_d], 1)])
    other = lax.ppermute(half, "tl", SWAP)
    field = jnp.stack([half, other], 3).reshape(2, 2, base, count)

    def update(slot):
        return adjoint_any(field[..., slot * local : (slot + 1) * local], kernels)

    every = jnp.concatenate([update(s) for s in range(depth)], 0)
    gradient = lax.psum_scatter(every, "outer", scatter_dimension=0, tiled=True)
    return gradient.reshape(2, local, cells).transpose(1, 0, 2)[None]


def wide(tiles):
    return jnp.concatenate([tiles[t] for t in range(tiles.shape[0])], axis=1)


def paired(part):
    return jnp.concatenate([part[0], part[1]], axis=1)


def tall(tiles):
    return tiles.reshape(tiles.shape[0] * tiles.shape[1], tiles.shape[2])


def dot(a, b):
    return jnp.dot(a, b, preferred_element_type=jnp.float32)


def near_sum_kernel(keep, got, out):
    out[...] = (keep[...] + got[...]).astype(out.dtype)


def near_sum(keep, got):
    vmem = pl.BlockSpec(memory_space=pltpu.VMEM)
    return pl.pallas_call(
        near_sum_kernel,
        in_specs=[vmem, vmem],
        out_specs=vmem,
        out_shape=jax.ShapeDtypeStruct(keep.shape, jnp.bfloat16),
        compiler_params=pltpu.CompilerParams(vmem_limit_bytes=VMEM_LIMIT),
        cost_estimate=cost(flops=keep.size, bytes_accessed=10 * keep.size, transcendentals=0),
        name="near_sum",
    )(keep, got)


def own_sum_kernel(place, keep, got, near, mine, to_x, to_y, to_d):
    for hi, blk, out in ((0, 0, mine), (1, 0, to_x), (0, 1, to_y), (1, 1, to_d)):
        added = jnp.where(place[0] == 1, 0.0, near[hi, blk].astype(jnp.float32))
        out[...] = keep[hi, blk] + got[hi, blk] + added


def own_sum(place, keep, got, near):
    vmem = pl.BlockSpec(memory_space=pltpu.VMEM)
    shape = keep.shape[2:]
    return pl.pallas_call(
        own_sum_kernel,
        in_specs=[pl.BlockSpec(memory_space=pltpu.SMEM)] + [vmem] * 3,
        out_specs=[vmem] * 4,
        out_shape=[jax.ShapeDtypeStruct(shape, jnp.float32)] * 4,
        compiler_params=pltpu.CompilerParams(vmem_limit_bytes=VMEM_LIMIT),
        cost_estimate=cost(flops=2 * keep.size, bytes_accessed=14 * keep.size, transcendentals=0),
        name="own_sum",
    )(place, keep, got, near)


def early_kernel(place, own_k, slot0, slot1, mid2, end2, *rest):
    total = rest[-1]

    @pl.when(pl.program_id(0) == 0)
    def _():
        total[...] = jnp.zeros_like(total)

    third = jnp.where(place[0] == 1, mid2[...], end2[...])
    rows = jnp.concatenate([wide(slot0[...]), wide(slot1[...]), wide(third)], axis=0)
    total[...] += dot(rows, paired(own_k))


def early(place, own_k, sky, r1, m1, r2, ready):
    count, rows, _ = r1.shape
    base = own_k.shape[2]
    tiles = count // 3
    k_spec = pl.BlockSpec((2, tiles * LANES, base), lambda i: (0, i, 0))
    s_spec = pl.BlockSpec((tiles, rows, LANES), lambda i: (i, 0, 0))
    shape = (3 * rows, 2 * base)
    return pl.pallas_call(
        early_kernel,
        grid=(3,),
        in_specs=[pl.BlockSpec(memory_space=pltpu.SMEM), k_spec]
        + [s_spec] * 4
        + [pl.BlockSpec(memory_space=pl.ANY)] * len(ready),
        out_specs=pl.BlockSpec(shape, lambda i: (0, 0)),
        out_shape=jax.ShapeDtypeStruct(shape, jnp.float32),
        compiler_params=pltpu.CompilerParams(vmem_limit_bytes=VMEM_LIMIT),
        cost_estimate=cost(
            flops=6 * rows * count * LANES * 2 * base, bytes_accessed=4 * 2**20, transcendentals=0
        ),
        name="early",
    )(place, own_k, sky, r1, m1, r2, *ready)


def late_kernel(
    place, done, own_k, far_k, slot0, slot1, mid2, end2, mid3, end3, own_a, far_a, sky_a, near_sky, peer_sky, peer_near_sky,
    near_k, near_far_k, keep, send, near_keep, near_send, total, near_total
):
    step = pl.program_id(0)
    is_mid = place[0] == 1
    done_rows = done.shape[0]
    rows = done_rows // 3

    @pl.when(step == 0)
    def _():
        total[0, :done_rows] = done[...]
        total[0, done_rows:] = jnp.zeros_like(total[0, done_rows:])
        total[1] = jnp.zeros_like(total[1])

    @pl.when(step < 3)
    def _():
        third = wide(jnp.where(is_mid, mid2[...], end2[...]))
        last = wide(jnp.where(is_mid, mid3[...], end3[...]))
        every = jnp.concatenate([wide(slot0[...]), wide(slot1[...]), third, last], axis=0)
        total[0, done_rows:] += dot(last, paired(own_k))
        total[1] += dot(every, paired(far_k))

    @pl.when((step == 3) & is_mid)
    def _():
        tiles = sky_a.shape[0]
        sky = jnp.concatenate(
            [wide(part[...]) for part in (sky_a, near_sky, peer_sky, peer_near_sky)], axis=0
        )
        for blk, part in enumerate((own_a, far_a)):
            total[blk] += dot(sky, paired(part))
        for blk, part in enumerate((near_k, near_far_k)):
            pair = jnp.concatenate([tall(part[:tiles]), tall(part[tiles:])], axis=1)
            near_total[blk] = dot(sky, pair)

        store_visibility(place, near_total, near_keep, near_send, (1, 0, 2, 3))

    @pl.when(step == 3)
    def _():
        store_visibility(place, total, keep, send, (0, 1, 2, 3))


def store_visibility(place, total, keep, send, slots):
    base = total.shape[2] // 2
    local = total.shape[1] // 8
    chunk = base // 4
    for blk in range(2):
        for two in range(2):
            planes = [[], []]
            for slot in (slots[2 * two], slots[2 * two + 1]):
                own = total[blk, slot * 2 * local : (slot + 1) * 2 * local, :]
                planes[0].append(own[:local, :base] - own[local:, base:])
                planes[1].append(own[local:, :base] + own[:local, base:])
            turned = [jnp.concatenate(planes[p], axis=0).T for p in range(2)]
            lanes = slice(two * 2 * local, (two + 1) * 2 * local)
            for near, even, odd in ((0, keep, send), (1, send, keep)):

                @pl.when(place[2] == near)
                def _():
                    for p in range(2):
                        for n in range(4):
                            out = even if n & 1 == 0 else odd
                            out[(n >> 1) ^ place[1], blk, p, :, lanes] = turned[p][
                                n * chunk : (n + 1) * chunk
                            ]


def late(place, done, own_k, far_k, sky_b, r1, m1, m2, own_a, far_a, sky_a, r2, r3, m3, chunk):
    count, rows, _ = m2.shape
    base = own_k.shape[2]
    tiles = count // 3
    k_spec = pl.BlockSpec((2, tiles * LANES, base), lambda i: (0, jnp.minimum(i, 2), 0))
    s_spec = pl.BlockSpec((tiles, rows, LANES), lambda i: (jnp.minimum(i, 2), 0, 0))
    a_spec = pl.BlockSpec((2, tiles * LANES, base), lambda i: (0, 0, 0))
    one = pl.BlockSpec((tiles, rows, LANES), lambda i: (0, 0, 0))
    second = pl.BlockSpec((tiles, rows, LANES), lambda i: (1, 0, 0))
    third = pl.BlockSpec((tiles, rows, LANES), lambda i: (2, 0, 0))
    two = pl.BlockSpec((2 * tiles, rows, LANES), lambda i: (0, 0, 0))
    shape = (2, 2, 2, chunk, 2 * rows)
    return pl.pallas_call(
        late_kernel,
        grid=(4,),
        in_specs=[
            pl.BlockSpec(memory_space=pltpu.SMEM),
            pl.BlockSpec(done.shape, lambda i: (0, 0)),
            k_spec, k_spec, s_spec, s_spec, s_spec, s_spec, s_spec, s_spec, a_spec, a_spec, one, third, one, second, two, two,
        ],
        out_specs=[pl.BlockSpec(shape, lambda i: (0,) * 5)] * 4,
        out_shape=[jax.ShapeDtypeStruct(shape, jnp.float32)] * 4,
        scratch_shapes=[
            pltpu.VMEM((2, 4 * rows, 2 * base), jnp.float32),
            pltpu.VMEM((2, 4 * rows, 2 * base), jnp.float32),
        ],
        compiler_params=pltpu.CompilerParams(vmem_limit_bytes=VMEM_LIMIT),
        cost_estimate=cost(
            flops=10 * rows * count * LANES * 2 * base, bytes_accessed=9 * 2**20, transcendentals=0
        ),
        name="late",
    )(
        place, done, own_k, far_k, sky_b, r1, m1, r2, m2, r3, own_a, far_a, sky_a, r2, m3, m3, r2, r3
    )


def pack_kernel(place, mid, end0, end1, out):
    is_mid = place[0] == 1
    head = end0.shape[0]

    @pl.when(is_mid)
    def _():
        out[...] = mid[...]

    @pl.when(jnp.logical_not(is_mid))
    def _():
        out[:head] = end0[...]
        out[head:] = end1[...]


def pack(place, mid, end0, end1):
    vmem = pl.BlockSpec(memory_space=pltpu.VMEM)
    return pl.pallas_call(
        pack_kernel,
        in_specs=[pl.BlockSpec(memory_space=pltpu.SMEM)] + [vmem] * 3,
        out_specs=vmem,
        out_shape=jax.ShapeDtypeStruct(mid.shape, mid.dtype),
        compiler_params=pltpu.CompilerParams(vmem_limit_bytes=VMEM_LIMIT),
        cost_estimate=cost(
            flops=0, bytes_accessed=2 * mid.size * mid.dtype.itemsize, transcendentals=0
        ),
        name="pack",
    )(place, mid, end0, end1)


def split(value):
    high = value.astype(jnp.bfloat16)
    return high, (value - high.astype(jnp.float32)).astype(jnp.bfloat16)


def times(value, high, low, dims):
    rows = value.shape[0]
    upper, lower = split(value)
    both = lax.dot_general(
        jnp.concatenate([upper, lower], axis=0), high, dims, preferred_element_type=jnp.float32
    )
    rest = lax.dot_general(upper, low, dims, preferred_element_type=jnp.float32)
    return both[:rows] + both[rows:] + rest


def delay_kernel(
    place, vis0, from_x, from_y, from_d, data, keep, turn, ch, cl, sh, sl, own_out, far_out, rows, back
):
    length = keep.shape[1]
    chunk = keep.shape[0]
    local = length // 8
    norm = 1.0 / math.sqrt(length)
    nn = (((1,), (0,)), ((), ()))
    lower = place[3] == 0
    own = vis0[...] + from_x[...]
    far = from_y[...] + from_d[...]

    def plane_of(slot):
        return pl.ds(pl.multiple_of(place[4 + slot] * 2 * local, 2 * local), 2 * local)

    for slot in range(4):
        lanes = slice(slot * local, (slot + 1) * local)
        for p in range(2):
            mine, other = own[p][:, lanes], far[p][:, lanes]
            both = jnp.where(
                lower,
                jnp.concatenate([mine, other], axis=1),
                jnp.concatenate([other, mine], axis=1),
            )
            rows[p * chunk : (p + 1) * chunk, plane_of(slot)] = both
    half = length // 2
    turn_cos, turn_sin = turn[0:1], turn[1:2]
    low_half, high_half = rows[:, :half], rows[:, half:]
    plus, minus = low_half + high_half, low_half - high_half
    odd_real = minus[:chunk] * turn_cos + minus[chunk:] * turn_sin
    odd_imag = minus[chunk:] * turn_cos - minus[:chunk] * turn_sin
    value = jnp.concatenate([plus, odd_real, odd_imag], axis=0)
    cos_sum = times(value, ch[...], cl[...], nn)
    sin_sum = times(value, sh[...], sl[...], nn)
    miss = []
    for odd in range(2):
        real, imag = (slice((2 * odd + p) * chunk, (2 * odd + p + 1) * chunk) for p in range(2))
        lanes = slice(odd * half, (odd + 1) * half)
        kept = keep[:, lanes]
        spec_real = (cos_sum[real] + sin_sum[imag]) * norm
        spec_imag = (cos_sum[imag] - sin_sum[real]) * norm
        miss.append(kept * (spec_real - data[0, :, lanes].astype(jnp.float32)))
        miss.append(kept * (spec_imag - data[1, :, lanes].astype(jnp.float32)))
    miss = jnp.concatenate(miss, axis=0)
    cos_back = times(miss, ch[...], cl[...], nn)
    sin_back = times(miss, sh[...], sl[...], nn)
    even_real, odd_real = (
        cos_back[at : at + chunk] - sin_back[at + chunk : at + 2 * chunk] for at in (0, 2 * chunk)
    )
    even_imag, odd_imag = (
        cos_back[at + chunk : at + 2 * chunk] + sin_back[at : at + chunk] for at in (0, 2 * chunk)
    )
    turned_real = odd_real * turn_cos - odd_imag * turn_sin
    turned_imag = odd_imag * turn_cos + odd_real * turn_sin
    back[:chunk, :half] = (even_real + turned_real) * norm
    back[:chunk, half:] = (even_real - turned_real) * norm
    back[chunk:, :half] = (even_imag + turned_imag) * norm
    back[chunk:, half:] = (even_imag - turned_imag) * norm
    for p in range(2):
        found = [back[p * chunk : (p + 1) * chunk, plane_of(slot)] for slot in range(4)]
        first = jnp.concatenate([f[:, :local] for f in found], axis=1)
        second = jnp.concatenate([f[:, local:] for f in found], axis=1)
        own_out[p] = jnp.where(lower, first, second).astype(jnp.bfloat16)
        far_out[p] = jnp.where(lower, second, first).astype(jnp.bfloat16)


def delay(place, *parts):
    shape = jax.ShapeDtypeStruct(parts[0].shape, jnp.bfloat16)
    chunk, length = parts[5].shape
    vmem = pl.BlockSpec(memory_space=pltpu.VMEM)
    return pl.pallas_call(
        delay_kernel,
        in_specs=[pl.BlockSpec(memory_space=pltpu.SMEM)] + [vmem] * len(parts),
        out_specs=(vmem, vmem),
        out_shape=(shape, shape),
        scratch_shapes=[pltpu.VMEM((2 * chunk, length), jnp.float32)] * 2,
        compiler_params=pltpu.CompilerParams(vmem_limit_bytes=VMEM_LIMIT),
        cost_estimate=cost(
            flops=24 * chunk * length * length, bytes_accessed=8 * length * length, transcendentals=0
        ),
        name="delay",
    )(place, *parts)


def field_rows(place, half, other, slots, out, at):
    chunk, local = half.shape[3], half.shape[4] // 4
    base = 4 * chunk
    for blk in range(2):
        for n in range(4):
            hi, lo = (n >> 1) ^ place[1], (n & 1) ^ place[2]
            planes = [
                jnp.where(
                    lo == 0,
                    half[hi, blk, p].astype(jnp.float32),
                    other[hi, blk, p].astype(jnp.float32),
                )
                for p in range(2)
            ]
            first = at + blk * 2 * base + n * chunk
            for i, s in enumerate(slots):
                real = planes[0][:, s * local : (s + 1) * local]
                imag = planes[1][:, s * local : (s + 1) * local]
                lanes = slice(i * 2 * local, (i + 1) * 2 * local)
                upper = jnp.concatenate([real, imag], axis=1)
                lower = jnp.concatenate([imag, -real], axis=1)
                out[first : first + chunk, lanes] = upper.astype(jnp.bfloat16)
                out[first + base : first + base + chunk, lanes] = lower.astype(jnp.bfloat16)


def store_tiles(sums, slot, out):
    lanes = slice(slot * LANES, (slot + 1) * LANES)
    for t in range(out.shape[0]):
        out[t] = sums[t * LANES : (t + 1) * LANES, lanes].T.astype(out.dtype)


def adjoint_kernel(slots, ends_only, place, half, other, own_k, far_k, *rest):
    outs, field = rest[:-1], rest[-1]
    step = pl.program_id(0)

    @pl.when((place[0] == 0) | (not ends_only))
    def _():
        @pl.when(step == 0)
        def _():
            field_rows(place, half, other, slots, field, 0)

        cells = jnp.concatenate([own_k[0], own_k[1], far_k[0], far_k[1]], axis=1)
        sums = dot(cells, field[...])
        for i in range(len(slots)):

            @pl.when(step == 0)
            def _():
                store_tiles(sums, i, outs[2 * i])

            @pl.when(step > 0)
            def _():
                store_tiles(sums, i, outs[2 * i + 1])


def adjoint(place, half, other, own_k, far_k, slots, dtype, ends_only=False):
    base = own_k.shape[2]
    count = own_k.shape[1] // LANES
    tiles = count // 3
    rows = half.shape[4] // 2
    k_spec = pl.BlockSpec((2, tiles * LANES, base), lambda i: (0, i, 0))
    f_spec = pl.BlockSpec(half.shape, lambda i: (0,) * 5)
    block = (tiles, rows, LANES)
    outs = pl.pallas_call(
        functools.partial(adjoint_kernel, slots, ends_only),
        grid=(3,),
        in_specs=[pl.BlockSpec(memory_space=pltpu.SMEM), f_spec, f_spec, k_spec, k_spec],
        out_specs=[
            pl.BlockSpec(block, lambda i: (0, 0, 0)),
            pl.BlockSpec(block, lambda i: (jnp.maximum(i - 1, 0), 0, 0)),
        ]
        * len(slots),
        out_shape=[
            jax.ShapeDtypeStruct((n * tiles, rows, LANES), dtype) for _ in slots for n in (1, 2)
        ],
        scratch_shapes=[pltpu.VMEM((4 * base, rows * len(slots)), jnp.bfloat16)],
        compiler_params=pltpu.CompilerParams(vmem_limit_bytes=VMEM_LIMIT),
        cost_estimate=cost(
            flops=8 * rows * len(slots) * count * LANES * base,
            bytes_accessed=(4 + 2 * len(slots)) * 2**20,
            transcendentals=0,
            times=20,
        ),
        name="adjoint",
    )(place, half, other, own_k, far_k)
    return [outs[2 * i : 2 * i + 2] for i in range(len(slots))]


def first_kernel(slot, place, half, other, own_k, far_k, out, field):
    @pl.when(place[0] == 0)
    def _():
        @pl.when(pl.program_id(0) == 0)
        def _():
            field_rows(place, half, other, (slot,), field, 0)

        cells = jnp.concatenate([own_k[0], own_k[1], far_k[0], far_k[1]], axis=1)
        store_tiles(dot(cells, field[...]), 0, out)


def first_adjoint(place, half, other, own_k, far_k, slot, begin, steps):
    base = own_k.shape[2]
    tiles = own_k.shape[1] // LANES // 3
    rows = half.shape[4] // 2
    k_spec = pl.BlockSpec((2, tiles * LANES, base), lambda i: (0, i + begin, 0))
    f_spec = pl.BlockSpec(half.shape, lambda i: (0,) * 5)
    return pl.pallas_call(
        functools.partial(first_kernel, slot),
        grid=(steps,),
        in_specs=[pl.BlockSpec(memory_space=pltpu.SMEM), f_spec, f_spec, k_spec, k_spec],
        out_specs=pl.BlockSpec((tiles, rows, LANES), lambda i: (i, 0, 0)),
        out_shape=jax.ShapeDtypeStruct((steps * tiles, rows, LANES), jnp.bfloat16),
        scratch_shapes=[pltpu.VMEM((4 * base, rows), jnp.bfloat16)],
        compiler_params=pltpu.CompilerParams(vmem_limit_bytes=VMEM_LIMIT),
        cost_estimate=cost(
            flops=8 * rows * steps * tiles * LANES * base,
            bytes_accessed=steps * 2**21,
            transcendentals=0,
            times=20,
        ),
        name="first_adjoint",
    )(place, half, other, own_k, far_k)


def near_kernel(
    place, half, other, near_half, near_other, own_a, far_a, near_k, near_far_k, send, part1, part0,
    field
):
    @pl.when(place[0] == 1)
    def _():
        field_rows(place, half, other, (3, 2, 1, 0), field, 0)
        rows = field.shape[0] // 2
        field_rows(place, near_half, near_other, (3, 2, 0, 1), field, rows)
        tiles = near_k.shape[0] // 2
        cells = jnp.concatenate(
            [own_a[0], own_a[1], far_a[0], far_a[1]]
            + [tall(part[i * tiles : (i + 1) * tiles]) for part in (near_k, near_far_k) for i in (0, 1)],
            axis=1,
        )
        sums = dot(cells, field[...])
        outs = (send.at[pl.ds(0, tiles)], send.at[pl.ds(tiles, tiles)], part1, part0)
        for i, out in enumerate(outs):
            store_tiles(sums, i, out)


def near_adjoint(place, half, other, near_half, near_other, own_a, far_a, r2, r3):
    base = own_a.shape[2]
    tiles = own_a.shape[1] // LANES
    rows = half.shape[4] // 2
    whole = lambda a: pl.BlockSpec(a.shape, lambda i: (0,) * a.ndim)
    two = pl.BlockSpec((2 * tiles, LANES, rows), lambda i: (0, 0, 0))
    one = pl.BlockSpec((tiles, LANES, rows), lambda i: (0, 0, 0))
    types = ((2, jnp.bfloat16), (1, jnp.float32), (1, jnp.float32))
    return pl.pallas_call(
        near_kernel,
        grid=(1,),
        in_specs=[pl.BlockSpec(memory_space=pltpu.SMEM)]
        + [whole(a) for a in (half, other, near_half, near_other, own_a, far_a)]
        + [two, two],
        out_specs=[two, one, one],
        out_shape=[jax.ShapeDtypeStruct((n * tiles, LANES, rows), t) for n, t in types],
        scratch_shapes=[pltpu.VMEM((8 * base, rows * 4), jnp.bfloat16)],
        compiler_params=pltpu.CompilerParams(vmem_limit_bytes=VMEM_LIMIT),
        cost_estimate=cost(
            flops=64 * rows * tiles * LANES * base,
            bytes_accessed=6 * 2**20,
            transcendentals=0,
            times=20,
        ),
        name="near_adjoint",
    )(place, half, other, near_half, near_other, own_a, far_a, r2, r3)


def final_kernel(place, part_a, peer_a, end_a, *rest):
    part_b, near_b, far_b = (rest[2 * i : 2 * i + 2] for i in range(3))
    out = rest[-1]
    step = pl.program_id(0)
    is_mid = place[0] == 1
    local = out.shape[0]

    def store(value):
        for t in range(value.shape[0]):
            lanes = slice(t * LANES, (t + 1) * LANES)
            out[:, 0, lanes] = value[t][:local]
            out[:, 1, lanes] = value[t][local:]

    @pl.when(step == 0)
    def _():
        mid = part_a[...] + peer_a[...].astype(jnp.float32)
        store(jnp.where(is_mid, mid, end_a[...].astype(jnp.float32)))

    @pl.when(step > 0)
    def _():
        def piece(parts):
            return jnp.where(step == 1, parts[0][...], parts[1][...]).astype(jnp.float32)

        store(piece(part_b) + piece(near_b) + jnp.where(is_mid, piece(far_b), 0.0))


def final(place, part_a, peer_a, end_a, part_b, near_b, far_b):
    tiles, _, rows = part_a.shape
    count = 4 * tiles
    shape = (tiles, LANES, rows)
    one = pl.BlockSpec(shape, lambda i: (0, 0, 0))
    second = pl.BlockSpec(shape, lambda i: (1, 0, 0))
    rest = pl.BlockSpec(shape, lambda i: (jnp.maximum(i - 2, 0), 0, 0))
    return pl.pallas_call(
        final_kernel,
        grid=(4,),
        in_specs=[pl.BlockSpec(memory_space=pltpu.SMEM), one, second, one] + [one, rest] * 3,
        out_specs=pl.BlockSpec((rows // 2, 2, tiles * LANES), lambda i: (0, 0, i)),
        out_shape=jax.ShapeDtypeStruct((rows // 2, 2, count * LANES), jnp.float32),
        compiler_params=pltpu.CompilerParams(vmem_limit_bytes=VMEM_LIMIT),
        cost_estimate=cost(
            flops=4 * rows * count * LANES, bytes_accessed=6 * 2**20, transcendentals=0
        ),
        name="final",
    )(place, part_a, peer_a, end_a, *part_b, *near_b, *far_b)


def table_parts(length):
    half = length // 2
    steps = np.arange(half)
    turn = steps * (2.0 * math.pi / length)
    parts = [np.stack([np.cos(turn), np.sin(turn)]).astype(np.float32)]
    angle = (steps[:, None] * steps[None, :] % half) * (2.0 * math.pi / half)
    for table in (np.cos(angle), np.sin(angle)):
        high = table.astype(ml_dtypes.bfloat16)
        parts += [high, (table - high.astype(np.float64)).astype(ml_dtypes.bfloat16)]
    return [jnp.asarray(part) for part in parts]


def line_body(sky, kernel, data, block_tiles, length_bin, wedge_keep):
    length = data.shape[3]
    local, cells = sky.shape[1], sky.shape[3]
    base = kernel.shape[4]
    hi, lo = lax.axis_index("th"), lax.axis_index("tl")
    zpos, ypos = lax.axis_index("outer"), lax.axis_index("inner")
    tile_pos = hi * 2 + lo
    chunk = base // 4
    is_mid = (zpos == 1) | (zpos == 2)
    order = jnp.array([[0, 1, 2, 3], [1, 0, 2, 3], [2, 3, 1, 0], [3, 2, 1, 0]], jnp.int32)[zpos]
    place = jnp.concatenate([jnp.stack([is_mid.astype(jnp.int32), hi, lo, ypos]), order])

    tiles = cells // LANES // 4
    cut = tiles * LANES
    own_sky = sky[0].reshape(local, 2, cells // LANES, LANES).transpose(2, 1, 0, 3)
    own_sky = own_sky.reshape(cells // LANES, 2 * local, LANES)
    sky_a, sky_b = own_sky[:tiles], own_sky[tiles:]
    def ends(*values):
        return [lax.ppermute(value, "outer", ENDS) for value in values]

    def mids(*values):
        return [lax.ppermute(value, ("tl", "outer"), MIDS) for value in values]

    def as_tiles(part):
        return part.reshape(2 * tiles, LANES, base)

    (r1,) = ends(sky_b)
    (m1,) = mids(sky_b)
    column = jnp.arange(block_tiles.shape[1], dtype=jnp.int32) == tile_pos
    weight = jnp.sum(jnp.where(column, block_tiles[0], 0)).astype(jnp.bfloat16)
    own_a = lax.optimization_barrier(kernel[0, 0, :, :cut] * weight)
    own_b = kernel[0, 0, :, cut:] * weight
    end2 = jnp.concatenate([as_tiles(own_a), sky_a])
    own_a, end2 = lax.optimization_barrier((own_a, end2))
    far_a = lax.ppermute(own_a, "inner", SWAP)
    pay2 = jnp.where(is_mid, m1, end2)
    end3 = jnp.concatenate([as_tiles(far_a), sky_a])
    own_b, far_a, m1, end3 = lax.optimization_barrier((own_b, far_a, m1, end3))
    (r2,) = ends(pay2)
    (m2,) = mids(r1)
    far_b = lax.ppermute(own_b, "inner", SWAP)
    (r3,) = ends(jnp.where(is_mid, m2, end3))
    (m3,) = mids(jnp.concatenate([sky_a, r2[2 * tiles :]]))

    parts = table_parts(length)
    def by_parity(value):
        pairs = value.reshape(value.shape[:-1] + (length // 2, 2))
        return jnp.swapaxes(pairs, -1, -2).reshape(value.shape)

    own_data = by_parity(lax.dynamic_slice_in_dim(data[0], tile_pos * chunk, chunk, 1))
    own_bins = lax.dynamic_slice_in_dim(length_bin[0], tile_pos * chunk, chunk, 0)
    keep = by_parity(wedge_keep.astype(jnp.float32))[own_bins]

    done = early(place, own_b, sky_b, r1, m1, r2, (own_data, keep))
    keep_vis, send_vis, near_keep, near_send = late(
        place, done, own_b, far_b, sky_b, r1, m1, m2, own_a, far_a, sky_a, r2, r3, m3, chunk
    )
    (near,) = ends(near_sum(near_keep, lax.ppermute(near_send, "tl", SWAP)))
    got = lax.ppermute(send_vis, "tl", SWAP)
    mine, to_x, to_y, to_d = own_sum(place, keep_vis, got, near)
    from_x = lax.ppermute(to_x, "th", SWAP)
    from_y = lax.ppermute(to_y, "inner", SWAP)
    from_d = lax.ppermute(to_d, ("th", "inner"), DIAG)
    own_back, far_back = delay(place, mine, from_x, from_y, from_d, own_data, keep, *parts)
    back_x = lax.ppermute(own_back, "th", SWAP)
    back_y = lax.ppermute(far_back, "inner", SWAP)
    back_d = lax.ppermute(far_back, ("th", "inner"), DIAG)
    half = jnp.stack([jnp.stack([own_back, back_y]), jnp.stack([back_x, back_d])])
    other = lax.ppermute(half, "tl", SWAP)
    (near_half,) = ends(half)

    low = jnp.bfloat16

    def plus(part, got):
        return (part + got.astype(jnp.float32)).astype(low)

    send3 = [first_adjoint(place, half, other, own_b, far_b, 3, *part) for part in PARTS]
    g1 = ends(*send3)
    near_half, _ = lax.optimization_barrier((near_half, send3[1]))
    near_other = lax.ppermute(near_half, "tl", SWAP)
    send_a, part1_a, part0_a = near_adjoint(
        place, half, other, near_half, near_other, own_a, far_a, r2, r3
    )
    (peer_a,) = mids(send_a)
    half, send_a = lax.optimization_barrier((half, send_a))
    part3, part2, part1, part0 = adjoint(
        place, half, other, own_b, far_b, (3, 2, 1, 0), jnp.float32
    )
    far3 = mids(*(plus(part, got) for part, got in zip(part3, g1)))
    ready_a = jnp.where(is_mid, plus(part1_a, peer_a[:tiles]), part2[0].astype(low))
    g2 = ends(ready_a, part2[1].astype(low))
    g2, far3 = lax.optimization_barrier((g2, far3))
    far2 = mids(*(plus(part, got) for part, got in zip(part2, g2)))
    g3 = ends(
        *(plus(part, jnp.where(is_mid, got, jnp.zeros_like(got))) for part, got in zip(part1, far3))
    )
    return final(place, part0_a, peer_a, g2[0], part0, g3, far2)[None]


def body(sky, kernel, *rest):
    local, cells = sky.shape[1], sky.shape[3]
    line = lax.axis_size("outer") == 4 and 2 * local == LANES and kernel.shape[4] == LANES
    chosen = line_body if line and cells % (4 * LANES) == 0 else any_body
    return chosen(sky, kernel, *rest)


def solution(mesh):
    tiles, freqs = mesh.shape["tile"], mesh.shape["freq"]
    fine = Mesh(mesh.devices.reshape(tiles // 2, 2, freqs // 2, 2), ("th", "tl", "outer", "inner"))
    tile, freq = ("th", "tl"), ("outer", "inner")
    return jax.shard_map(
        body,
        mesh=fine,
        in_specs=(
            P(tile, freq, None, None),
            P(tile, freq, None, None, None),
            P(freq, None, None, None),
            P(freq, None),
            P(freq, None),
            P(),
        ),
        out_specs=P(tile, freq, None, None),
        check_vma=False,
    )
```

```python
import functools
import math

import jax
import jax.numpy as jnp
import ml_dtypes
import numpy as np
from jax import lax
from jax.experimental import pallas as pl
from jax.experimental.pallas import tpu as pltpu
from jax.sharding import Mesh, PartitionSpec as P

SWAP = [(0, 1), (1, 0)]
ENDS = [(0, 1), (1, 0), (2, 3), (3, 2)]
MIDS = [(1, 2), (2, 1), (5, 6), (6, 5), (0, 4), (4, 0), (3, 7), (7, 3)]
DIAG = [(0, 3), (1, 2), (2, 1), (3, 0)]
LANES = 128
PARTS = ((0, 1), (1, 2))
VMEM_LIMIT = 24 * 2**20
NT = (((1,), (1,)), ((), ()))


def cost(flops, bytes_accessed, transcendentals, times=1):
    return pl.CostEstimate(
        flops=times * flops, bytes_accessed=times * bytes_accessed, transcendentals=transcendentals
    )


def xor_chunks(rows, hi, lo):
    planes, count, cells = rows.shape
    rows = rows.reshape(planes, 2, 2, count // 4, cells)
    rows = jnp.where(hi == 1, rows[:, ::-1], rows)
    rows = jnp.where(lo == 1, rows[:, :, ::-1], rows)
    return rows.reshape(planes * count, cells)


def project(kernel_rows, sky_rows):
    out = lax.dot_general(
        kernel_rows, sky_rows, (((1,), (1,)), ((), ())), preferred_element_type=jnp.float32
    )
    base, chans = out.shape[0] // 2, out.shape[1] // 2
    real = out[:base, :chans] - out[base:, chans:]
    imag = out[:base, chans:] + out[base:, :chans]
    return jnp.stack([real, imag])


def adjoint_any(field, kernel_rows):
    total = 0.0
    for blk in range(2):
        real, imag = field[blk][0], field[blk][1]
        lhs = jnp.concatenate(
            [jnp.concatenate([real, imag], 1), jnp.concatenate([imag, -real], 1)], 0
        )
        total = total + lax.dot_general(
            lhs, kernel_rows[blk], (((0,), (0,)), ((), ())), preferred_element_type=jnp.float32
        )
    return total


def tables(channels, length):
    product = channels[:, None] * jnp.arange(length, dtype=jnp.int32)[None, :] % length
    angle = product.astype(jnp.float32) * (2.0 * math.pi / length)
    return jnp.cos(angle), jnp.sin(angle)


def mm(a, b):
    return jnp.einsum("bc,ck->bk", a, b, precision=lax.Precision.HIGHEST)


def mmt(a, b):
    return jnp.einsum("bk,ck->bc", a, b, precision=lax.Precision.HIGHEST)


def any_body(sky, kernel, data, block_tiles, length_bin, wedge_keep):
    length = data.shape[3]
    local, cells = sky.shape[1], sky.shape[3]
    base = kernel.shape[4]
    hi, lo = lax.axis_index("th"), lax.axis_index("tl")
    zpos, ypos = lax.axis_index("outer"), lax.axis_index("inner")
    depth = lax.axis_size("outer")
    tile_pos = hi * 2 + lo
    chunk = base // 4

    column = jnp.arange(block_tiles.shape[1], dtype=jnp.int32) == tile_pos
    weight = jnp.sum(jnp.where(column, block_tiles[0], 0)).astype(jnp.bfloat16)

    own_sky = sky[0].transpose(1, 0, 2).reshape(2 * local, cells)
    own_rows = xor_chunks((kernel[0, 0] * weight).transpose(0, 2, 1), hi, lo)
    kernels = [own_rows, lax.ppermute(own_rows, "inner", SWAP)]

    every = lax.all_gather(own_sky, "outer")
    order = jnp.arange(depth, dtype=jnp.int32)
    vis = [
        jnp.concatenate([project(rows, every[s]) for s in range(depth)], axis=2)
        for rows in kernels
    ]

    def channels(half):
        place = (order[:, None] * 2 + half) * local + jnp.arange(local, dtype=jnp.int32)[None, :]
        return place.reshape(-1)

    own_cos, own_sin = tables(channels(ypos), length)
    far_cos, far_sin = tables(channels(1 - ypos), length)

    count = vis[0].shape[2]
    vis = jnp.stack(vis).reshape(2, 2, 2, 2, chunk, count)
    vis = vis[:, :, :, 0] + lax.ppermute(vis[:, :, :, 1], "tl", SWAP)
    from_x = lax.ppermute(vis[0, :, 1], "th", SWAP)
    from_y = lax.ppermute(vis[1, :, 0], "inner", SWAP)
    from_d = lax.ppermute(vis[1, :, 1], ("th", "inner"), DIAG)
    own_vis = vis[0, :, 0] + from_x
    far_vis = from_y + from_d

    norm = 1.0 / math.sqrt(length)
    own_data = lax.dynamic_slice_in_dim(data[0], tile_pos * chunk, chunk, 1).astype(jnp.float32)
    own_bins = lax.dynamic_slice_in_dim(length_bin[0], tile_pos * chunk, chunk, 0)
    keep = wedge_keep[own_bins].astype(jnp.float32)
    cos_sum = [mm(own_vis[p], own_cos) + mm(far_vis[p], far_cos) for p in range(2)]
    sin_sum = [mm(own_vis[p], own_sin) + mm(far_vis[p], far_sin) for p in range(2)]
    miss_real = keep * ((cos_sum[0] + sin_sum[1]) * norm - own_data[0])
    miss_imag = keep * ((cos_sum[1] - sin_sum[0]) * norm - own_data[1])

    def back(cosine, sine):
        real = (mmt(miss_real, cosine) - mmt(miss_imag, sine)) * norm
        imag = (mmt(miss_imag, cosine) + mmt(miss_real, sine)) * norm
        return jnp.stack([real, imag]).astype(jnp.bfloat16)

    own_back, far_back = back(own_cos, own_sin), back(far_cos, far_sin)
    back_x = lax.ppermute(own_back, "th", SWAP)
    back_y = lax.ppermute(far_back, "inner", SWAP)
    back_d = lax.ppermute(far_back, ("th", "inner"), DIAG)
    half = jnp.stack([jnp.stack([own_back, back_x], 1), jnp.stack([back_y, back_d], 1)])
    other = lax.ppermute(half, "tl", SWAP)
    field = jnp.stack([half, other], 3).reshape(2, 2, base, count)

    def update(slot):
        return adjoint_any(field[..., slot * local : (slot + 1) * local], kernels)

    every = jnp.concatenate([update(s) for s in range(depth)], 0)
    gradient = lax.psum_scatter(every, "outer", scatter_dimension=0, tiled=True)
    return gradient.reshape(2, local, cells).transpose(1, 0, 2)[None]


def wide(tiles):
    return jnp.concatenate([tiles[t] for t in range(tiles.shape[0])], axis=1)


def paired(part):
    return jnp.concatenate([part[0], part[1]], axis=1)


def tall(tiles):
    return tiles.reshape(tiles.shape[0] * tiles.shape[1], tiles.shape[2])


def dot(a, b):
    return jnp.dot(a, b, preferred_element_type=jnp.float32)


def near_sum_kernel(keep, got, out):
    out[...] = (keep[...] + got[...]).astype(out.dtype)


def near_sum(keep, got):
    vmem = pl.BlockSpec(memory_space=pltpu.VMEM)
    return pl.pallas_call(
        near_sum_kernel,
        in_specs=[vmem, vmem],
        out_specs=vmem,
        out_shape=jax.ShapeDtypeStruct(keep.shape, jnp.bfloat16),
        compiler_params=pltpu.CompilerParams(vmem_limit_bytes=VMEM_LIMIT),
        cost_estimate=cost(flops=keep.size, bytes_accessed=10 * keep.size, transcendentals=0),
        name="near_sum",
    )(keep, got)


def own_sum_kernel(place, keep, got, near, mine, to_x, to_y, to_d):
    for hi, blk, out in ((0, 0, mine), (1, 0, to_x), (0, 1, to_y), (1, 1, to_d)):
        added = jnp.where(place[0] == 1, 0.0, near[hi, blk].astype(jnp.float32))
        out[...] = keep[hi, blk] + got[hi, blk] + added


def own_sum(place, keep, got, near):
    vmem = pl.BlockSpec(memory_space=pltpu.VMEM)
    shape = keep.shape[2:]
    return pl.pallas_call(
        own_sum_kernel,
        in_specs=[pl.BlockSpec(memory_space=pltpu.SMEM)] + [vmem] * 3,
        out_specs=[vmem] * 4,
        out_shape=[jax.ShapeDtypeStruct(shape, jnp.float32)] * 4,
        compiler_params=pltpu.CompilerParams(vmem_limit_bytes=VMEM_LIMIT),
        cost_estimate=cost(flops=2 * keep.size, bytes_accessed=14 * keep.size, transcendentals=0),
        name="own_sum",
    )(place, keep, got, near)


def early_kernel(place, own_k, slot0, slot1, mid2, end2, *rest):
    total = rest[-1]

    @pl.when(pl.program_id(0) == 0)
    def _():
        total[...] = jnp.zeros_like(total)

    third = jnp.where(place[0] == 1, mid2[...], end2[...])
    rows = jnp.concatenate([wide(slot0[...]), wide(slot1[...]), wide(third)], axis=0)
    total[...] += dot(rows, paired(own_k))


def early(place, own_k, sky, r1, m1, r2, ready):
    count, rows, _ = r1.shape
    base = own_k.shape[2]
    tiles = count // 3
    k_spec = pl.BlockSpec((2, tiles * LANES, base), lambda i: (0, i, 0))
    s_spec = pl.BlockSpec((tiles, rows, LANES), lambda i: (i, 0, 0))
    shape = (3 * rows, 2 * base)
    return pl.pallas_call(
        early_kernel,
        grid=(3,),
        in_specs=[pl.BlockSpec(memory_space=pltpu.SMEM), k_spec]
        + [s_spec] * 4
        + [pl.BlockSpec(memory_space=pl.ANY)] * len(ready),
        out_specs=pl.BlockSpec(shape, lambda i: (0, 0)),
        out_shape=jax.ShapeDtypeStruct(shape, jnp.float32),
        compiler_params=pltpu.CompilerParams(vmem_limit_bytes=VMEM_LIMIT),
        cost_estimate=cost(
            flops=6 * rows * count * LANES * 2 * base, bytes_accessed=4 * 2**20, transcendentals=0
        ),
        name="early",
    )(place, own_k, sky, r1, m1, r2, *ready)


def late_kernel(
    place, done, own_k, far_k, slot0, slot1, mid2, end2, mid3, end3, own_a, far_a, sky_a, near_sky, peer_sky, peer_near_sky,
    near_k, near_far_k, keep, send, near_keep, near_send, total, near_total
):
    step = pl.program_id(0)
    is_mid = place[0] == 1
    done_rows = done.shape[0]
    rows = done_rows // 3

    @pl.when(step == 0)
    def _():
        total[0, :done_rows] = done[...]
        total[0, done_rows:] = jnp.zeros_like(total[0, done_rows:])
        total[1] = jnp.zeros_like(total[1])

    @pl.when(step < 3)
    def _():
        third = wide(jnp.where(is_mid, mid2[...], end2[...]))
        last = wide(jnp.where(is_mid, mid3[...], end3[...]))
        every = jnp.concatenate([wide(slot0[...]), wide(slot1[...]), third, last], axis=0)
        total[0, done_rows:] += dot(last, paired(own_k))
        total[1] += dot(every, paired(far_k))

    @pl.when((step == 3) & is_mid)
    def _():
        tiles = sky_a.shape[0]
        sky = jnp.concatenate(
            [wide(part[...]) for part in (sky_a, near_sky, peer_sky, peer_near_sky)], axis=0
        )
        for blk, part in enumerate((own_a, far_a)):
            total[blk] += dot(sky, paired(part))
        for blk, part in enumerate((near_k, near_far_k)):
            pair = jnp.concatenate([tall(part[:tiles]), tall(part[tiles:])], axis=1)
            near_total[blk] = dot(sky, pair)

        store_visibility(place, near_total, near_keep, near_send, (1, 0, 2, 3))

    @pl.when(step == 3)
    def _():
        store_visibility(place, total, keep, send, (0, 1, 2, 3))


def store_visibility(place, total, keep, send, slots):
    base = total.shape[2] // 2
    local = total.shape[1] // 8
    chunk = base // 4
    for blk in range(2):
        for two in range(2):
            planes = [[], []]
            for slot in (slots[2 * two], slots[2 * two + 1]):
                own = total[blk, slot * 2 * local : (slot + 1) * 2 * local, :]
                planes[0].append(own[:local, :base] - own[local:, base:])
                planes[1].append(own[local:, :base] + own[:local, base:])
            turned = [jnp.concatenate(planes[p], axis=0).T for p in range(2)]
            lanes = slice(two * 2 * local, (two + 1) * 2 * local)
            for near, even, odd in ((0, keep, send), (1, send, keep)):

                @pl.when(place[2] == near)
                def _():
                    for p in range(2):
                        for n in range(4):
                            out = even if n & 1 == 0 else odd
                            out[(n >> 1) ^ place[1], blk, p, :, lanes] = turned[p][
                                n * chunk : (n + 1) * chunk
                            ]


def late(place, done, own_k, far_k, sky_b, r1, m1, m2, own_a, far_a, sky_a, r2, r3, m3, chunk):
    count, rows, _ = m2.shape
    base = own_k.shape[2]
    tiles = count // 3
    k_spec = pl.BlockSpec((2, tiles * LANES, base), lambda i: (0, jnp.minimum(i, 2), 0))
    s_spec = pl.BlockSpec((tiles, rows, LANES), lambda i: (jnp.minimum(i, 2), 0, 0))
    a_spec = pl.BlockSpec((2, tiles * LANES, base), lambda i: (0, 0, 0))
    one = pl.BlockSpec((tiles, rows, LANES), lambda i: (0, 0, 0))
    second = pl.BlockSpec((tiles, rows, LANES), lambda i: (1, 0, 0))
    third = pl.BlockSpec((tiles, rows, LANES), lambda i: (2, 0, 0))
    two = pl.BlockSpec((2 * tiles, rows, LANES), lambda i: (0, 0, 0))
    shape = (2, 2, 2, chunk, 2 * rows)
    return pl.pallas_call(
        late_kernel,
        grid=(4,),
        in_specs=[
            pl.BlockSpec(memory_space=pltpu.SMEM),
            pl.BlockSpec(done.shape, lambda i: (0, 0)),
            k_spec, k_spec, s_spec, s_spec, s_spec, s_spec, s_spec, s_spec, a_spec, a_spec, one, third, one, second, two, two,
        ],
        out_specs=[pl.BlockSpec(shape, lambda i: (0,) * 5)] * 4,
        out_shape=[jax.ShapeDtypeStruct(shape, jnp.float32)] * 4,
        scratch_shapes=[
            pltpu.VMEM((2, 4 * rows, 2 * base), jnp.float32),
            pltpu.VMEM((2, 4 * rows, 2 * base), jnp.float32),
        ],
        compiler_params=pltpu.CompilerParams(vmem_limit_bytes=VMEM_LIMIT),
        cost_estimate=cost(
            flops=10 * rows * count * LANES * 2 * base, bytes_accessed=9 * 2**20, transcendentals=0
        ),
        name="late",
    )(
        place, done, own_k, far_k, sky_b, r1, m1, r2, m2, r3, own_a, far_a, sky_a, r2, m3, m3, r2, r3
    )


def pack_kernel(place, mid, end0, end1, out):
    is_mid = place[0] == 1
    head = end0.shape[0]

    @pl.when(is_mid)
    def _():
        out[...] = mid[...]

    @pl.when(jnp.logical_not(is_mid))
    def _():
        out[:head] = end0[...]
        out[head:] = end1[...]


def pack(place, mid, end0, end1):
    vmem = pl.BlockSpec(memory_space=pltpu.VMEM)
    return pl.pallas_call(
        pack_kernel,
        in_specs=[pl.BlockSpec(memory_space=pltpu.SMEM)] + [vmem] * 3,
        out_specs=vmem,
        out_shape=jax.ShapeDtypeStruct(mid.shape, mid.dtype),
        compiler_params=pltpu.CompilerParams(vmem_limit_bytes=VMEM_LIMIT),
        cost_estimate=cost(
            flops=0, bytes_accessed=2 * mid.size * mid.dtype.itemsize, transcendentals=0
        ),
        name="pack",
    )(place, mid, end0, end1)


def split(value):
    high = value.astype(jnp.bfloat16)
    return high, (value - high.astype(jnp.float32)).astype(jnp.bfloat16)


def times(value, high, low, dims):
    rows = value.shape[0]
    upper, lower = split(value)
    both = lax.dot_general(
        jnp.concatenate([upper, lower], axis=0), high, dims, preferred_element_type=jnp.float32
    )
    rest = lax.dot_general(upper, low, dims, preferred_element_type=jnp.float32)
    return both[:rows] + both[rows:] + rest


def delay_kernel(
    place, vis0, from_x, from_y, from_d, data, keep, turn, ch, cl, sh, sl, own_out, far_out, rows, back
):
    length = keep.shape[1]
    chunk = keep.shape[0]
    local = length // 8
    norm = 1.0 / math.sqrt(length)
    nn = (((1,), (0,)), ((), ()))
    lower = place[3] == 0
    own = vis0[...] + from_x[...]
    far = from_y[...] + from_d[...]

    def plane_of(slot):
        return pl.ds(pl.multiple_of(place[4 + slot] * 2 * local, 2 * local), 2 * local)

    for slot in range(4):
        lanes = slice(slot * local, (slot + 1) * local)
        for p in range(2):
            mine, other = own[p][:, lanes], far[p][:, lanes]
            both = jnp.where(
                lower,
                jnp.concatenate([mine, other], axis=1),
                jnp.concatenate([other, mine], axis=1),
            )
            rows[p * chunk : (p + 1) * chunk, plane_of(slot)] = both
    half = length // 2
    turn_cos, turn_sin = turn[0:1], turn[1:2]
    low_half, high_half = rows[:, :half], rows[:, half:]
    plus, minus = low_half + high_half, low_half - high_half
    odd_real = minus[:chunk] * turn_cos + minus[chunk:] * turn_sin
    odd_imag = minus[chunk:] * turn_cos - minus[:chunk] * turn_sin
    value = jnp.concatenate([plus, odd_real, odd_imag], axis=0)
    cos_sum = times(value, ch[...], cl[...], nn)
    sin_sum = times(value, sh[...], sl[...], nn)
    miss = []
    for odd in range(2):
        real, imag = (slice((2 * odd + p) * chunk, (2 * odd + p + 1) * chunk) for p in range(2))
        lanes = slice(odd * half, (odd + 1) * half)
        kept = keep[:, lanes]
        spec_real = (cos_sum[real] + sin_sum[imag]) * norm
        spec_imag = (cos_sum[imag] - sin_sum[real]) * norm
        miss.append(kept * (spec_real - data[0, :, lanes].astype(jnp.float32)))
        miss.append(kept * (spec_imag - data[1, :, lanes].astype(jnp.float32)))
    miss = jnp.concatenate(miss, axis=0)
    cos_back = times(miss, ch[...], cl[...], nn)
    sin_back = times(miss, sh[...], sl[...], nn)
    even_real, odd_real = (
        cos_back[at : at + chunk] - sin_back[at + chunk : at + 2 * chunk] for at in (0, 2 * chunk)
    )
    even_imag, odd_imag = (
        cos_back[at + chunk : at + 2 * chunk] + sin_back[at : at + chunk] for at in (0, 2 * chunk)
    )
    turned_real = odd_real * turn_cos - odd_imag * turn_sin
    turned_imag = odd_imag * turn_cos + odd_real * turn_sin
    back[:chunk, :half] = (even_real + turned_real) * norm
    back[:chunk, half:] = (even_real - turned_real) * norm
    back[chunk:, :half] = (even_imag + turned_imag) * norm
    back[chunk:, half:] = (even_imag - turned_imag) * norm
    for p in range(2):
        found = [back[p * chunk : (p + 1) * chunk, plane_of(slot)] for slot in range(4)]
        first = jnp.concatenate([f[:, :local] for f in found], axis=1)
        second = jnp.concatenate([f[:, local:] for f in found], axis=1)
        own_out[p] = jnp.where(lower, first, second).astype(jnp.bfloat16)
        far_out[p] = jnp.where(lower, second, first).astype(jnp.bfloat16)


def delay(place, *parts):
    shape = jax.ShapeDtypeStruct(parts[0].shape, jnp.bfloat16)
    chunk, length = parts[5].shape
    vmem = pl.BlockSpec(memory_space=pltpu.VMEM)
    return pl.pallas_call(
        delay_kernel,
        in_specs=[pl.BlockSpec(memory_space=pltpu.SMEM)] + [vmem] * len(parts),
        out_specs=(vmem, vmem),
        out_shape=(shape, shape),
        scratch_shapes=[pltpu.VMEM((2 * chunk, length), jnp.float32)] * 2,
        compiler_params=pltpu.CompilerParams(vmem_limit_bytes=VMEM_LIMIT),
        cost_estimate=cost(
            flops=24 * chunk * length * length, bytes_accessed=8 * length * length, transcendentals=0
        ),
        name="delay",
    )(place, *parts)


def field_rows(place, half, other, slots, out, at):
    chunk, local = half.shape[3], half.shape[4] // 4
    base = 4 * chunk
    for blk in range(2):
        for n in range(4):
            hi, lo = (n >> 1) ^ place[1], (n & 1) ^ place[2]
            planes = [
                jnp.where(
                    lo == 0,
                    half[hi, blk, p].astype(jnp.float32),
                    other[hi, blk, p].astype(jnp.float32),
                )
                for p in range(2)
            ]
            first = at + blk * 2 * base + n * chunk
            for i, s in enumerate(slots):
                real = planes[0][:, s * local : (s + 1) * local]
                imag = planes[1][:, s * local : (s + 1) * local]
                lanes = slice(i * 2 * local, (i + 1) * 2 * local)
                upper = jnp.concatenate([real, imag], axis=1)
                lower = jnp.concatenate([imag, -real], axis=1)
                out[first : first + chunk, lanes] = upper.astype(jnp.bfloat16)
                out[first + base : first + base + chunk, lanes] = lower.astype(jnp.bfloat16)


def store_tiles(sums, slot, out):
    lanes = slice(slot * LANES, (slot + 1) * LANES)
    for t in range(out.shape[0]):
        out[t] = sums[t * LANES : (t + 1) * LANES, lanes].T.astype(out.dtype)


def adjoint_kernel(slots, ends_only, place, half, other, own_k, far_k, *rest):
    outs, field = rest[:-1], rest[-1]
    step = pl.program_id(0)

    @pl.when((place[0] == 0) | (not ends_only))
    def _():
        @pl.when(step == 0)
        def _():
            field_rows(place, half, other, slots, field, 0)

        cells = jnp.concatenate([own_k[0], own_k[1], far_k[0], far_k[1]], axis=1)
        sums = dot(cells, field[...])
        for i in range(len(slots)):

            @pl.when(step == 0)
            def _():
                store_tiles(sums, i, outs[2 * i])

            @pl.when(step > 0)
            def _():
                store_tiles(sums, i, outs[2 * i + 1])


def adjoint(place, half, other, own_k, far_k, slots, dtype, ends_only=False):
    base = own_k.shape[2]
    count = own_k.shape[1] // LANES
    tiles = count // 3
    rows = half.shape[4] // 2
    k_spec = pl.BlockSpec((2, tiles * LANES, base), lambda i: (0, i, 0))
    f_spec = pl.BlockSpec(half.shape, lambda i: (0,) * 5)
    block = (tiles, rows, LANES)
    outs = pl.pallas_call(
        functools.partial(adjoint_kernel, slots, ends_only),
        grid=(3,),
        in_specs=[pl.BlockSpec(memory_space=pltpu.SMEM), f_spec, f_spec, k_spec, k_spec],
        out_specs=[
            pl.BlockSpec(block, lambda i: (0, 0, 0)),
            pl.BlockSpec(block, lambda i: (jnp.maximum(i - 1, 0), 0, 0)),
        ]
        * len(slots),
        out_shape=[
            jax.ShapeDtypeStruct((n * tiles, rows, LANES), dtype) for _ in slots for n in (1, 2)
        ],
        scratch_shapes=[pltpu.VMEM((4 * base, rows * len(slots)), jnp.bfloat16)],
        compiler_params=pltpu.CompilerParams(vmem_limit_bytes=VMEM_LIMIT),
        cost_estimate=cost(
            flops=8 * rows * len(slots) * count * LANES * base,
            bytes_accessed=(4 + 2 * len(slots)) * 2**20,
            transcendentals=0,
            times=20,
        ),
        name="adjoint",
    )(place, half, other, own_k, far_k)
    return [outs[2 * i : 2 * i + 2] for i in range(len(slots))]


def first_kernel(slot, place, half, other, own_k, far_k, out, field):
    @pl.when(place[0] == 0)
    def _():
        @pl.when(pl.program_id(0) == 0)
        def _():
            field_rows(place, half, other, (slot,), field, 0)

        cells = jnp.concatenate([own_k[0], own_k[1], far_k[0], far_k[1]], axis=1)
        store_tiles(dot(cells, field[...]), 0, out)


def first_adjoint(place, half, other, own_k, far_k, slot, begin, steps):
    base = own_k.shape[2]
    tiles = own_k.shape[1] // LANES // 3
    rows = half.shape[4] // 2
    k_spec = pl.BlockSpec((2, tiles * LANES, base), lambda i: (0, i + begin, 0))
    f_spec = pl.BlockSpec(half.shape, lambda i: (0,) * 5)
    return pl.pallas_call(
        functools.partial(first_kernel, slot),
        grid=(steps,),
        in_specs=[pl.BlockSpec(memory_space=pltpu.SMEM), f_spec, f_spec, k_spec, k_spec],
        out_specs=pl.BlockSpec((tiles, rows, LANES), lambda i: (i, 0, 0)),
        out_shape=jax.ShapeDtypeStruct((steps * tiles, rows, LANES), jnp.bfloat16),
        scratch_shapes=[pltpu.VMEM((4 * base, rows), jnp.bfloat16)],
        compiler_params=pltpu.CompilerParams(vmem_limit_bytes=VMEM_LIMIT),
        cost_estimate=cost(
            flops=8 * rows * steps * tiles * LANES * base,
            bytes_accessed=steps * 2**21,
            transcendentals=0,
            times=20,
        ),
        name="first_adjoint",
    )(place, half, other, own_k, far_k)


def near_kernel(
    slots, place, half, other, near_half, near_other, own_a, far_a, near_k, near_far_k, *rest
):
    field = rest[-1]

    @pl.when(place[0] == 1)
    def _():
        field_rows(place, half, other, slots, field, 0)
        rows = field.shape[0] // 2
        swapped = [(1, 0, 2, 3)[slot] for slot in slots]
        field_rows(place, near_half, near_other, swapped, field, rows)
        tiles = near_k.shape[0] // 2
        cells = jnp.concatenate(
            [own_a[0], own_a[1], far_a[0], far_a[1]]
            + [tall(part[i * tiles : (i + 1) * tiles]) for part in (near_k, near_far_k) for i in (0, 1)],
            axis=1,
        )
        sums = dot(cells, field[...])
        outs = rest[:-1]
        if len(outs) == 1:
            outs = (outs[0].at[pl.ds(0, tiles)], outs[0].at[pl.ds(tiles, tiles)])
        for i, out in enumerate(outs):
            store_tiles(sums, i, out)


def near_adjoint(place, half, other, near_half, near_other, own_a, far_a, r2, r3, slots, dtype):
    base = own_a.shape[2]
    tiles = own_a.shape[1] // LANES
    rows = half.shape[4] // 2
    whole = lambda a: pl.BlockSpec(a.shape, lambda i: (0,) * a.ndim)
    two = pl.BlockSpec((2 * tiles, LANES, rows), lambda i: (0, 0, 0))
    one = pl.BlockSpec((tiles, LANES, rows), lambda i: (0, 0, 0))
    counts = (2,) if dtype == jnp.bfloat16 else (1, 1)
    return pl.pallas_call(
        functools.partial(near_kernel, slots),
        grid=(1,),
        in_specs=[pl.BlockSpec(memory_space=pltpu.SMEM)]
        + [whole(a) for a in (half, other, near_half, near_other, own_a, far_a)]
        + [two, two],
        out_specs=[two if n == 2 else one for n in counts],
        out_shape=[jax.ShapeDtypeStruct((n * tiles, LANES, rows), dtype) for n in counts],
        scratch_shapes=[pltpu.VMEM((8 * base, rows * 2), jnp.bfloat16)],
        compiler_params=pltpu.CompilerParams(vmem_limit_bytes=VMEM_LIMIT),
        cost_estimate=cost(
            flops=32 * rows * tiles * LANES * base,
            bytes_accessed=5 * 2**20,
            transcendentals=0,
            times=20,
        ),
        name="near_adjoint",
    )(place, half, other, near_half, near_other, own_a, far_a, r2, r3)


def store_rows(out, value):
    local = out.shape[0]
    for t in range(value.shape[0]):
        lanes = slice(t * LANES, (t + 1) * LANES)
        out[:, 0, lanes] = value[t][:local]
        out[:, 1, lanes] = value[t][local:]


def final_a_kernel(place, part_a, peer_a, end_a, out):
    mid = part_a[...] + peer_a[...].astype(jnp.float32)
    store_rows(out, jnp.where(place[0] == 1, mid, end_a[...].astype(jnp.float32)))


def final_b_kernel(place, part, near, far, before, out):
    value = part[...] + near[...].astype(jnp.float32)
    store_rows(out, value + jnp.where(place[0] == 1, far[...].astype(jnp.float32), 0.0))


def final(place, part_a, peer_a, end_a, part_b, near_b, far_b):
    tiles, rows, _ = part_a.shape
    shape = (tiles, rows, LANES)
    smem = pl.BlockSpec(memory_space=pltpu.SMEM)
    one = pl.BlockSpec(shape, lambda i: (0, 0, 0))
    second = pl.BlockSpec(shape, lambda i: (1, 0, 0))
    block = (rows // 2, 2, tiles * LANES)
    whole = jax.ShapeDtypeStruct((rows // 2, 2, 4 * tiles * LANES), jnp.float32)
    params = pltpu.CompilerParams(vmem_limit_bytes=VMEM_LIMIT)
    done = pl.pallas_call(
        final_a_kernel,
        grid=(1,),
        in_specs=[smem, one, second, one],
        out_specs=pl.BlockSpec(block, lambda i: (0, 0, 0)),
        out_shape=whole,
        compiler_params=params,
        cost_estimate=cost(flops=2 * rows * tiles * LANES, bytes_accessed=2**20, transcendentals=0),
        name="final_a",
    )(place, part_a, peer_a, end_a)
    for piece, begin, steps in ((1, 2, 2), (0, 1, 1)):
        each = pl.BlockSpec(shape, lambda i: (i, 0, 0))
        done = pl.pallas_call(
            final_b_kernel,
            grid=(steps,),
            in_specs=[smem, each, each, each, pl.BlockSpec(memory_space=pl.ANY)],
            out_specs=pl.BlockSpec(block, functools.partial(lambda start, i: (0, 0, i + start), begin)),
            out_shape=whole,
            input_output_aliases={4: 0},
            compiler_params=params,
            cost_estimate=cost(
                flops=3 * steps * rows * tiles * LANES, bytes_accessed=2**20 * steps, transcendentals=0
            ),
            name="final_b",
        )(place, part_b[piece], near_b[piece], far_b[piece], done)
    return done


def table_parts(length):
    half = length // 2
    steps = np.arange(half)
    turn = steps * (2.0 * math.pi / length)
    parts = [np.stack([np.cos(turn), np.sin(turn)]).astype(np.float32)]
    angle = (steps[:, None] * steps[None, :] % half) * (2.0 * math.pi / half)
    for table in (np.cos(angle), np.sin(angle)):
        high = table.astype(ml_dtypes.bfloat16)
        parts += [high, (table - high.astype(np.float64)).astype(ml_dtypes.bfloat16)]
    return [jnp.asarray(part) for part in parts]


def line_body(sky, kernel, data, block_tiles, length_bin, wedge_keep):
    length = data.shape[3]
    local, cells = sky.shape[1], sky.shape[3]
    base = kernel.shape[4]
    hi, lo = lax.axis_index("th"), lax.axis_index("tl")
    zpos, ypos = lax.axis_index("outer"), lax.axis_index("inner")
    tile_pos = hi * 2 + lo
    chunk = base // 4
    is_mid = (zpos == 1) | (zpos == 2)
    order = jnp.array([[0, 1, 2, 3], [1, 0, 2, 3], [2, 3, 1, 0], [3, 2, 1, 0]], jnp.int32)[zpos]
    place = jnp.concatenate([jnp.stack([is_mid.astype(jnp.int32), hi, lo, ypos]), order])

    tiles = cells // LANES // 4
    cut = tiles * LANES
    own_sky = sky[0].reshape(local, 2, cells // LANES, LANES).transpose(2, 1, 0, 3)
    own_sky = own_sky.reshape(cells // LANES, 2 * local, LANES)
    sky_a, sky_b = own_sky[:tiles], own_sky[tiles:]
    def ends(*values):
        return [lax.ppermute(value, "outer", ENDS) for value in values]

    def mids(*values):
        return [lax.ppermute(value, ("tl", "outer"), MIDS) for value in values]

    def as_tiles(part):
        return part.reshape(2 * tiles, LANES, base)

    (r1,) = ends(sky_b)
    (m1,) = mids(sky_b)
    column = jnp.arange(block_tiles.shape[1], dtype=jnp.int32) == tile_pos
    weight = jnp.sum(jnp.where(column, block_tiles[0], 0)).astype(jnp.bfloat16)
    own_a = lax.optimization_barrier(kernel[0, 0, :, :cut] * weight)
    own_b = kernel[0, 0, :, cut:] * weight
    end2 = jnp.concatenate([as_tiles(own_a), sky_a])
    own_a, end2 = lax.optimization_barrier((own_a, end2))
    far_a = lax.ppermute(own_a, "inner", SWAP)
    pay2 = jnp.where(is_mid, m1, end2)
    end3 = jnp.concatenate([as_tiles(far_a), sky_a])
    own_b, far_a, m1, end3 = lax.optimization_barrier((own_b, far_a, m1, end3))
    (r2,) = ends(pay2)
    (m2,) = mids(r1)
    far_b = lax.ppermute(own_b, "inner", SWAP)
    (r3,) = ends(jnp.where(is_mid, m2, end3))
    (m3,) = mids(jnp.concatenate([sky_a, r2[2 * tiles :]]))

    parts = table_parts(length)
    def by_parity(value):
        pairs = value.reshape(value.shape[:-1] + (length // 2, 2))
        return jnp.swapaxes(pairs, -1, -2).reshape(value.shape)

    own_data = by_parity(lax.dynamic_slice_in_dim(data[0], tile_pos * chunk, chunk, 1))
    own_bins = lax.dynamic_slice_in_dim(length_bin[0], tile_pos * chunk, chunk, 0)
    keep = by_parity(wedge_keep.astype(jnp.float32))[own_bins]

    done = early(place, own_b, sky_b, r1, m1, r2, (own_data, keep))
    keep_vis, send_vis, near_keep, near_send = late(
        place, done, own_b, far_b, sky_b, r1, m1, m2, own_a, far_a, sky_a, r2, r3, m3, chunk
    )
    (near,) = ends(near_sum(near_keep, lax.ppermute(near_send, "tl", SWAP)))
    got = lax.ppermute(send_vis, "tl", SWAP)
    mine, to_x, to_y, to_d = own_sum(place, keep_vis, got, near)
    from_x = lax.ppermute(to_x, "th", SWAP)
    from_y = lax.ppermute(to_y, "inner", SWAP)
    from_d = lax.ppermute(to_d, ("th", "inner"), DIAG)
    own_back, far_back = delay(place, mine, from_x, from_y, from_d, own_data, keep, *parts)
    back_x = lax.ppermute(own_back, "th", SWAP)
    back_y = lax.ppermute(far_back, "inner", SWAP)
    back_d = lax.ppermute(far_back, ("th", "inner"), DIAG)
    half = jnp.stack([jnp.stack([own_back, back_y]), jnp.stack([back_x, back_d])])
    other = lax.ppermute(half, "tl", SWAP)
    (near_half,) = ends(half)

    low = jnp.bfloat16

    def plus(part, got):
        return (part + got.astype(jnp.float32)).astype(low)

    send3 = [first_adjoint(place, half, other, own_b, far_b, 3, *part) for part in PARTS]
    g1 = ends(*send3)
    near_half, _ = lax.optimization_barrier((near_half, send3[1]))
    near_other = lax.ppermute(near_half, "tl", SWAP)
    near_args = (half, other, near_half, near_other, own_a, far_a, r2, r3)
    (send_a,) = near_adjoint(place, *near_args, (3, 2), low)
    (peer_a,) = mids(send_a)
    half, send_a = lax.optimization_barrier((half, send_a))
    part1_a, part0_a = near_adjoint(place, half, *near_args[1:], (1, 0), jnp.float32)
    part3, part2, part1, part0 = adjoint(
        place, half, other, own_b, far_b, (3, 2, 1, 0), jnp.float32
    )
    far3 = mids(*(plus(part, got) for part, got in zip(part3, g1)))
    ready_a = jnp.where(is_mid, plus(part1_a, peer_a[:tiles]), part2[0].astype(low))
    g2 = ends(ready_a, part2[1].astype(low))
    g2, far3 = lax.optimization_barrier((g2, far3))
    far2 = mids(*(plus(part, got) for part, got in zip(part2, g2)))
    g3 = ends(
        *(plus(part, jnp.where(is_mid, got, jnp.zeros_like(got))) for part, got in zip(part1, far3))
    )
    return final(place, part0_a, peer_a, g2[0], part0, g3, far2)[None]


def body(sky, kernel, *rest):
    local, cells = sky.shape[1], sky.shape[3]
    line = lax.axis_size("outer") == 4 and 2 * local == LANES and kernel.shape[4] == LANES
    chosen = line_body if line and cells % (4 * LANES) == 0 else any_body
    return chosen(sky, kernel, *rest)


def solution(mesh):
    tiles, freqs = mesh.shape["tile"], mesh.shape["freq"]
    fine = Mesh(mesh.devices.reshape(tiles // 2, 2, freqs // 2, 2), ("th", "tl", "outer", "inner"))
    tile, freq = ("th", "tl"), ("outer", "inner")
    return jax.shard_map(
        body,
        mesh=fine,
        in_specs=(
            P(tile, freq, None, None),
            P(tile, freq, None, None, None),
            P(freq, None, None, None),
            P(freq, None),
            P(freq, None),
            P(),
        ),
        out_specs=P(tile, freq, None, None),
        check_vma=False,
    )
```

```python
import functools
import math

import jax
import jax.numpy as jnp
import ml_dtypes
import numpy as np
from jax import lax
from jax.experimental import pallas as pl
from jax.experimental.pallas import tpu as pltpu
from jax.sharding import Mesh, PartitionSpec as P

SWAP = [(0, 1), (1, 0)]
ENDS = [(0, 1), (1, 0), (2, 3), (3, 2)]
MIDS = [(1, 2), (2, 1), (5, 6), (6, 5), (0, 4), (4, 0), (3, 7), (7, 3)]
DIAG = [(0, 3), (1, 2), (2, 1), (3, 0)]
LANES = 128
PARTS = ((0, 1), (1, 2))
VMEM_LIMIT = 24 * 2**20
NT = (((1,), (1,)), ((), ()))


def cost(flops, bytes_accessed, transcendentals, times=1):
    return pl.CostEstimate(
        flops=times * flops, bytes_accessed=times * bytes_accessed, transcendentals=transcendentals
    )


def xor_chunks(rows, hi, lo):
    planes, count, cells = rows.shape
    rows = rows.reshape(planes, 2, 2, count // 4, cells)
    rows = jnp.where(hi == 1, rows[:, ::-1], rows)
    rows = jnp.where(lo == 1, rows[:, :, ::-1], rows)
    return rows.reshape(planes * count, cells)


def project(kernel_rows, sky_rows):
    out = lax.dot_general(
        kernel_rows, sky_rows, (((1,), (1,)), ((), ())), preferred_element_type=jnp.float32
    )
    base, chans = out.shape[0] // 2, out.shape[1] // 2
    real = out[:base, :chans] - out[base:, chans:]
    imag = out[:base, chans:] + out[base:, :chans]
    return jnp.stack([real, imag])


def adjoint_any(field, kernel_rows):
    total = 0.0
    for blk in range(2):
        real, imag = field[blk][0], field[blk][1]
        lhs = jnp.concatenate(
            [jnp.concatenate([real, imag], 1), jnp.concatenate([imag, -real], 1)], 0
        )
        total = total + lax.dot_general(
            lhs, kernel_rows[blk], (((0,), (0,)), ((), ())), preferred_element_type=jnp.float32
        )
    return total


def tables(channels, length):
    product = channels[:, None] * jnp.arange(length, dtype=jnp.int32)[None, :] % length
    angle = product.astype(jnp.float32) * (2.0 * math.pi / length)
    return jnp.cos(angle), jnp.sin(angle)


def mm(a, b):
    return jnp.einsum("bc,ck->bk", a, b, precision=lax.Precision.HIGHEST)


def mmt(a, b):
    return jnp.einsum("bk,ck->bc", a, b, precision=lax.Precision.HIGHEST)


def any_body(sky, kernel, data, block_tiles, length_bin, wedge_keep):
    length = data.shape[3]
    local, cells = sky.shape[1], sky.shape[3]
    base = kernel.shape[4]
    hi, lo = lax.axis_index("th"), lax.axis_index("tl")
    zpos, ypos = lax.axis_index("outer"), lax.axis_index("inner")
    depth = lax.axis_size("outer")
    tile_pos = hi * 2 + lo
    chunk = base // 4

    column = jnp.arange(block_tiles.shape[1], dtype=jnp.int32) == tile_pos
    weight = jnp.sum(jnp.where(column, block_tiles[0], 0)).astype(jnp.bfloat16)

    own_sky = sky[0].transpose(1, 0, 2).reshape(2 * local, cells)
    own_rows = xor_chunks((kernel[0, 0] * weight).transpose(0, 2, 1), hi, lo)
    kernels = [own_rows, lax.ppermute(own_rows, "inner", SWAP)]

    every = lax.all_gather(own_sky, "outer")
    order = jnp.arange(depth, dtype=jnp.int32)
    vis = [
        jnp.concatenate([project(rows, every[s]) for s in range(depth)], axis=2)
        for rows in kernels
    ]

    def channels(half):
        place = (order[:, None] * 2 + half) * local + jnp.arange(local, dtype=jnp.int32)[None, :]
        return place.reshape(-1)

    own_cos, own_sin = tables(channels(ypos), length)
    far_cos, far_sin = tables(channels(1 - ypos), length)

    count = vis[0].shape[2]
    vis = jnp.stack(vis).reshape(2, 2, 2, 2, chunk, count)
    vis = vis[:, :, :, 0] + lax.ppermute(vis[:, :, :, 1], "tl", SWAP)
    from_x = lax.ppermute(vis[0, :, 1], "th", SWAP)
    from_y = lax.ppermute(vis[1, :, 0], "inner", SWAP)
    from_d = lax.ppermute(vis[1, :, 1], ("th", "inner"), DIAG)
    own_vis = vis[0, :, 0] + from_x
    far_vis = from_y + from_d

    norm = 1.0 / math.sqrt(length)
    own_data = lax.dynamic_slice_in_dim(data[0], tile_pos * chunk, chunk, 1).astype(jnp.float32)
    own_bins = lax.dynamic_slice_in_dim(length_bin[0], tile_pos * chunk, chunk, 0)
    keep = wedge_keep[own_bins].astype(jnp.float32)
    cos_sum = [mm(own_vis[p], own_cos) + mm(far_vis[p], far_cos) for p in range(2)]
    sin_sum = [mm(own_vis[p], own_sin) + mm(far_vis[p], far_sin) for p in range(2)]
    miss_real = keep * ((cos_sum[0] + sin_sum[1]) * norm - own_data[0])
    miss_imag = keep * ((cos_sum[1] - sin_sum[0]) * norm - own_data[1])

    def back(cosine, sine):
        real = (mmt(miss_real, cosine) - mmt(miss_imag, sine)) * norm
        imag = (mmt(miss_imag, cosine) + mmt(miss_real, sine)) * norm
        return jnp.stack([real, imag]).astype(jnp.bfloat16)

    own_back, far_back = back(own_cos, own_sin), back(far_cos, far_sin)
    back_x = lax.ppermute(own_back, "th", SWAP)
    back_y = lax.ppermute(far_back, "inner", SWAP)
    back_d = lax.ppermute(far_back, ("th", "inner"), DIAG)
    half = jnp.stack([jnp.stack([own_back, back_x], 1), jnp.stack([back_y, back_d], 1)])
    other = lax.ppermute(half, "tl", SWAP)
    field = jnp.stack([half, other], 3).reshape(2, 2, base, count)

    def update(slot):
        return adjoint_any(field[..., slot * local : (slot + 1) * local], kernels)

    every = jnp.concatenate([update(s) for s in range(depth)], 0)
    gradient = lax.psum_scatter(every, "outer", scatter_dimension=0, tiled=True)
    return gradient.reshape(2, local, cells).transpose(1, 0, 2)[None]


def wide(tiles):
    return jnp.concatenate([tiles[t] for t in range(tiles.shape[0])], axis=1)


def paired(part):
    return jnp.concatenate([part[0], part[1]], axis=1)


def tall(tiles):
    return tiles.reshape(tiles.shape[0] * tiles.shape[1], tiles.shape[2])


def dot(a, b):
    return jnp.dot(a, b, preferred_element_type=jnp.float32)


def near_sum_kernel(keep, got, out):
    out[...] = (keep[...] + got[...]).astype(out.dtype)


def near_sum(keep, got):
    vmem = pl.BlockSpec(memory_space=pltpu.VMEM)
    return pl.pallas_call(
        near_sum_kernel,
        in_specs=[vmem, vmem],
        out_specs=vmem,
        out_shape=jax.ShapeDtypeStruct(keep.shape, jnp.bfloat16),
        compiler_params=pltpu.CompilerParams(vmem_limit_bytes=VMEM_LIMIT),
        cost_estimate=cost(flops=keep.size, bytes_accessed=10 * keep.size, transcendentals=0),
        name="near_sum",
    )(keep, got)


def own_sum_kernel(place, keep, got, near, mine, to_x, to_y, to_d):
    for hi, blk, out in ((0, 0, mine), (1, 0, to_x), (0, 1, to_y), (1, 1, to_d)):
        added = jnp.where(place[0] == 1, 0.0, near[hi, blk].astype(jnp.float32))
        out[...] = keep[hi, blk] + got[hi, blk] + added


def own_sum(place, keep, got, near):
    vmem = pl.BlockSpec(memory_space=pltpu.VMEM)
    shape = keep.shape[2:]
    return pl.pallas_call(
        own_sum_kernel,
        in_specs=[pl.BlockSpec(memory_space=pltpu.SMEM)] + [vmem] * 3,
        out_specs=[vmem] * 4,
        out_shape=[jax.ShapeDtypeStruct(shape, jnp.float32)] * 4,
        compiler_params=pltpu.CompilerParams(vmem_limit_bytes=VMEM_LIMIT),
        cost_estimate=cost(flops=2 * keep.size, bytes_accessed=14 * keep.size, transcendentals=0),
        name="own_sum",
    )(place, keep, got, near)


def early_kernel(place, own_k, slot0, slot1, mid2, end2, *rest):
    total = rest[-1]

    @pl.when(pl.program_id(0) == 0)
    def _():
        total[...] = jnp.zeros_like(total)

    third = jnp.where(place[0] == 1, mid2[...], end2[...])
    rows = jnp.concatenate([wide(slot0[...]), wide(slot1[...]), wide(third)], axis=0)
    total[...] += dot(rows, paired(own_k))


def early(place, own_k, sky, r1, m1, r2, ready):
    count, rows, _ = r1.shape
    base = own_k.shape[2]
    tiles = count // 3
    k_spec = pl.BlockSpec((2, tiles * LANES, base), lambda i: (0, i, 0))
    s_spec = pl.BlockSpec((tiles, rows, LANES), lambda i: (i, 0, 0))
    shape = (3 * rows, 2 * base)
    return pl.pallas_call(
        early_kernel,
        grid=(3,),
        in_specs=[pl.BlockSpec(memory_space=pltpu.SMEM), k_spec]
        + [s_spec] * 4
        + [pl.BlockSpec(memory_space=pl.ANY)] * len(ready),
        out_specs=pl.BlockSpec(shape, lambda i: (0, 0)),
        out_shape=jax.ShapeDtypeStruct(shape, jnp.float32),
        compiler_params=pltpu.CompilerParams(vmem_limit_bytes=VMEM_LIMIT),
        cost_estimate=cost(
            flops=6 * rows * count * LANES * 2 * base, bytes_accessed=4 * 2**20, transcendentals=0
        ),
        name="early",
    )(place, own_k, sky, r1, m1, r2, *ready)


def late_kernel(
    place, done, own_k, far_k, slot0, slot1, mid2, end2, mid3, end3, own_a, far_a, sky_a, near_sky, peer_sky, peer_near_sky,
    near_k, near_far_k, keep, send, near_keep, near_send, total, near_total
):
    step = pl.program_id(0)
    is_mid = place[0] == 1
    done_rows = done.shape[0]
    rows = done_rows // 3

    @pl.when(step == 0)
    def _():
        total[0, :done_rows] = done[...]
        total[0, done_rows:] = jnp.zeros_like(total[0, done_rows:])
        total[1] = jnp.zeros_like(total[1])

    @pl.when(step < 3)
    def _():
        third = wide(jnp.where(is_mid, mid2[...], end2[...]))
        last = wide(jnp.where(is_mid, mid3[...], end3[...]))
        every = jnp.concatenate([wide(slot0[...]), wide(slot1[...]), third, last], axis=0)
        total[0, done_rows:] += dot(last, paired(own_k))
        total[1] += dot(every, paired(far_k))

    @pl.when((step == 3) & is_mid)
    def _():
        tiles = sky_a.shape[0]
        sky = jnp.concatenate(
            [wide(part[...]) for part in (sky_a, near_sky, peer_sky, peer_near_sky)], axis=0
        )
        for blk, part in enumerate((own_a, far_a)):
            total[blk] += dot(sky, paired(part))
        for blk, part in enumerate((near_k, near_far_k)):
            pair = jnp.concatenate([tall(part[:tiles]), tall(part[tiles:])], axis=1)
            near_total[blk] = dot(sky, pair)

        store_visibility(place, near_total, near_keep, near_send, (1, 0, 2, 3))

    @pl.when(step == 3)
    def _():
        store_visibility(place, total, keep, send, (0, 1, 2, 3))


def store_visibility(place, total, keep, send, slots):
    base = total.shape[2] // 2
    local = total.shape[1] // 8
    chunk = base // 4
    for blk in range(2):
        for two in range(2):
            planes = [[], []]
            for slot in (slots[2 * two], slots[2 * two + 1]):
                own = total[blk, slot * 2 * local : (slot + 1) * 2 * local, :]
                planes[0].append(own[:local, :base] - own[local:, base:])
                planes[1].append(own[local:, :base] + own[:local, base:])
            turned = [jnp.concatenate(planes[p], axis=0).T for p in range(2)]
            lanes = slice(two * 2 * local, (two + 1) * 2 * local)
            for near, even, odd in ((0, keep, send), (1, send, keep)):

                @pl.when(place[2] == near)
                def _():
                    for p in range(2):
                        for n in range(4):
                            out = even if n & 1 == 0 else odd
                            out[(n >> 1) ^ place[1], blk, p, :, lanes] = turned[p][
                                n * chunk : (n + 1) * chunk
                            ]


def late(place, done, own_k, far_k, sky_b, r1, m1, m2, own_a, far_a, sky_a, r2, r3, m3, chunk):
    count, rows, _ = m2.shape
    base = own_k.shape[2]
    tiles = count // 3
    k_spec = pl.BlockSpec((2, tiles * LANES, base), lambda i: (0, jnp.minimum(i, 2), 0))
    s_spec = pl.BlockSpec((tiles, rows, LANES), lambda i: (jnp.minimum(i, 2), 0, 0))
    a_spec = pl.BlockSpec((2, tiles * LANES, base), lambda i: (0, 0, 0))
    one = pl.BlockSpec((tiles, rows, LANES), lambda i: (0, 0, 0))
    second = pl.BlockSpec((tiles, rows, LANES), lambda i: (1, 0, 0))
    third = pl.BlockSpec((tiles, rows, LANES), lambda i: (2, 0, 0))
    two = pl.BlockSpec((2 * tiles, rows, LANES), lambda i: (0, 0, 0))
    shape = (2, 2, 2, chunk, 2 * rows)
    return pl.pallas_call(
        late_kernel,
        grid=(4,),
        in_specs=[
            pl.BlockSpec(memory_space=pltpu.SMEM),
            pl.BlockSpec(done.shape, lambda i: (0, 0)),
            k_spec, k_spec, s_spec, s_spec, s_spec, s_spec, s_spec, s_spec, a_spec, a_spec, one, third, one, second, two, two,
        ],
        out_specs=[pl.BlockSpec(shape, lambda i: (0,) * 5)] * 4,
        out_shape=[jax.ShapeDtypeStruct(shape, jnp.float32)] * 4,
        scratch_shapes=[
            pltpu.VMEM((2, 4 * rows, 2 * base), jnp.float32),
            pltpu.VMEM((2, 4 * rows, 2 * base), jnp.float32),
        ],
        compiler_params=pltpu.CompilerParams(vmem_limit_bytes=VMEM_LIMIT),
        cost_estimate=cost(
            flops=10 * rows * count * LANES * 2 * base, bytes_accessed=9 * 2**20, transcendentals=0
        ),
        name="late",
    )(
        place, done, own_k, far_k, sky_b, r1, m1, r2, m2, r3, own_a, far_a, sky_a, r2, m3, m3, r2, r3
    )


def pack_kernel(place, mid, end0, end1, out):
    is_mid = place[0] == 1
    head = end0.shape[0]

    @pl.when(is_mid)
    def _():
        out[...] = mid[...]

    @pl.when(jnp.logical_not(is_mid))
    def _():
        out[:head] = end0[...]
        out[head:] = end1[...]


def pack(place, mid, end0, end1):
    vmem = pl.BlockSpec(memory_space=pltpu.VMEM)
    return pl.pallas_call(
        pack_kernel,
        in_specs=[pl.BlockSpec(memory_space=pltpu.SMEM)] + [vmem] * 3,
        out_specs=vmem,
        out_shape=jax.ShapeDtypeStruct(mid.shape, mid.dtype),
        compiler_params=pltpu.CompilerParams(vmem_limit_bytes=VMEM_LIMIT),
        cost_estimate=cost(
            flops=0, bytes_accessed=2 * mid.size * mid.dtype.itemsize, transcendentals=0
        ),
        name="pack",
    )(place, mid, end0, end1)


def split(value):
    high = value.astype(jnp.bfloat16)
    return high, (value - high.astype(jnp.float32)).astype(jnp.bfloat16)


def times(value, high, low, dims):
    rows = value.shape[0]
    upper, lower = split(value)
    both = lax.dot_general(
        jnp.concatenate([upper, lower], axis=0), high, dims, preferred_element_type=jnp.float32
    )
    rest = lax.dot_general(upper, low, dims, preferred_element_type=jnp.float32)
    return both[:rows] + both[rows:] + rest


def delay_kernel(
    place, vis0, from_x, from_y, from_d, data, keep, turn, ch, cl, sh, sl, own_out, far_out, rows, back
):
    length = keep.shape[1]
    chunk = keep.shape[0]
    local = length // 8
    norm = 1.0 / math.sqrt(length)
    nn = (((1,), (0,)), ((), ()))
    lower = place[3] == 0
    own = vis0[...] + from_x[...]
    far = from_y[...] + from_d[...]

    def plane_of(slot):
        return pl.ds(pl.multiple_of(place[4 + slot] * 2 * local, 2 * local), 2 * local)

    for slot in range(4):
        lanes = slice(slot * local, (slot + 1) * local)
        for p in range(2):
            mine, other = own[p][:, lanes], far[p][:, lanes]
            both = jnp.where(
                lower,
                jnp.concatenate([mine, other], axis=1),
                jnp.concatenate([other, mine], axis=1),
            )
            rows[p * chunk : (p + 1) * chunk, plane_of(slot)] = both
    half = length // 2
    turn_cos, turn_sin = turn[0:1], turn[1:2]
    low_half, high_half = rows[:, :half], rows[:, half:]
    plus, minus = low_half + high_half, low_half - high_half
    odd_real = minus[:chunk] * turn_cos + minus[chunk:] * turn_sin
    odd_imag = minus[chunk:] * turn_cos - minus[:chunk] * turn_sin
    value = jnp.concatenate([plus, odd_real, odd_imag], axis=0)
    cos_sum = times(value, ch[...], cl[...], nn)
    sin_sum = times(value, sh[...], sl[...], nn)
    miss = []
    for odd in range(2):
        real, imag = (slice((2 * odd + p) * chunk, (2 * odd + p + 1) * chunk) for p in range(2))
        lanes = slice(odd * half, (odd + 1) * half)
        kept = keep[:, lanes]
        spec_real = (cos_sum[real] + sin_sum[imag]) * norm
        spec_imag = (cos_sum[imag] - sin_sum[real]) * norm
        miss.append(kept * (spec_real - data[0, :, lanes].astype(jnp.float32)))
        miss.append(kept * (spec_imag - data[1, :, lanes].astype(jnp.float32)))
    miss = jnp.concatenate(miss, axis=0)
    cos_back = times(miss, ch[...], cl[...], nn)
    sin_back = times(miss, sh[...], sl[...], nn)
    even_real, odd_real = (
        cos_back[at : at + chunk] - sin_back[at + chunk : at + 2 * chunk] for at in (0, 2 * chunk)
    )
    even_imag, odd_imag = (
        cos_back[at + chunk : at + 2 * chunk] + sin_back[at : at + chunk] for at in (0, 2 * chunk)
    )
    turned_real = odd_real * turn_cos - odd_imag * turn_sin
    turned_imag = odd_imag * turn_cos + odd_real * turn_sin
    back[:chunk, :half] = (even_real + turned_real) * norm
    back[:chunk, half:] = (even_real - turned_real) * norm
    back[chunk:, :half] = (even_imag + turned_imag) * norm
    back[chunk:, half:] = (even_imag - turned_imag) * norm
    for p in range(2):
        found = [back[p * chunk : (p + 1) * chunk, plane_of(slot)] for slot in range(4)]
        first = jnp.concatenate([f[:, :local] for f in found], axis=1)
        second = jnp.concatenate([f[:, local:] for f in found], axis=1)
        own_out[p] = jnp.where(lower, first, second).astype(jnp.bfloat16)
        far_out[p] = jnp.where(lower, second, first).astype(jnp.bfloat16)


def delay(place, *parts):
    shape = jax.ShapeDtypeStruct(parts[0].shape, jnp.bfloat16)
    chunk, length = parts[5].shape
    vmem = pl.BlockSpec(memory_space=pltpu.VMEM)
    return pl.pallas_call(
        delay_kernel,
        in_specs=[pl.BlockSpec(memory_space=pltpu.SMEM)] + [vmem] * len(parts),
        out_specs=(vmem, vmem),
        out_shape=(shape, shape),
        scratch_shapes=[pltpu.VMEM((2 * chunk, length), jnp.float32)] * 2,
        compiler_params=pltpu.CompilerParams(vmem_limit_bytes=VMEM_LIMIT),
        cost_estimate=cost(
            flops=24 * chunk * length * length, bytes_accessed=8 * length * length, transcendentals=0
        ),
        name="delay",
    )(place, *parts)


def field_rows(place, half, other, slots, out, at):
    chunk, local = half.shape[3], half.shape[4] // 4
    base = 4 * chunk
    for blk in range(2):
        for n in range(4):
            hi, lo = (n >> 1) ^ place[1], (n & 1) ^ place[2]
            planes = [
                jnp.where(
                    lo == 0,
                    half[hi, blk, p].astype(jnp.float32),
                    other[hi, blk, p].astype(jnp.float32),
                )
                for p in range(2)
            ]
            first = at + blk * 2 * base + n * chunk
            for i, s in enumerate(slots):
                real = planes[0][:, s * local : (s + 1) * local]
                imag = planes[1][:, s * local : (s + 1) * local]
                lanes = slice(i * 2 * local, (i + 1) * 2 * local)
                upper = jnp.concatenate([real, imag], axis=1)
                lower = jnp.concatenate([imag, -real], axis=1)
                out[first : first + chunk, lanes] = upper.astype(jnp.bfloat16)
                out[first + base : first + base + chunk, lanes] = lower.astype(jnp.bfloat16)


def store_tiles(sums, slot, out):
    lanes = slice(slot * LANES, (slot + 1) * LANES)
    for t in range(out.shape[0]):
        out[t] = sums[t * LANES : (t + 1) * LANES, lanes].T.astype(out.dtype)


def adjoint_kernel(slots, ends_only, place, half, other, own_k, far_k, *rest):
    outs, field = rest[:-1], rest[-1]
    step = pl.program_id(0)

    @pl.when((place[0] == 0) | (not ends_only))
    def _():
        @pl.when(step == 0)
        def _():
            field_rows(place, half, other, slots, field, 0)

        cells = jnp.concatenate([own_k[0], own_k[1], far_k[0], far_k[1]], axis=1)
        sums = dot(cells, field[...])
        for i in range(len(slots)):

            @pl.when(step == 0)
            def _():
                store_tiles(sums, i, outs[2 * i])

            @pl.when(step > 0)
            def _():
                store_tiles(sums, i, outs[2 * i + 1])


def adjoint(place, half, other, own_k, far_k, slots, dtype, ends_only=False):
    base = own_k.shape[2]
    count = own_k.shape[1] // LANES
    tiles = count // 3
    rows = half.shape[4] // 2
    k_spec = pl.BlockSpec((2, tiles * LANES, base), lambda i: (0, i, 0))
    f_spec = pl.BlockSpec(half.shape, lambda i: (0,) * 5)
    block = (tiles, rows, LANES)
    outs = pl.pallas_call(
        functools.partial(adjoint_kernel, slots, ends_only),
        grid=(3,),
        in_specs=[pl.BlockSpec(memory_space=pltpu.SMEM), f_spec, f_spec, k_spec, k_spec],
        out_specs=[
            pl.BlockSpec(block, lambda i: (0, 0, 0)),
            pl.BlockSpec(block, lambda i: (jnp.maximum(i - 1, 0), 0, 0)),
        ]
        * len(slots),
        out_shape=[
            jax.ShapeDtypeStruct((n * tiles, rows, LANES), dtype) for _ in slots for n in (1, 2)
        ],
        scratch_shapes=[pltpu.VMEM((4 * base, rows * len(slots)), jnp.bfloat16)],
        compiler_params=pltpu.CompilerParams(vmem_limit_bytes=VMEM_LIMIT),
        cost_estimate=cost(
            flops=8 * rows * len(slots) * count * LANES * base,
            bytes_accessed=(4 + 2 * len(slots)) * 2**20,
            transcendentals=0,
            times=20,
        ),
        name="adjoint",
    )(place, half, other, own_k, far_k)
    return [outs[2 * i : 2 * i + 2] for i in range(len(slots))]


def first_kernel(slot, place, half, other, own_k, far_k, out, field):
    @pl.when(place[0] == 0)
    def _():
        @pl.when(pl.program_id(0) == 0)
        def _():
            field_rows(place, half, other, (slot,), field, 0)

        cells = jnp.concatenate([own_k[0], own_k[1], far_k[0], far_k[1]], axis=1)
        store_tiles(dot(cells, field[...]), 0, out)


def first_adjoint(place, half, other, own_k, far_k, slot, begin, steps):
    base = own_k.shape[2]
    tiles = own_k.shape[1] // LANES // 3
    rows = half.shape[4] // 2
    k_spec = pl.BlockSpec((2, tiles * LANES, base), lambda i: (0, i + begin, 0))
    f_spec = pl.BlockSpec(half.shape, lambda i: (0,) * 5)
    return pl.pallas_call(
        functools.partial(first_kernel, slot),
        grid=(steps,),
        in_specs=[pl.BlockSpec(memory_space=pltpu.SMEM), f_spec, f_spec, k_spec, k_spec],
        out_specs=pl.BlockSpec((tiles, rows, LANES), lambda i: (i, 0, 0)),
        out_shape=jax.ShapeDtypeStruct((steps * tiles, rows, LANES), jnp.bfloat16),
        scratch_shapes=[pltpu.VMEM((4 * base, rows), jnp.bfloat16)],
        compiler_params=pltpu.CompilerParams(vmem_limit_bytes=VMEM_LIMIT),
        cost_estimate=cost(
            flops=8 * rows * steps * tiles * LANES * base,
            bytes_accessed=steps * 2**21,
            transcendentals=0,
            times=20,
        ),
        name="first_adjoint",
    )(place, half, other, own_k, far_k)


def near_kernel(
    slots, place, half, other, near_half, near_other, own_a, far_a, near_k, near_far_k, *rest
):
    field = rest[-1]

    @pl.when(place[0] == 1)
    def _():
        field_rows(place, half, other, slots, field, 0)
        rows = field.shape[0] // 2
        swapped = [(1, 0, 2, 3)[slot] for slot in slots]
        field_rows(place, near_half, near_other, swapped, field, rows)
        tiles = near_k.shape[0] // 2
        cells = jnp.concatenate(
            [own_a[0], own_a[1], far_a[0], far_a[1]]
            + [tall(part[i * tiles : (i + 1) * tiles]) for part in (near_k, near_far_k) for i in (0, 1)],
            axis=1,
        )
        sums = dot(cells, field[...])
        outs = rest[:-1]
        if len(outs) == 1:
            outs = (outs[0].at[pl.ds(0, tiles)], outs[0].at[pl.ds(tiles, tiles)])
        for i, out in enumerate(outs):
            store_tiles(sums, i, out)


def near_adjoint(place, half, other, near_half, near_other, own_a, far_a, r2, r3, slots, dtype):
    base = own_a.shape[2]
    tiles = own_a.shape[1] // LANES
    rows = half.shape[4] // 2
    whole = lambda a: pl.BlockSpec(a.shape, lambda i: (0,) * a.ndim)
    two = pl.BlockSpec((2 * tiles, LANES, rows), lambda i: (0, 0, 0))
    one = pl.BlockSpec((tiles, LANES, rows), lambda i: (0, 0, 0))
    counts = (2,) if dtype == jnp.bfloat16 else (1, 1)
    return pl.pallas_call(
        functools.partial(near_kernel, slots),
        grid=(1,),
        in_specs=[pl.BlockSpec(memory_space=pltpu.SMEM)]
        + [whole(a) for a in (half, other, near_half, near_other, own_a, far_a)]
        + [two, two],
        out_specs=[two if n == 2 else one for n in counts],
        out_shape=[jax.ShapeDtypeStruct((n * tiles, LANES, rows), dtype) for n in counts],
        scratch_shapes=[pltpu.VMEM((8 * base, rows * 2), jnp.bfloat16)],
        compiler_params=pltpu.CompilerParams(vmem_limit_bytes=VMEM_LIMIT),
        cost_estimate=cost(
            flops=32 * rows * tiles * LANES * base,
            bytes_accessed=5 * 2**20,
            transcendentals=0,
            times=20,
        ),
        name="near_adjoint",
    )(place, half, other, near_half, near_other, own_a, far_a, r2, r3)


def store_rows(out, value):
    local = out.shape[0]
    for t in range(value.shape[0]):
        lanes = slice(t * LANES, (t + 1) * LANES)
        out[:, 0, lanes] = value[t][:local]
        out[:, 1, lanes] = value[t][local:]


def final_a_kernel(place, part_a, peer_a, end_a, out):
    mid = part_a[...] + peer_a[...].astype(jnp.float32)
    store_rows(out, jnp.where(place[0] == 1, mid, end_a[...].astype(jnp.float32)))


def final_b_kernel(place, part, near, far, before, out):
    value = part[...] + near[...].astype(jnp.float32)
    store_rows(out, value + jnp.where(place[0] == 1, far[...].astype(jnp.float32), 0.0))


def final(place, part_a, peer_a, end_a, part_b, near_b, far_b):
    tiles, rows, _ = part_a.shape
    shape = (tiles, rows, LANES)
    smem = pl.BlockSpec(memory_space=pltpu.SMEM)
    one = pl.BlockSpec(shape, lambda i: (0, 0, 0))
    second = pl.BlockSpec(shape, lambda i: (1, 0, 0))
    block = (rows // 2, 2, tiles * LANES)
    whole = jax.ShapeDtypeStruct((rows // 2, 2, 4 * tiles * LANES), jnp.float32)
    params = pltpu.CompilerParams(vmem_limit_bytes=VMEM_LIMIT)
    done = pl.pallas_call(
        final_a_kernel,
        grid=(1,),
        in_specs=[smem, one, second, one],
        out_specs=pl.BlockSpec(block, lambda i: (0, 0, 0)),
        out_shape=whole,
        compiler_params=params,
        cost_estimate=cost(flops=2 * rows * tiles * LANES, bytes_accessed=2**20, transcendentals=0),
        name="final_a",
    )(place, part_a, peer_a, end_a)
    for piece, begin, steps in ((1, 2, 2), (0, 1, 1)):
        each = pl.BlockSpec(shape, lambda i: (i, 0, 0))
        done = pl.pallas_call(
            final_b_kernel,
            grid=(steps,),
            in_specs=[smem, each, each, each, pl.BlockSpec(memory_space=pl.ANY)],
            out_specs=pl.BlockSpec(block, functools.partial(lambda start, i: (0, 0, i + start), begin)),
            out_shape=whole,
            input_output_aliases={4: 0},
            compiler_params=params,
            cost_estimate=cost(
                flops=3 * steps * rows * tiles * LANES, bytes_accessed=2**20 * steps, transcendentals=0
            ),
            name="final_b",
        )(place, part_b[piece], near_b[piece], far_b[piece], done)
    return done


def table_parts(length):
    half = length // 2
    steps = np.arange(half)
    turn = steps * (2.0 * math.pi / length)
    parts = [np.stack([np.cos(turn), np.sin(turn)]).astype(np.float32)]
    angle = (steps[:, None] * steps[None, :] % half) * (2.0 * math.pi / half)
    for table in (np.cos(angle), np.sin(angle)):
        high = table.astype(ml_dtypes.bfloat16)
        parts += [high, (table - high.astype(np.float64)).astype(ml_dtypes.bfloat16)]
    return [jnp.asarray(part) for part in parts]


def line_body(sky, kernel, data, block_tiles, length_bin, wedge_keep):
    length = data.shape[3]
    local, cells = sky.shape[1], sky.shape[3]
    base = kernel.shape[4]
    hi, lo = lax.axis_index("th"), lax.axis_index("tl")
    zpos, ypos = lax.axis_index("outer"), lax.axis_index("inner")
    tile_pos = hi * 2 + lo
    chunk = base // 4
    is_mid = (zpos == 1) | (zpos == 2)
    order = jnp.array([[0, 1, 2, 3], [1, 0, 2, 3], [2, 3, 1, 0], [3, 2, 1, 0]], jnp.int32)[zpos]
    place = jnp.concatenate([jnp.stack([is_mid.astype(jnp.int32), hi, lo, ypos]), order])

    tiles = cells // LANES // 4
    cut = tiles * LANES
    own_sky = sky[0].reshape(local, 2, cells // LANES, LANES).transpose(2, 1, 0, 3)
    own_sky = own_sky.reshape(cells // LANES, 2 * local, LANES)
    sky_a, sky_b = own_sky[:tiles], own_sky[tiles:]
    def ends(*values):
        return [lax.ppermute(value, "outer", ENDS) for value in values]

    def mids(*values):
        return [lax.ppermute(value, ("tl", "outer"), MIDS) for value in values]

    def as_tiles(part):
        return part.reshape(2 * tiles, LANES, base)

    (r1,) = ends(sky_b)
    (m1,) = mids(sky_b)
    column = jnp.arange(block_tiles.shape[1], dtype=jnp.int32) == tile_pos
    weight = jnp.sum(jnp.where(column, block_tiles[0], 0)).astype(jnp.bfloat16)
    own_a = lax.optimization_barrier(kernel[0, 0, :, :cut] * weight)
    own_b = kernel[0, 0, :, cut:] * weight
    end2 = jnp.concatenate([as_tiles(own_a), sky_a])
    own_a, end2 = lax.optimization_barrier((own_a, end2))
    far_a = lax.ppermute(own_a, "inner", SWAP)
    pay2 = jnp.where(is_mid, m1, end2)
    end3 = jnp.concatenate([as_tiles(far_a), sky_a])
    own_b, far_a, m1, end3 = lax.optimization_barrier((own_b, far_a, m1, end3))
    (r2,) = ends(pay2)
    (m2,) = mids(r1)
    far_b = lax.ppermute(own_b, "inner", SWAP)
    (r3,) = ends(jnp.where(is_mid, m2, end3))
    (m3,) = mids(jnp.concatenate([sky_a, r2[2 * tiles :]]))

    parts = table_parts(length)
    def by_parity(value):
        pairs = value.reshape(value.shape[:-1] + (length // 2, 2))
        return jnp.swapaxes(pairs, -1, -2).reshape(value.shape)

    own_data = by_parity(lax.dynamic_slice_in_dim(data[0], tile_pos * chunk, chunk, 1))
    own_bins = lax.dynamic_slice_in_dim(length_bin[0], tile_pos * chunk, chunk, 0)
    keep = by_parity(wedge_keep.astype(jnp.float32))[own_bins]

    done = early(place, own_b, sky_b, r1, m1, r2, (own_data, keep))
    keep_vis, send_vis, near_keep, near_send = late(
        place, done, own_b, far_b, sky_b, r1, m1, m2, own_a, far_a, sky_a, r2, r3, m3, chunk
    )
    (near,) = ends(near_sum(near_keep, lax.ppermute(near_send, "tl", SWAP)))
    got = lax.ppermute(send_vis, "tl", SWAP)
    mine, to_x, to_y, to_d = own_sum(place, keep_vis, got, near)
    from_x = lax.ppermute(to_x, "th", SWAP)
    from_y = lax.ppermute(to_y, "inner", SWAP)
    from_d = lax.ppermute(to_d, ("th", "inner"), DIAG)
    own_back, far_back = delay(place, mine, from_x, from_y, from_d, own_data, keep, *parts)
    back_x = lax.ppermute(own_back, "th", SWAP)
    back_y = lax.ppermute(far_back, "inner", SWAP)
    back_d = lax.ppermute(far_back, ("th", "inner"), DIAG)
    half = jnp.stack([jnp.stack([own_back, back_y]), jnp.stack([back_x, back_d])])
    other = lax.ppermute(half, "tl", SWAP)
    (near_half,) = ends(half)

    low = jnp.bfloat16

    def plus(part, got):
        return (part + got.astype(jnp.float32)).astype(low)

    send3 = [first_adjoint(place, half, other, own_b, far_b, 3, *part) for part in PARTS]
    g1 = ends(*send3)
    near_half, _ = lax.optimization_barrier((near_half, send3[1]))
    near_other = lax.ppermute(near_half, "tl", SWAP)
    near_args = (half, other, near_half, near_other, own_a, far_a, r2, r3)
    (send_a,) = near_adjoint(place, *near_args, (3, 2), low)
    (peer_a,) = mids(send_a)
    half, send_a = lax.optimization_barrier((half, send_a))
    part1_a, part0_a = near_adjoint(place, half, *near_args[1:], (1, 0), jnp.float32)
    part3, part2, part1, part0 = adjoint(
        place, half, other, own_b, far_b, (3, 2, 1, 0), jnp.float32
    )
    got_0, peer_a = lax.optimization_barrier((g1[0], peer_a))
    far3 = mids(plus(part3[0], got_0), plus(part3[1], g1[1]))
    ready_a = jnp.where(is_mid, plus(part1_a, peer_a[:tiles]), part2[0].astype(low))
    g2 = ends(ready_a, part2[1].astype(low))
    g2, far3 = lax.optimization_barrier((g2, far3))
    far2 = mids(*(plus(part, got) for part, got in zip(part2, g2)))
    g3 = ends(
        *(plus(part, jnp.where(is_mid, got, jnp.zeros_like(got))) for part, got in zip(part1, far3))
    )
    return final(place, part0_a, peer_a, g2[0], part0, g3, far2)[None]


def body(sky, kernel, *rest):
    local, cells = sky.shape[1], sky.shape[3]
    line = lax.axis_size("outer") == 4 and 2 * local == LANES and kernel.shape[4] == LANES
    chosen = line_body if line and cells % (4 * LANES) == 0 else any_body
    return chosen(sky, kernel, *rest)


def solution(mesh):
    tiles, freqs = mesh.shape["tile"], mesh.shape["freq"]
    fine = Mesh(mesh.devices.reshape(tiles // 2, 2, freqs // 2, 2), ("th", "tl", "outer", "inner"))
    tile, freq = ("th", "tl"), ("outer", "inner")
    return jax.shard_map(
        body,
        mesh=fine,
        in_specs=(
            P(tile, freq, None, None),
            P(tile, freq, None, None, None),
            P(freq, None, None, None),
            P(freq, None),
            P(freq, None),
            P(),
        ),
        out_specs=P(tile, freq, None, None),
        check_vma=False,
    )
```

```python
import functools
import math

import jax
import jax.numpy as jnp
import ml_dtypes
import numpy as np
from jax import lax
from jax.experimental import pallas as pl
from jax.experimental.pallas import tpu as pltpu
from jax.sharding import Mesh, PartitionSpec as P

SWAP = [(0, 1), (1, 0)]
ENDS = [(0, 1), (1, 0), (2, 3), (3, 2)]
MIDS = [(1, 2), (2, 1), (5, 6), (6, 5), (0, 4), (4, 0), (3, 7), (7, 3)]
DIAG = [(0, 3), (1, 2), (2, 1), (3, 0)]
LANES = 128
PARTS = ((0, 1), (1, 2))
VMEM_LIMIT = 24 * 2**20
NT = (((1,), (1,)), ((), ()))


def cost(flops, bytes_accessed, transcendentals, times=1):
    return pl.CostEstimate(
        flops=times * flops, bytes_accessed=times * bytes_accessed, transcendentals=transcendentals
    )


def xor_chunks(rows, hi, lo):
    planes, count, cells = rows.shape
    rows = rows.reshape(planes, 2, 2, count // 4, cells)
    rows = jnp.where(hi == 1, rows[:, ::-1], rows)
    rows = jnp.where(lo == 1, rows[:, :, ::-1], rows)
    return rows.reshape(planes * count, cells)


def project(kernel_rows, sky_rows):
    out = lax.dot_general(
        kernel_rows, sky_rows, (((1,), (1,)), ((), ())), preferred_element_type=jnp.float32
    )
    base, chans = out.shape[0] // 2, out.shape[1] // 2
    real = out[:base, :chans] - out[base:, chans:]
    imag = out[:base, chans:] + out[base:, :chans]
    return jnp.stack([real, imag])


def adjoint_any(field, kernel_rows):
    total = 0.0
    for blk in range(2):
        real, imag = field[blk][0], field[blk][1]
        lhs = jnp.concatenate(
            [jnp.concatenate([real, imag], 1), jnp.concatenate([imag, -real], 1)], 0
        )
        total = total + lax.dot_general(
            lhs, kernel_rows[blk], (((0,), (0,)), ((), ())), preferred_element_type=jnp.float32
        )
    return total


def tables(channels, length):
    product = channels[:, None] * jnp.arange(length, dtype=jnp.int32)[None, :] % length
    angle = product.astype(jnp.float32) * (2.0 * math.pi / length)
    return jnp.cos(angle), jnp.sin(angle)


def mm(a, b):
    return jnp.einsum("bc,ck->bk", a, b, precision=lax.Precision.HIGHEST)


def mmt(a, b):
    return jnp.einsum("bk,ck->bc", a, b, precision=lax.Precision.HIGHEST)


def any_body(sky, kernel, data, block_tiles, length_bin, wedge_keep):
    length = data.shape[3]
    local, cells = sky.shape[1], sky.shape[3]
    base = kernel.shape[4]
    hi, lo = lax.axis_index("th"), lax.axis_index("tl")
    zpos, ypos = lax.axis_index("outer"), lax.axis_index("inner")
    depth = lax.axis_size("outer")
    tile_pos = hi * 2 + lo
    chunk = base // 4

    column = jnp.arange(block_tiles.shape[1], dtype=jnp.int32) == tile_pos
    weight = jnp.sum(jnp.where(column, block_tiles[0], 0)).astype(jnp.bfloat16)

    own_sky = sky[0].transpose(1, 0, 2).reshape(2 * local, cells)
    own_rows = xor_chunks((kernel[0, 0] * weight).transpose(0, 2, 1), hi, lo)
    kernels = [own_rows, lax.ppermute(own_rows, "inner", SWAP)]

    every = lax.all_gather(own_sky, "outer")
    order = jnp.arange(depth, dtype=jnp.int32)
    vis = [
        jnp.concatenate([project(rows, every[s]) for s in range(depth)], axis=2)
        for rows in kernels
    ]

    def channels(half):
        place = (order[:, None] * 2 + half) * local + jnp.arange(local, dtype=jnp.int32)[None, :]
        return place.reshape(-1)

    own_cos, own_sin = tables(channels(ypos), length)
    far_cos, far_sin = tables(channels(1 - ypos), length)

    count = vis[0].shape[2]
    vis = jnp.stack(vis).reshape(2, 2, 2, 2, chunk, count)
    vis = vis[:, :, :, 0] + lax.ppermute(vis[:, :, :, 1], "tl", SWAP)
    from_x = lax.ppermute(vis[0, :, 1], "th", SWAP)
    from_y = lax.ppermute(vis[1, :, 0], "inner", SWAP)
    from_d = lax.ppermute(vis[1, :, 1], ("th", "inner"), DIAG)
    own_vis = vis[0, :, 0] + from_x
    far_vis = from_y + from_d

    norm = 1.0 / math.sqrt(length)
    own_data = lax.dynamic_slice_in_dim(data[0], tile_pos * chunk, chunk, 1).astype(jnp.float32)
    own_bins = lax.dynamic_slice_in_dim(length_bin[0], tile_pos * chunk, chunk, 0)
    keep = wedge_keep[own_bins].astype(jnp.float32)
    cos_sum = [mm(own_vis[p], own_cos) + mm(far_vis[p], far_cos) for p in range(2)]
    sin_sum = [mm(own_vis[p], own_sin) + mm(far_vis[p], far_sin) for p in range(2)]
    miss_real = keep * ((cos_sum[0] + sin_sum[1]) * norm - own_data[0])
    miss_imag = keep * ((cos_sum[1] - sin_sum[0]) * norm - own_data[1])

    def back(cosine, sine):
        real = (mmt(miss_real, cosine) - mmt(miss_imag, sine)) * norm
        imag = (mmt(miss_imag, cosine) + mmt(miss_real, sine)) * norm
        return jnp.stack([real, imag]).astype(jnp.bfloat16)

    own_back, far_back = back(own_cos, own_sin), back(far_cos, far_sin)
    back_x = lax.ppermute(own_back, "th", SWAP)
    back_y = lax.ppermute(far_back, "inner", SWAP)
    back_d = lax.ppermute(far_back, ("th", "inner"), DIAG)
    half = jnp.stack([jnp.stack([own_back, back_x], 1), jnp.stack([back_y, back_d], 1)])
    other = lax.ppermute(half, "tl", SWAP)
    field = jnp.stack([half, other], 3).reshape(2, 2, base, count)

    def update(slot):
        return adjoint_any(field[..., slot * local : (slot + 1) * local], kernels)

    every = jnp.concatenate([update(s) for s in range(depth)], 0)
    gradient = lax.psum_scatter(every, "outer", scatter_dimension=0, tiled=True)
    return gradient.reshape(2, local, cells).transpose(1, 0, 2)[None]


def wide(tiles):
    return jnp.concatenate([tiles[t] for t in range(tiles.shape[0])], axis=1)


def paired(part):
    return jnp.concatenate([part[0], part[1]], axis=1)


def tall(tiles):
    return tiles.reshape(tiles.shape[0] * tiles.shape[1], tiles.shape[2])


def dot(a, b):
    return jnp.dot(a, b, preferred_element_type=jnp.float32)


def near_sum_kernel(keep, got, out):
    out[...] = (keep[...] + got[...]).astype(out.dtype)


def near_sum(keep, got):
    vmem = pl.BlockSpec(memory_space=pltpu.VMEM)
    return pl.pallas_call(
        near_sum_kernel,
        in_specs=[vmem, vmem],
        out_specs=vmem,
        out_shape=jax.ShapeDtypeStruct(keep.shape, jnp.bfloat16),
        compiler_params=pltpu.CompilerParams(vmem_limit_bytes=VMEM_LIMIT),
        cost_estimate=cost(flops=keep.size, bytes_accessed=10 * keep.size, transcendentals=0),
        name="near_sum",
    )(keep, got)


def own_sum_kernel(place, keep, got, near, mine, to_x, to_y, to_d):
    for hi, blk, out in ((0, 0, mine), (1, 0, to_x), (0, 1, to_y), (1, 1, to_d)):
        added = jnp.where(place[0] == 1, 0.0, near[hi, blk].astype(jnp.float32))
        out[...] = keep[hi, blk] + got[hi, blk] + added


def own_sum(place, keep, got, near):
    vmem = pl.BlockSpec(memory_space=pltpu.VMEM)
    shape = keep.shape[2:]
    return pl.pallas_call(
        own_sum_kernel,
        in_specs=[pl.BlockSpec(memory_space=pltpu.SMEM)] + [vmem] * 3,
        out_specs=[vmem] * 4,
        out_shape=[jax.ShapeDtypeStruct(shape, jnp.float32)] * 4,
        compiler_params=pltpu.CompilerParams(vmem_limit_bytes=VMEM_LIMIT),
        cost_estimate=cost(flops=2 * keep.size, bytes_accessed=14 * keep.size, transcendentals=0),
        name="own_sum",
    )(place, keep, got, near)


def early_kernel(place, own_k, slot0, slot1, mid2, end2, *rest):
    total = rest[-1]

    @pl.when(pl.program_id(0) == 0)
    def _():
        total[...] = jnp.zeros_like(total)

    third = jnp.where(place[0] == 1, mid2[...], end2[...])
    rows = jnp.concatenate([wide(slot0[...]), wide(slot1[...]), wide(third)], axis=0)
    total[...] += dot(rows, paired(own_k))


def early(place, own_k, sky, r1, m1, r2, ready):
    count, rows, _ = r1.shape
    base = own_k.shape[2]
    tiles = count // 3
    k_spec = pl.BlockSpec((2, tiles * LANES, base), lambda i: (0, i, 0))
    s_spec = pl.BlockSpec((tiles, rows, LANES), lambda i: (i, 0, 0))
    shape = (3 * rows, 2 * base)
    return pl.pallas_call(
        early_kernel,
        grid=(3,),
        in_specs=[pl.BlockSpec(memory_space=pltpu.SMEM), k_spec]
        + [s_spec] * 4
        + [pl.BlockSpec(memory_space=pl.ANY)] * len(ready),
        out_specs=pl.BlockSpec(shape, lambda i: (0, 0)),
        out_shape=jax.ShapeDtypeStruct(shape, jnp.float32),
        compiler_params=pltpu.CompilerParams(vmem_limit_bytes=VMEM_LIMIT),
        cost_estimate=cost(
            flops=6 * rows * count * LANES * 2 * base, bytes_accessed=4 * 2**20, transcendentals=0
        ),
        name="early",
    )(place, own_k, sky, r1, m1, r2, *ready)


def late_kernel(
    place, done, own_k, far_k, slot0, slot1, mid2, end2, mid3, end3, own_a, far_a, sky_a, near_sky, peer_sky, peer_near_sky,
    near_k, near_far_k, keep, send, near_keep, near_send, total, near_total
):
    step = pl.program_id(0)
    is_mid = place[0] == 1
    done_rows = done.shape[0]
    rows = done_rows // 3

    @pl.when(step == 0)
    def _():
        total[0, :done_rows] = done[...]
        total[0, done_rows:] = jnp.zeros_like(total[0, done_rows:])
        total[1] = jnp.zeros_like(total[1])

    @pl.when(step < 3)
    def _():
        third = wide(jnp.where(is_mid, mid2[...], end2[...]))
        last = wide(jnp.where(is_mid, mid3[...], end3[...]))
        every = jnp.concatenate([wide(slot0[...]), wide(slot1[...]), third, last], axis=0)
        total[0, done_rows:] += dot(last, paired(own_k))
        total[1] += dot(every, paired(far_k))

    @pl.when((step == 3) & is_mid)
    def _():
        tiles = sky_a.shape[0]
        sky = jnp.concatenate(
            [wide(part[...]) for part in (sky_a, near_sky, peer_sky, peer_near_sky)], axis=0
        )
        for blk, part in enumerate((own_a, far_a)):
            total[blk] += dot(sky, paired(part))
        for blk, part in enumerate((near_k, near_far_k)):
            pair = jnp.concatenate([tall(part[:tiles]), tall(part[tiles:])], axis=1)
            near_total[blk] = dot(sky, pair)

        store_visibility(place, near_total, near_keep, near_send, (1, 0, 2, 3))

    @pl.when(step == 3)
    def _():
        store_visibility(place, total, keep, send, (0, 1, 2, 3))


def store_visibility(place, total, keep, send, slots):
    base = total.shape[2] // 2
    local = total.shape[1] // 8
    chunk = base // 4
    for blk in range(2):
        for two in range(2):
            planes = [[], []]
            for slot in (slots[2 * two], slots[2 * two + 1]):
                own = total[blk, slot * 2 * local : (slot + 1) * 2 * local, :]
                planes[0].append(own[:local, :base] - own[local:, base:])
                planes[1].append(own[local:, :base] + own[:local, base:])
            turned = [jnp.concatenate(planes[p], axis=0).T for p in range(2)]
            lanes = slice(two * 2 * local, (two + 1) * 2 * local)
            for near, even, odd in ((0, keep, send), (1, send, keep)):

                @pl.when(place[2] == near)
                def _():
                    for p in range(2):
                        for n in range(4):
                            out = even if n & 1 == 0 else odd
                            out[(n >> 1) ^ place[1], blk, p, :, lanes] = turned[p][
                                n * chunk : (n + 1) * chunk
                            ]


def late(place, done, own_k, far_k, sky_b, r1, m1, m2, own_a, far_a, sky_a, r2, r3, m3, chunk):
    count, rows, _ = m2.shape
    base = own_k.shape[2]
    tiles = count // 3
    k_spec = pl.BlockSpec((2, tiles * LANES, base), lambda i: (0, jnp.minimum(i, 2), 0))
    s_spec = pl.BlockSpec((tiles, rows, LANES), lambda i: (jnp.minimum(i, 2), 0, 0))
    a_spec = pl.BlockSpec((2, tiles * LANES, base), lambda i: (0, 0, 0))
    one = pl.BlockSpec((tiles, rows, LANES), lambda i: (0, 0, 0))
    second = pl.BlockSpec((tiles, rows, LANES), lambda i: (1, 0, 0))
    third = pl.BlockSpec((tiles, rows, LANES), lambda i: (2, 0, 0))
    two = pl.BlockSpec((2 * tiles, rows, LANES), lambda i: (0, 0, 0))
    shape = (2, 2, 2, chunk, 2 * rows)
    return pl.pallas_call(
        late_kernel,
        grid=(4,),
        in_specs=[
            pl.BlockSpec(memory_space=pltpu.SMEM),
            pl.BlockSpec(done.shape, lambda i: (0, 0)),
            k_spec, k_spec, s_spec, s_spec, s_spec, s_spec, s_spec, s_spec, a_spec, a_spec, one, third, one, second, two, two,
        ],
        out_specs=[pl.BlockSpec(shape, lambda i: (0,) * 5)] * 4,
        out_shape=[jax.ShapeDtypeStruct(shape, jnp.float32)] * 4,
        scratch_shapes=[
            pltpu.VMEM((2, 4 * rows, 2 * base), jnp.float32),
            pltpu.VMEM((2, 4 * rows, 2 * base), jnp.float32),
        ],
        compiler_params=pltpu.CompilerParams(vmem_limit_bytes=VMEM_LIMIT),
        cost_estimate=cost(
            flops=10 * rows * count * LANES * 2 * base, bytes_accessed=9 * 2**20, transcendentals=0
        ),
        name="late",
    )(
        place, done, own_k, far_k, sky_b, r1, m1, r2, m2, r3, own_a, far_a, sky_a, r2, m3, m3, r2, r3
    )


def pack_kernel(place, mid, end0, end1, out):
    is_mid = place[0] == 1
    head = end0.shape[0]

    @pl.when(is_mid)
    def _():
        out[...] = mid[...]

    @pl.when(jnp.logical_not(is_mid))
    def _():
        out[:head] = end0[...]
        out[head:] = end1[...]


def pack(place, mid, end0, end1):
    vmem = pl.BlockSpec(memory_space=pltpu.VMEM)
    return pl.pallas_call(
        pack_kernel,
        in_specs=[pl.BlockSpec(memory_space=pltpu.SMEM)] + [vmem] * 3,
        out_specs=vmem,
        out_shape=jax.ShapeDtypeStruct(mid.shape, mid.dtype),
        compiler_params=pltpu.CompilerParams(vmem_limit_bytes=VMEM_LIMIT),
        cost_estimate=cost(
            flops=0, bytes_accessed=2 * mid.size * mid.dtype.itemsize, transcendentals=0
        ),
        name="pack",
    )(place, mid, end0, end1)


def split(value):
    high = value.astype(jnp.bfloat16)
    return high, (value - high.astype(jnp.float32)).astype(jnp.bfloat16)


def times(value, high, low, dims):
    rows = value.shape[0]
    upper, lower = split(value)
    both = lax.dot_general(
        jnp.concatenate([upper, lower], axis=0), high, dims, preferred_element_type=jnp.float32
    )
    rest = lax.dot_general(upper, low, dims, preferred_element_type=jnp.float32)
    return both[:rows] + both[rows:] + rest


def delay_kernel(
    place, vis0, from_x, from_y, from_d, data, keep, turn, ch, cl, sh, sl, own_out, far_out, rows, back
):
    length = keep.shape[1]
    chunk = keep.shape[0]
    local = length // 8
    norm = 1.0 / math.sqrt(length)
    nn = (((1,), (0,)), ((), ()))
    lower = place[3] == 0
    own = vis0[...] + from_x[...]
    far = from_y[...] + from_d[...]

    def plane_of(slot):
        return pl.ds(pl.multiple_of(place[4 + slot] * 2 * local, 2 * local), 2 * local)

    for slot in range(4):
        lanes = slice(slot * local, (slot + 1) * local)
        for p in range(2):
            mine, other = own[p][:, lanes], far[p][:, lanes]
            both = jnp.where(
                lower,
                jnp.concatenate([mine, other], axis=1),
                jnp.concatenate([other, mine], axis=1),
            )
            rows[p * chunk : (p + 1) * chunk, plane_of(slot)] = both
    half = length // 2
    turn_cos, turn_sin = turn[0:1], turn[1:2]
    low_half, high_half = rows[:, :half], rows[:, half:]
    plus, minus = low_half + high_half, low_half - high_half
    odd_real = minus[:chunk] * turn_cos + minus[chunk:] * turn_sin
    odd_imag = minus[chunk:] * turn_cos - minus[:chunk] * turn_sin
    value = jnp.concatenate([plus, odd_real, odd_imag], axis=0)
    cos_sum = times(value, ch[...], cl[...], nn)
    sin_sum = times(value, sh[...], sl[...], nn)
    miss = []
    for odd in range(2):
        real, imag = (slice((2 * odd + p) * chunk, (2 * odd + p + 1) * chunk) for p in range(2))
        lanes = slice(odd * half, (odd + 1) * half)
        kept = keep[:, lanes]
        spec_real = (cos_sum[real] + sin_sum[imag]) * norm
        spec_imag = (cos_sum[imag] - sin_sum[real]) * norm
        miss.append(kept * (spec_real - data[0, :, lanes].astype(jnp.float32)))
        miss.append(kept * (spec_imag - data[1, :, lanes].astype(jnp.float32)))
    miss = jnp.concatenate(miss, axis=0)
    cos_back = times(miss, ch[...], cl[...], nn)
    sin_back = times(miss, sh[...], sl[...], nn)
    even_real, odd_real = (
        cos_back[at : at + chunk] - sin_back[at + chunk : at + 2 * chunk] for at in (0, 2 * chunk)
    )
    even_imag, odd_imag = (
        cos_back[at + chunk : at + 2 * chunk] + sin_back[at : at + chunk] for at in (0, 2 * chunk)
    )
    turned_real = odd_real * turn_cos - odd_imag * turn_sin
    turned_imag = odd_imag * turn_cos + odd_real * turn_sin
    back[:chunk, :half] = (even_real + turned_real) * norm
    back[:chunk, half:] = (even_real - turned_real) * norm
    back[chunk:, :half] = (even_imag + turned_imag) * norm
    back[chunk:, half:] = (even_imag - turned_imag) * norm
    for p in range(2):
        found = [back[p * chunk : (p + 1) * chunk, plane_of(slot)] for slot in range(4)]
        first = jnp.concatenate([f[:, :local] for f in found], axis=1)
        second = jnp.concatenate([f[:, local:] for f in found], axis=1)
        own_out[p] = jnp.where(lower, first, second).astype(jnp.bfloat16)
        far_out[p] = jnp.where(lower, second, first).astype(jnp.bfloat16)


def delay(place, *parts):
    shape = jax.ShapeDtypeStruct(parts[0].shape, jnp.bfloat16)
    chunk, length = parts[5].shape
    vmem = pl.BlockSpec(memory_space=pltpu.VMEM)
    return pl.pallas_call(
        delay_kernel,
        in_specs=[pl.BlockSpec(memory_space=pltpu.SMEM)] + [vmem] * len(parts),
        out_specs=(vmem, vmem),
        out_shape=(shape, shape),
        scratch_shapes=[pltpu.VMEM((2 * chunk, length), jnp.float32)] * 2,
        compiler_params=pltpu.CompilerParams(vmem_limit_bytes=VMEM_LIMIT),
        cost_estimate=cost(
            flops=24 * chunk * length * length, bytes_accessed=8 * length * length, transcendentals=0
        ),
        name="delay",
    )(place, *parts)


def field_rows(place, half, other, slots, out, at):
    chunk, local = half.shape[3], half.shape[4] // 4
    base = 4 * chunk
    for blk in range(2):
        for n in range(4):
            hi, lo = (n >> 1) ^ place[1], (n & 1) ^ place[2]
            planes = [
                jnp.where(
                    lo == 0,
                    half[hi, blk, p].astype(jnp.float32),
                    other[hi, blk, p].astype(jnp.float32),
                )
                for p in range(2)
            ]
            first = at + blk * 2 * base + n * chunk
            for i, s in enumerate(slots):
                real = planes[0][:, s * local : (s + 1) * local]
                imag = planes[1][:, s * local : (s + 1) * local]
                lanes = slice(i * 2 * local, (i + 1) * 2 * local)
                upper = jnp.concatenate([real, imag], axis=1)
                lower = jnp.concatenate([imag, -real], axis=1)
                out[first : first + chunk, lanes] = upper.astype(jnp.bfloat16)
                out[first + base : first + base + chunk, lanes] = lower.astype(jnp.bfloat16)


def store_tiles(sums, slot, out):
    lanes = slice(slot * LANES, (slot + 1) * LANES)
    for t in range(out.shape[0]):
        out[t] = sums[t * LANES : (t + 1) * LANES, lanes].T.astype(out.dtype)


def adjoint_kernel(slots, ends_only, place, half, other, own_k, far_k, *rest):
    outs, field = rest[:-1], rest[-1]
    step = pl.program_id(0)

    @pl.when((place[0] == 0) | (not ends_only))
    def _():
        @pl.when(step == 0)
        def _():
            field_rows(place, half, other, slots, field, 0)

        cells = jnp.concatenate([own_k[0], own_k[1], far_k[0], far_k[1]], axis=1)
        sums = dot(cells, field[...])
        for i in range(len(slots)):

            @pl.when(step == 0)
            def _():
                store_tiles(sums, i, outs[2 * i])

            @pl.when(step > 0)
            def _():
                store_tiles(sums, i, outs[2 * i + 1])


def adjoint(place, half, other, own_k, far_k, slots, dtype, ends_only=False):
    base = own_k.shape[2]
    count = own_k.shape[1] // LANES
    tiles = count // 3
    rows = half.shape[4] // 2
    k_spec = pl.BlockSpec((2, tiles * LANES, base), lambda i: (0, i, 0))
    f_spec = pl.BlockSpec(half.shape, lambda i: (0,) * 5)
    block = (tiles, rows, LANES)
    outs = pl.pallas_call(
        functools.partial(adjoint_kernel, slots, ends_only),
        grid=(3,),
        in_specs=[pl.BlockSpec(memory_space=pltpu.SMEM), f_spec, f_spec, k_spec, k_spec],
        out_specs=[
            pl.BlockSpec(block, lambda i: (0, 0, 0)),
            pl.BlockSpec(block, lambda i: (jnp.maximum(i - 1, 0), 0, 0)),
        ]
        * len(slots),
        out_shape=[
            jax.ShapeDtypeStruct((n * tiles, rows, LANES), dtype) for _ in slots for n in (1, 2)
        ],
        scratch_shapes=[pltpu.VMEM((4 * base, rows * len(slots)), jnp.bfloat16)],
        compiler_params=pltpu.CompilerParams(vmem_limit_bytes=VMEM_LIMIT),
        cost_estimate=cost(
            flops=8 * rows * len(slots) * count * LANES * base,
            bytes_accessed=(4 + 2 * len(slots)) * 2**20,
            transcendentals=0,
            times=20,
        ),
        name="adjoint",
    )(place, half, other, own_k, far_k)
    return [outs[2 * i : 2 * i + 2] for i in range(len(slots))]


def first_kernel(slot, place, half, other, own_k, far_k, out, field):
    @pl.when(place[0] == 0)
    def _():
        @pl.when(pl.program_id(0) == 0)
        def _():
            field_rows(place, half, other, (slot,), field, 0)

        cells = jnp.concatenate([own_k[0], own_k[1], far_k[0], far_k[1]], axis=1)
        store_tiles(dot(cells, field[...]), 0, out)


def first_adjoint(place, half, other, own_k, far_k, slot, begin, steps):
    base = own_k.shape[2]
    tiles = own_k.shape[1] // LANES // 3
    rows = half.shape[4] // 2
    k_spec = pl.BlockSpec((2, tiles * LANES, base), lambda i: (0, i + begin, 0))
    f_spec = pl.BlockSpec(half.shape, lambda i: (0,) * 5)
    return pl.pallas_call(
        functools.partial(first_kernel, slot),
        grid=(steps,),
        in_specs=[pl.BlockSpec(memory_space=pltpu.SMEM), f_spec, f_spec, k_spec, k_spec],
        out_specs=pl.BlockSpec((tiles, rows, LANES), lambda i: (i, 0, 0)),
        out_shape=jax.ShapeDtypeStruct((steps * tiles, rows, LANES), jnp.bfloat16),
        scratch_shapes=[pltpu.VMEM((4 * base, rows), jnp.bfloat16)],
        compiler_params=pltpu.CompilerParams(vmem_limit_bytes=VMEM_LIMIT),
        cost_estimate=cost(
            flops=8 * rows * steps * tiles * LANES * base,
            bytes_accessed=steps * 2**21,
            transcendentals=0,
            times=20,
        ),
        name="first_adjoint",
    )(place, half, other, own_k, far_k)


def near_kernel(
    slots, place, half, other, near_half, near_other, own_a, far_a, near_k, near_far_k, *rest
):
    field = rest[-1]

    @pl.when(place[0] == 1)
    def _():
        field_rows(place, half, other, slots, field, 0)
        rows = field.shape[0] // 2
        swapped = [(1, 0, 2, 3)[slot] for slot in slots]
        field_rows(place, near_half, near_other, swapped, field, rows)
        tiles = near_k.shape[0] // 2
        cells = jnp.concatenate(
            [own_a[0], own_a[1], far_a[0], far_a[1]]
            + [tall(part[i * tiles : (i + 1) * tiles]) for part in (near_k, near_far_k) for i in (0, 1)],
            axis=1,
        )
        sums = dot(cells, field[...])
        outs = rest[:-1]
        if len(outs) == 1:
            outs = (outs[0].at[pl.ds(0, tiles)], outs[0].at[pl.ds(tiles, tiles)])
        for i, out in enumerate(outs):
            store_tiles(sums, i, out)


def near_adjoint(place, half, other, near_half, near_other, own_a, far_a, r2, r3, slots, dtype):
    base = own_a.shape[2]
    tiles = own_a.shape[1] // LANES
    rows = half.shape[4] // 2
    whole = lambda a: pl.BlockSpec(a.shape, lambda i: (0,) * a.ndim)
    two = pl.BlockSpec((2 * tiles, LANES, rows), lambda i: (0, 0, 0))
    one = pl.BlockSpec((tiles, LANES, rows), lambda i: (0, 0, 0))
    counts = (2,) if dtype == jnp.bfloat16 else (1, 1)
    return pl.pallas_call(
        functools.partial(near_kernel, slots),
        grid=(1,),
        in_specs=[pl.BlockSpec(memory_space=pltpu.SMEM)]
        + [whole(a) for a in (half, other, near_half, near_other, own_a, far_a)]
        + [two, two],
        out_specs=[two if n == 2 else one for n in counts],
        out_shape=[jax.ShapeDtypeStruct((n * tiles, LANES, rows), dtype) for n in counts],
        scratch_shapes=[pltpu.VMEM((8 * base, rows * 2), jnp.bfloat16)],
        compiler_params=pltpu.CompilerParams(vmem_limit_bytes=VMEM_LIMIT),
        cost_estimate=cost(
            flops=32 * rows * tiles * LANES * base,
            bytes_accessed=5 * 2**20,
            transcendentals=0,
            times=20,
        ),
        name="near_adjoint",
    )(place, half, other, near_half, near_other, own_a, far_a, r2, r3)


def store_rows(out, value):
    local = out.shape[0]
    for t in range(value.shape[0]):
        lanes = slice(t * LANES, (t + 1) * LANES)
        out[:, 0, lanes] = value[t][:local]
        out[:, 1, lanes] = value[t][local:]


def final_a_kernel(place, part_a, peer_a, end_a, out):
    mid = part_a[...] + peer_a[...].astype(jnp.float32)
    store_rows(out, jnp.where(place[0] == 1, mid, end_a[...].astype(jnp.float32)))


def final_b_kernel(place, part, near, far, before, out):
    value = part[...] + near[...].astype(jnp.float32)
    store_rows(out, value + jnp.where(place[0] == 1, far[...].astype(jnp.float32), 0.0))


def final(place, part_a, peer_a, end_a, part_b, near_b, far_b):
    tiles, rows, _ = part_a.shape
    shape = (tiles, rows, LANES)
    smem = pl.BlockSpec(memory_space=pltpu.SMEM)
    one = pl.BlockSpec(shape, lambda i: (0, 0, 0))
    second = pl.BlockSpec(shape, lambda i: (1, 0, 0))
    block = (rows // 2, 2, tiles * LANES)
    whole = jax.ShapeDtypeStruct((rows // 2, 2, 4 * tiles * LANES), jnp.float32)
    params = pltpu.CompilerParams(vmem_limit_bytes=VMEM_LIMIT)
    done = pl.pallas_call(
        final_a_kernel,
        grid=(1,),
        in_specs=[smem, one, second, one],
        out_specs=pl.BlockSpec(block, lambda i: (0, 0, 0)),
        out_shape=whole,
        compiler_params=params,
        cost_estimate=cost(flops=2 * rows * tiles * LANES, bytes_accessed=2**20, transcendentals=0),
        name="final_a",
    )(place, part_a, peer_a, end_a)
    for piece, begin, steps in ((1, 2, 2), (0, 1, 1)):
        each = pl.BlockSpec(shape, lambda i: (i, 0, 0))
        done = pl.pallas_call(
            final_b_kernel,
            grid=(steps,),
            in_specs=[smem, each, each, each, pl.BlockSpec(memory_space=pl.ANY)],
            out_specs=pl.BlockSpec(block, functools.partial(lambda start, i: (0, 0, i + start), begin)),
            out_shape=whole,
            input_output_aliases={4: 0},
            compiler_params=params,
            cost_estimate=cost(
                flops=3 * steps * rows * tiles * LANES, bytes_accessed=2**20 * steps, transcendentals=0
            ),
            name="final_b",
        )(place, part_b[piece], near_b[piece], far_b[piece], done)
    return done


def table_parts(length):
    half = length // 2
    steps = np.arange(half)
    turn = steps * (2.0 * math.pi / length)
    parts = [np.stack([np.cos(turn), np.sin(turn)]).astype(np.float32)]
    angle = (steps[:, None] * steps[None, :] % half) * (2.0 * math.pi / half)
    for table in (np.cos(angle), np.sin(angle)):
        high = table.astype(ml_dtypes.bfloat16)
        parts += [high, (table - high.astype(np.float64)).astype(ml_dtypes.bfloat16)]
    return [jnp.asarray(part) for part in parts]


def line_body(sky, kernel, data, block_tiles, length_bin, wedge_keep):
    length = data.shape[3]
    local, cells = sky.shape[1], sky.shape[3]
    base = kernel.shape[4]
    hi, lo = lax.axis_index("th"), lax.axis_index("tl")
    zpos, ypos = lax.axis_index("outer"), lax.axis_index("inner")
    tile_pos = hi * 2 + lo
    chunk = base // 4
    is_mid = (zpos == 1) | (zpos == 2)
    order = jnp.array([[0, 1, 2, 3], [1, 0, 2, 3], [2, 3, 1, 0], [3, 2, 1, 0]], jnp.int32)[zpos]
    place = jnp.concatenate([jnp.stack([is_mid.astype(jnp.int32), hi, lo, ypos]), order])

    tiles = cells // LANES // 4
    cut = tiles * LANES
    own_sky = sky[0].reshape(local, 2, cells // LANES, LANES).transpose(2, 1, 0, 3)
    own_sky = own_sky.reshape(cells // LANES, 2 * local, LANES)
    sky_a, sky_b = own_sky[:tiles], own_sky[tiles:]
    def ends(*values):
        return [lax.ppermute(value, "outer", ENDS) for value in values]

    def mids(*values):
        return [lax.ppermute(value, ("tl", "outer"), MIDS) for value in values]

    def as_tiles(part):
        return part.reshape(2 * tiles, LANES, base)

    (r1,) = ends(sky_b)
    (m1,) = mids(sky_b)
    column = jnp.arange(block_tiles.shape[1], dtype=jnp.int32) == tile_pos
    weight = jnp.sum(jnp.where(column, block_tiles[0], 0)).astype(jnp.bfloat16)
    own_a = lax.optimization_barrier(kernel[0, 0, :, :cut] * weight)
    own_b = kernel[0, 0, :, cut:] * weight
    end2 = jnp.concatenate([as_tiles(own_a), sky_a])
    own_a, end2 = lax.optimization_barrier((own_a, end2))
    far_a = lax.ppermute(own_a, "inner", SWAP)
    pay2 = jnp.where(is_mid, m1, end2)
    end3 = jnp.concatenate([as_tiles(far_a), sky_a])
    own_b, far_a, end3 = lax.optimization_barrier((own_b, far_a, end3))
    (r2,) = ends(pay2)
    (m2,) = mids(r1)
    far_b = lax.ppermute(own_b, "inner", SWAP)
    (r3,) = ends(jnp.where(is_mid, m2, end3))
    (m3,) = mids(jnp.concatenate([sky_a, r2[2 * tiles :]]))

    parts = table_parts(length)
    def by_parity(value):
        pairs = value.reshape(value.shape[:-1] + (length // 2, 2))
        return jnp.swapaxes(pairs, -1, -2).reshape(value.shape)

    own_data = by_parity(lax.dynamic_slice_in_dim(data[0], tile_pos * chunk, chunk, 1))
    own_bins = lax.dynamic_slice_in_dim(length_bin[0], tile_pos * chunk, chunk, 0)
    keep = by_parity(wedge_keep.astype(jnp.float32))[own_bins]

    done = early(place, own_b, sky_b, r1, m1, r2, (own_data, keep))
    keep_vis, send_vis, near_keep, near_send = late(
        place, done, own_b, far_b, sky_b, r1, m1, m2, own_a, far_a, sky_a, r2, r3, m3, chunk
    )
    (near,) = ends(near_sum(near_keep, lax.ppermute(near_send, "tl", SWAP)))
    got = lax.ppermute(send_vis, "tl", SWAP)
    mine, to_x, to_y, to_d = own_sum(place, keep_vis, got, near)
    from_x = lax.ppermute(to_x, "th", SWAP)
    from_y = lax.ppermute(to_y, "inner", SWAP)
    from_d = lax.ppermute(to_d, ("th", "inner"), DIAG)
    own_back, far_back = delay(place, mine, from_x, from_y, from_d, own_data, keep, *parts)
    back_x = lax.ppermute(own_back, "th", SWAP)
    back_y = lax.ppermute(far_back, "inner", SWAP)
    back_d = lax.ppermute(far_back, ("th", "inner"), DIAG)
    half = jnp.stack([jnp.stack([own_back, back_y]), jnp.stack([back_x, back_d])])
    other = lax.ppermute(half, "tl", SWAP)
    (near_half,) = ends(half)

    low = jnp.bfloat16

    def plus(part, got):
        return (part + got.astype(jnp.float32)).astype(low)

    send3 = [first_adjoint(place, half, other, own_b, far_b, 3, *part) for part in PARTS]
    g1 = ends(*send3)
    near_half, _ = lax.optimization_barrier((near_half, send3[1]))
    near_other = lax.ppermute(near_half, "tl", SWAP)
    near_args = (half, other, near_half, near_other, own_a, far_a, r2, r3)
    (send_a,) = near_adjoint(place, *near_args, (3, 2), low)
    (peer_a,) = mids(send_a)
    half, send_a = lax.optimization_barrier((half, send_a))
    part1_a, part0_a = near_adjoint(place, half, *near_args[1:], (1, 0), jnp.float32)
    part3, part2, part1, part0 = adjoint(
        place, half, other, own_b, far_b, (3, 2, 1, 0), jnp.float32
    )
    far3 = mids(*(plus(part, got) for part, got in zip(part3, g1)))
    ready_a = jnp.where(is_mid, plus(part1_a, peer_a[:tiles]), part2[0].astype(low))
    g2 = ends(ready_a, part2[1].astype(low))
    g2, far3 = lax.optimization_barrier((g2, far3))
    far2 = mids(*(plus(part, got) for part, got in zip(part2, g2)))
    g3 = ends(
        *(plus(part, jnp.where(is_mid, got, jnp.zeros_like(got))) for part, got in zip(part1, far3))
    )
    return final(place, part0_a, peer_a, g2[0], part0, g3, far2)[None]


def body(sky, kernel, *rest):
    local, cells = sky.shape[1], sky.shape[3]
    line = lax.axis_size("outer") == 4 and 2 * local == LANES and kernel.shape[4] == LANES
    chosen = line_body if line and cells % (4 * LANES) == 0 else any_body
    return chosen(sky, kernel, *rest)


def solution(mesh):
    tiles, freqs = mesh.shape["tile"], mesh.shape["freq"]
    fine = Mesh(mesh.devices.reshape(tiles // 2, 2, freqs // 2, 2), ("th", "tl", "outer", "inner"))
    tile, freq = ("th", "tl"), ("outer", "inner")
    return jax.shard_map(
        body,
        mesh=fine,
        in_specs=(
            P(tile, freq, None, None),
            P(tile, freq, None, None, None),
            P(freq, None, None, None),
            P(freq, None),
            P(freq, None),
            P(),
        ),
        out_specs=P(tile, freq, None, None),
        check_vma=False,
    )
```
